32 devices in a mesh: row: 4 (over y, core), col: 8 (over z, x).
Axes of the slice: x: 2, y: 2, z: 4, core: 2. Of those that a mesh axis runs over, the one named last changes fastest.
Arguments:
- density: bfloat16 [32, 15, 128, 128], P(('row', 'col')), may hold values from -0.5 to 0.5
- pattern: int32 [32, 15], P(('row', 'col')), may hold values 0 or 1
- filter_mask: int32 [32, 29], P(('row', 'col')), may hold values 0 or 1
Outputs:
- purified: bfloat16 [32, 29, 128, 128], P(('row', 'col'))
The draws below stay inside these ranges and needn't reach their ends.
All inputs are finite; a program needn't handle non-finite values. No bound on the sum of `pattern` or of `filter_mask` on one device may be relied on, other than what follows from the above.
Results may differ from the reference program's by a relative error of at most 0.0045.
Values may be sent and summed in bfloat16 or wider, within the bound.
No kernel may reach another device: no remote copies, remote signals or barrier semaphores. Data moves between devices by JAX's collectives and lax.ppermute only.
A program may use at most 64 MiB of HBM per device.

```python
import jax
import jax.numpy as jnp
from jax import lax

BLOCK_EDGE = 128
BAND_REACH = 7
ROWS_DEV = 1
BAND_SLOTS = 15
WIDE_SLOTS = 29
BLOCK_ROWS = 32


def touch_ends(result, rng, least, high):
    place = [jax.random.randint(jax.random.fold_in(rng, axis), (), 0, length) for axis, length in enumerate(result.shape)]
    widest = result.shape.index(max(result.shape))
    beside = place[:widest] + [(place[widest] + 1) % result.shape[widest]] + place[widest + 1:]
    return result.at[tuple(place)].set(least).at[tuple(beside)].set(high)


def block_levels(rng, extent, split, low, high):
    level = 1.0
    for position, blocks in split:
        steps = jax.random.uniform(jax.random.fold_in(jax.random.fold_in(rng, 6), position), (blocks,), jnp.float32, low / len(split), high / len(split))
        level = level * jnp.repeat(jnp.exp(steps), extent[position] // blocks).reshape((-1,) + (1,) * (len(extent) - 1 - position))
    return level


def normal_values(rng, extent, scale, bound, cuts=(), kind=jnp.bfloat16):
    loudness = block_levels(rng, extent, cuts, -0.22, 0.18) if cuts else 1.0
    entries = jax.random.normal(rng, extent, jnp.float32) * scale * loudness
    return jnp.minimum(jnp.maximum(entries, -bound), bound).astype(kind)


def setup_inputs(seed: int = 0) -> dict:
    seeds = jax.random.split(jax.random.key(seed), 4)
    density = normal_values(seeds[0], (BLOCK_ROWS, BAND_SLOTS, BLOCK_EDGE, BLOCK_EDGE), 0.08, 0.5, ((0, 32),))
    pattern = touch_ends((jax.random.randint(seeds[1], (BLOCK_ROWS, BAND_SLOTS), 0, 16) < 13).astype(jnp.int32), jax.random.fold_in(seeds[1], 1), 0, 1)
    filter_mask = touch_ends((jax.random.randint(seeds[2], (BLOCK_ROWS, WIDE_SLOTS), 0, 4) < 3).astype(jnp.int32), jax.random.fold_in(seeds[2], 1), 0, 1)
    return {"density": density, "pattern": pattern, "filter_mask": filter_mask}


def wrap_pad(blocks, width):
    return jnp.concatenate([blocks[blocks.shape[0] - width:], blocks, blocks[:width]], axis=0)


def band_product(left_blocks, extended, offset, band_reach, out_slots, slot_shift):
    row_count = left_blocks.shape[0]
    slot_count = left_blocks.shape[1]
    ext_slots = extended.shape[1]
    columns = []
    for target in range(out_slots):
        picked = [source for source in range(slot_count) if 0 <= target - source + slot_shift < ext_slots]
        lowest = picked[0]
        highest = picked[-1] + 1
        pieces = jnp.stack([extended[offset - band_reach + source: offset - band_reach + source + row_count, target - source + slot_shift] for source in range(lowest, highest)], axis=1)
        columns.append(jnp.einsum("rsab,rsbc->rac", left_blocks[:, lowest:highest].astype(jnp.float32), pieces.astype(jnp.float32)))
    return jnp.stack(columns, axis=1)


def reference(density, pattern, filter_mask):
    masked = density * pattern[:, :, None, None].astype(jnp.bfloat16)
    retain = filter_mask[:, :, None, None].astype(jnp.float32)
    groups = BLOCK_ROWS // ROWS_DEV
    padded = wrap_pad(masked, BAND_REACH)

    def square_group(index):
        start = (index * ROWS_DEV).astype(jnp.int32)
        own_rows = lax.dynamic_slice_in_dim(padded, start + BAND_REACH, ROWS_DEV, 0)
        window = lax.dynamic_slice_in_dim(padded, start, ROWS_DEV + 2 * BAND_REACH, 0)
        return band_product(own_rows, window, BAND_REACH, BAND_REACH, WIDE_SLOTS, 0)

    square = lax.map(square_group, jnp.arange(groups, dtype=jnp.int32))
    square = square.reshape(BLOCK_ROWS, WIDE_SLOTS, BLOCK_EDGE, BLOCK_EDGE)
    square_kept = square * retain
    square_round = square_kept.astype(jnp.bfloat16)
    padded_square = wrap_pad(square_round, BAND_REACH)

    def result_group(index):
        start = (index * ROWS_DEV).astype(jnp.int32)
        own_rows = lax.dynamic_slice_in_dim(padded, start + BAND_REACH, ROWS_DEV, 0)
        window = lax.dynamic_slice_in_dim(padded_square, start, ROWS_DEV + 2 * BAND_REACH, 0)
        cubed = band_product(own_rows, window, BAND_REACH, BAND_REACH, WIDE_SLOTS, BAND_REACH)
        kept_own = lax.dynamic_slice_in_dim(square_kept, start, ROWS_DEV, 0)
        retain_own = lax.dynamic_slice_in_dim(retain, start, ROWS_DEV, 0)
        return (retain_own * (3.0 * kept_own - 2.0 * cubed)).astype(jnp.bfloat16)

    purified = lax.map(result_group, jnp.arange(groups, dtype=jnp.int32))
    return purified.reshape(BLOCK_ROWS, WIDE_SLOTS, BLOCK_EDGE, BLOCK_EDGE)
```

```python
import functools

import jax
import jax.numpy as jnp
from jax import lax
from jax.experimental import pallas as pl
from jax.experimental.pallas import tpu as pltpu
from jax.sharding import PartitionSpec as P

AXES = ("row", "col")


def window(payload, need):
    groups, width = lax.axis_size("row"), lax.axis_size("col")
    count = groups * width
    here = lax.axis_index("row") * width + lax.axis_index("col")
    steps = jnp.arange(-need, need + 1, dtype=jnp.int32)
    if count <= 2 * need + 4:
        table = lax.all_gather(payload, AXES, axis=0, tiled=False)
        return table, (here + steps) % count
    group = lax.all_gather(payload, "col", axis=0, tiled=False)
    below, above = [], []
    for hop in range(1, -(-need // width) + 1):
        part = min(width, need - (hop - 1) * width)
        up = [(g, (g + hop) % groups) for g in range(groups)]
        down = [(g, (g - hop) % groups) for g in range(groups)]
        below.insert(0, lax.ppermute(group[width - part :], "row", up))
        above.append(lax.ppermute(group[:part], "row", down))
    table = jnp.concatenate(below + [group] + above, axis=0)
    return table, lax.axis_index("col") + need + steps


def purify(reach, edge, where, keep, table, out, dense, square, own, arrived):
    near, far = reach, 2 * reach
    row_base, col_base = far + 1, far + 2
    kept_cols = 2 * far + 1

    def rows(k, n):
        return pl.ds(pl.multiple_of((k + row_base) * edge, edge), n * edge)

    def cols(c, n):
        return pl.ds(pl.multiple_of((c + col_base) * edge, edge), n * edge)

    copies = []
    for k in range(-far, far + 1):
        low = max(k - reach, -far)
        high = min(k + reach, far + 1)
        first = low - (k - reach)
        n = high - low + 1
        copies.append(
            pltpu.make_async_copy(
                table.at[where[k + far], :edge, pl.ds(first * edge, n * edge)],
                dense.at[rows(k, 1), cols(low, n)],
                arrived.at[k + far],
            )
        )
    for copy in copies:
        copy.start()
    zero = jnp.zeros((edge, edge), dense.dtype)
    for k in range(-far, far + 1):
        for c in (k - reach - 1, k + reach + 1):
            if -far - 2 <= c <= far + 1:
                dense[rows(k, 1), cols(c, 1)] = zero
    dense[rows(-far - 1, 1), :] = jnp.zeros((edge, dense.shape[1]), dense.dtype)
    for copy in copies:
        copy.wait()

    def column(index, carry):
        c = 2 * index - far
        for d in range(-far, far + 1, 2):
            r = c - d
            low = max(-reach, -d - reach)
            size = 2 * reach + 2 - abs(d)

            @pl.when((r >= -near - 1) & (r <= near - 1))
            def _():
                s = jnp.dot(
                    dense[rows(r, 2), cols(c + low, size)],
                    dense[rows(c + low, size), cols(c, 2)],
                    preferred_element_type=jnp.float32,
                )
                parts = []
                for i in range(2):
                    line = []
                    for j in range(2):
                        u = jnp.clip(c + j - r - i + far, 0, kept_cols - 1)
                        m = keep[jnp.maximum(r + i + near, 0), u]
                        line.append(s[i * edge : (i + 1) * edge, j * edge : (j + 1) * edge] * m)
                    parts.append(jnp.concatenate(line, axis=1))
                for i in range(2):
                    square[pl.ds(pl.multiple_of((r + i + near + 1) * edge, edge), edge), :] = parts[i].astype(square.dtype)

                @pl.when(r == 0)
                def _():
                    own[...] = parts[0]

        for r in range(-near - 1, near, 2):

            @pl.when((c - r > far) | (c - r < -far))
            def _():
                square[(r + near + 1) * edge : (r + near + 3) * edge, :] = jnp.zeros((2 * edge, 2 * edge), square.dtype)

        cube = jnp.dot(
            dense[rows(0, 1), cols(-near, 2 * near + 1)],
            square[edge:, :],
            preferred_element_type=jnp.float32,
        )
        value = 3.0 * own[...] - 2.0 * cube
        for j in range(2):
            u = 2 * index + j
            m = keep[near, jnp.minimum(u, kept_cols - 1)]

            @pl.when(u < kept_cols)
            def _():
                out[u] = (m * value[:, j * edge : (j + 1) * edge]).astype(out.dtype)

        return carry

    lax.fori_loop(0, far + 1, column, 0)


def shards(density, pattern, filter_mask):
    slots, edge = density.shape[1], density.shape[2]
    wide = filter_mask.shape[1]
    reach = (slots - 1) // 2
    far = 2 * reach
    masked = density[0] * pattern[0][:, None, None].astype(density.dtype)
    flat = jnp.transpose(masked, (1, 0, 2)).reshape(edge, slots * edge)
    note = jnp.zeros((16, slots * edge), density.dtype).at[0, :wide].set(filter_mask[0].astype(density.dtype))
    payload = jnp.concatenate([flat, note], axis=0)
    table, where = window(payload, far)
    keep = table[where[reach : 3 * reach + 1], edge, :wide].astype(jnp.float32)
    smem = pl.BlockSpec(memory_space=pltpu.SMEM)
    result = pl.pallas_call(
        functools.partial(purify, reach, edge),
        out_shape=jax.ShapeDtypeStruct((wide, edge, edge), density.dtype),
        in_specs=[smem, smem, pl.BlockSpec(memory_space=pl.ANY)],
        out_specs=pl.BlockSpec(memory_space=pltpu.VMEM),
        scratch_shapes=[
            pltpu.VMEM(((2 * far + 2) * edge, (2 * far + 4) * edge), density.dtype),
            pltpu.VMEM(((2 * reach + 2) * edge, 2 * edge), density.dtype),
            pltpu.VMEM((edge, 2 * edge), jnp.float32),
            pltpu.SemaphoreType.DMA((2 * far + 1,)),
        ],
        compiler_params=pltpu.CompilerParams(vmem_limit_bytes=56 * 2**20),
        cost_estimate=pl.CostEstimate(flops=16 * 10**9, bytes_accessed=14 * 2**20, transcendentals=0),
    )(where, keep, table)
    return result[None]


def solution(mesh):
    in_specs = (
        P(AXES, None, None, None),
        P(AXES, None),
        P(AXES, None),
    )
    out_specs = P(AXES, None, None, None)
    return jax.shard_map(shards, mesh=mesh, in_specs=in_specs, out_specs=out_specs, check_vma=False)
```

```python
import functools

import jax
import jax.numpy as jnp
from jax import lax
from jax.experimental import pallas as pl
from jax.experimental.pallas import tpu as pltpu
from jax.sharding import Mesh, PartitionSpec as P

NOTE = 16
CORES = 2


def window(payload, need):
    width = lax.axis_size("col")
    groups = lax.axis_size("y") * CORES
    count = groups * width
    core, column = lax.axis_index("core"), lax.axis_index("col")
    group = lax.axis_index("y") * CORES + core
    steps = jnp.arange(-need, need + 1, dtype=jnp.int32)
    if count <= 2 * need + 4:
        mine = lax.all_gather(payload, ("y", "col"), axis=0, tiled=False)
        other = lax.ppermute(mine, "core", [(0, 1), (1, 0)])
        row = (group * width + column + steps) % count
        far_group = row // width
        return (mine, other), (far_group % CORES != core).astype(jnp.int32), far_group // CORES * width + row % width
    block = lax.all_gather(payload, "col", axis=0, tiled=False)
    below, above = [], []
    for hop in range(1, -(-need // width) + 1):
        part = min(width, need - (hop - 1) * width)
        up = [(g, (g + hop) % groups) for g in range(groups)]
        down = [(g, (g - hop) % groups) for g in range(groups)]
        below.insert(0, lax.ppermute(block[width - part :], ("y", "core"), up))
        above.append(lax.ppermute(block[:part], ("y", "core"), down))
    tables = below + [block] + above
    place, which, start = column + need + steps, jnp.zeros_like(steps), jnp.zeros_like(steps)
    edge = 0
    for t, table in enumerate(tables):
        which, start = jnp.where(place >= edge, t, which), jnp.where(place >= edge, edge, start)
        edge += table.shape[0]
    return tuple(tables), which, place - start


def purify(reach, edge, count, which, where, *refs):
    tables, (out, band, square, own, notes, keep, arrived, noted) = refs[:count], refs[count:]
    far = 2 * reach
    slots, wide = 2 * reach + 1, 4 * reach + 1
    kind = band.dtype

    def span(first, n):
        first = first * edge
        return pl.ds(first if isinstance(first, int) else pl.multiple_of(first, edge), n * edge)

    def fetch(k, carry):
        for t, table in enumerate(tables):

            @pl.when(which[k] == t)
            def _():
                for s in range(slots):
                    pltpu.make_async_copy(
                        table.at[where[k], pl.ds(s * edge, edge)],
                        band.at[span(k, 1), pl.ds((s + 1) * edge, edge)],
                        arrived.at[k],
                    ).start()

                @pl.when((k >= reach) & (k <= 3 * reach))
                def _():
                    pltpu.make_async_copy(
                        table.at[where[k], pl.ds(slots * edge, NOTE)], notes.at[k - reach], noted
                    ).start()

        return carry

    lax.fori_loop(0, 2 * far + 1, fetch, 0)

    def ready(k):
        whole = tables[0].at[0, pl.ds(0, slots * edge)]
        pltpu.make_async_copy(whole, band.at[pl.ds(0, slots * edge), pl.ds(0, edge)], arrived.at[k]).wait()

    def clear(k, carry):
        zero = jnp.zeros((edge, edge), kind)
        band[span(k, 1), pl.ds(0, edge)] = zero
        band[span(k, 1), pl.ds((slots + 1) * edge, edge)] = zero
        return carry

    lax.fori_loop(0, 2 * far + 2, clear, 0)
    band[span(2 * far + 1, 1), :] = jnp.zeros((edge, band.shape[1]), kind)

    def clear_square(r, carry):
        zero = jnp.zeros((edge, edge), kind)
        square[span(r, 1), pl.ds(0, edge)] = zero
        square[span(r, 1), pl.ds((wide + 1) * edge, edge)] = zero
        return carry

    lax.fori_loop(0, slots + 1, clear_square, 0)

    for r in range(slots):
        pltpu.make_async_copy(tables[0].at[0, pl.ds(0, NOTE)], notes.at[r], noted).wait()
    notes[slots] = jnp.zeros(notes.shape[1:], kind)
    spots = keep.shape[1]
    diagonal = lax.broadcasted_iota(jnp.int32, (spots, edge), 0) == lax.broadcasted_iota(jnp.int32, (spots, edge), 1)

    def spread(r, carry):
        line = notes[r].astype(jnp.float32)[:1]
        value = jnp.sum(jnp.where(diagonal, line, 0.0), axis=1, keepdims=True)
        keep[r] = jnp.broadcast_to(value, (spots, edge))
        return carry

    lax.fori_loop(0, slots + 1, spread, 0)

    for k in range(far):
        ready(k)

    def row_pair(pair, carry):
        r = 2 * pair
        ready(r + far)

        @pl.when(r + far + 1 <= 2 * far)
        def _():
            ready(r + far + 1)

        middle = jnp.where((r == reach) | (r + 1 == reach), 1, 0)
        for d in range(-far, far + 1, 2):
            low, high = max(-reach, d - reach), min(reach + 1, d + reach + 1)
            size = high - low + 1
            left = jnp.concatenate(
                [
                    band[span(r + reach, 1), pl.ds((low + reach + 1) * edge, size * edge)],
                    band[span(r + reach + 1, 1), pl.ds((low + reach) * edge, size * edge)],
                ],
                axis=0,
            )
            right = jnp.concatenate(
                [
                    band[span(r + reach + e, 1), pl.ds((d - e + reach + 1) * edge, 2 * edge)]
                    for e in range(low, high + 1)
                ],
                axis=0,
            )
            product = jnp.dot(left, right, preferred_element_type=jnp.float32)
            for i in range(2):
                u = d + far - i
                mask = jnp.concatenate(
                    [keep[r + i, pl.ds(min(max(u + j, 0), wide - 1), 1), :] for j in range(2)], axis=1
                )
                kept = product[i * edge : (i + 1) * edge] * mask
                square[span(r + i, 1), pl.ds((u + 1) * edge, 2 * edge)] = kept.astype(kind)
                if i == reach % 2:
                    own[middle, :, pl.ds((u + 1) * edge, 2 * edge)] = kept
        return carry

    lax.fori_loop(0, (slots + 1) // 2, row_pair, 0)

    for c in range(-far, far + 1, 2):
        low, high = max(-reach, c - far), min(reach, c + far + 1)
        left = band[span(far, 1), pl.ds((low + reach + 1) * edge, (high - low + 1) * edge)]
        right = jnp.concatenate(
            [square[span(r + reach, 1), pl.ds((c - r + far + 1) * edge, 2 * edge)] for r in range(low, high + 1)],
            axis=0,
        )
        cube = jnp.dot(left, right, preferred_element_type=jnp.float32)
        for j in range(2):
            u = c + far + j
            if u < wide:
                kept = own[1, :, pl.ds((u + 1) * edge, edge)]
                value = 3.0 * kept - 2.0 * cube[:, j * edge : (j + 1) * edge]
                out[u] = (keep[reach, pl.ds(u, 1), :] * value).astype(out.dtype)


def shards(density, pattern, filter_mask):
    slots, edge = density.shape[1], density.shape[2]
    wide = filter_mask.shape[1]
    reach = (slots - 1) // 2
    far = 2 * reach
    masked = density[0] * pattern[0][:, None, None].astype(density.dtype)
    note = jnp.zeros((NOTE, edge), density.dtype).at[0, :wide].set(filter_mask[0].astype(density.dtype))
    payload = jnp.concatenate([masked.reshape(slots * edge, edge), note], axis=0)
    tables, which, where = window(payload, far)
    smem = pl.BlockSpec(memory_space=pltpu.SMEM)
    result = pl.pallas_call(
        functools.partial(purify, reach, edge, len(tables)),
        out_shape=jax.ShapeDtypeStruct((wide, edge, edge), density.dtype),
        in_specs=[smem, smem] + [pl.BlockSpec(memory_space=pl.ANY)] * len(tables),
        out_specs=pl.BlockSpec(memory_space=pltpu.VMEM),
        scratch_shapes=[
            pltpu.VMEM(((2 * far + 2) * edge, (slots + 2) * edge), density.dtype),
            pltpu.VMEM(((slots + 1) * edge, (wide + 2) * edge), density.dtype),
            pltpu.VMEM((2, edge, (wide + 2) * edge), jnp.float32),
            pltpu.VMEM((slots + 1, NOTE, edge), density.dtype),
            pltpu.VMEM((slots + 1, -(-wide // 8) * 8, edge), jnp.float32),
            pltpu.SemaphoreType.DMA((2 * far + 1,)),
            pltpu.SemaphoreType.DMA,
        ],
        compiler_params=pltpu.CompilerParams(vmem_limit_bytes=56 * 2**20),
        cost_estimate=pl.CostEstimate(flops=17 * 10**9, bytes_accessed=15 * 2**20, transcendentals=0),
    )(which, where, *tables)
    return result[None]


def solution(mesh):
    groups, width = mesh.devices.shape
    devices = Mesh(mesh.devices.reshape(groups // CORES, CORES, width), ("y", "core", "col"))
    axes = ("y", "core", "col")
    in_specs = (P(axes, None, None, None), P(axes, None), P(axes, None))
    out_specs = P(axes, None, None, None)
    return jax.shard_map(shards, mesh=devices, in_specs=in_specs, out_specs=out_specs, check_vma=False)
```

```python
import functools

import jax
import jax.numpy as jnp
from jax import lax
from jax.experimental import pallas as pl
from jax.experimental.pallas import tpu as pltpu
from jax.sharding import PartitionSpec as P

NOTE = 16
AXES = ("row", "col")


def cube(payload, count, half):
    def swap(value, mask):
        return lax.ppermute(value, AXES, [(i, i ^ mask) for i in range(count)])

    x, core, y = 1, 8, 16
    rows = {0: [payload]}
    for z in (2, 4, 6):
        rows[z] = [swap(payload, z)]
    for z in (0, 2, 4, 6):
        rows[z | x] = [swap(rows[z][0], x)]
        rows[z | y] = [swap(rows[z][0], y)]
        if z == 2:
            continue
        rows[z | x | y] = [swap(rows[z | y][0][:half], x), swap(rows[z | x][0][half:], y)]
        if z == 0:
            rows[2 | x | y] = [swap(piece, 2) for piece in rows[x | y]]
    for mask in list(rows):
        rows[mask | core] = [swap(piece, core) for piece in rows[mask]]
    return rows


def window(payload, need, half):
    groups, width = lax.axis_size("row"), lax.axis_size("col")
    count = groups * width
    size = payload.shape[0]
    column = lax.axis_index("col")
    here = lax.axis_index("row") * width + column
    pieces, offsets = [], []
    if (groups, width) == (4, 8):
        for mask, arrays in sorted(cube(payload, count, half).items()):
            start = 0
            for array in arrays:
                pieces.append((array, 1, start))
                offsets.append((((here ^ mask) - here + count // 2) % count - count // 2)[None])
                start += array.shape[0]
    else:
        block = lax.all_gather(payload, "col", axis=0, tiled=True)
        pieces.append((block, width, 0))
        offsets.append(jnp.arange(width, dtype=jnp.int32) - column)
        for hop in range(1, -(-need // width) + 1):
            part = min(width, need - (hop - 1) * width)
            up = [(g, (g + hop) % groups) for g in range(groups)]
            down = [(g, (g - hop) % groups) for g in range(groups)]
            steps = jnp.arange(part, dtype=jnp.int32) - column
            pieces.append((lax.ppermute(block[(width - part) * size :], "row", up), part, 0))
            offsets.append(steps - (hop - 1) * width - part)
            pieces.append((lax.ppermute(block[: part * size], "row", down), part, 0))
            offsets.append(steps + hop * width)
    offsets = jnp.concatenate(offsets).astype(jnp.int32)
    return pieces, jnp.where(jnp.abs(offsets) <= need, offsets + need, -1)


def purify(reach, edge, layout, place, *refs):
    count = len(layout)
    tables, (out, band, square, own, notes, keep, arrived, noted) = refs[:count], refs[count:]
    far = 2 * reach
    slots, wide = 2 * reach + 1, 4 * reach + 1
    kind = band.dtype
    size = slots * edge + NOTE

    def span(first, n):
        first = first * edge
        return pl.ds(first if isinstance(first, int) else pl.multiple_of(first, edge), n * edge)

    base = 0
    for table, (number, start) in zip(tables, layout):
        held = table.shape[0] // number
        first, last = start // edge, min((start + held) // edge, slots)

        def fetch(j, carry, table=table, base=base, start=start, held=held, first=first, last=last):
            k = place[base + j]
            begin = j * held - start

            @pl.when(k >= 0)
            def _():
                def block(s, carry):
                    pltpu.make_async_copy(
                        table.at[pl.ds(pl.multiple_of(begin + s * edge, 16), edge)],
                        band.at[span(k, 1), span(s + 1, 1)],
                        arrived.at[k],
                    ).start()
                    return carry

                lax.fori_loop(first, last, block, 0)

                if start + held == size:

                    @pl.when((k >= reach) & (k <= 3 * reach))
                    def _():
                        pltpu.make_async_copy(
                            table.at[pl.ds(pl.multiple_of(begin + slots * edge, 16), NOTE)],
                            notes.at[k - reach],
                            noted,
                        ).start()

            return carry

        lax.fori_loop(0, number, fetch, 0)
        base += number

    def ready(k):
        whole = tables[0].at[pl.ds(0, slots * edge)]
        pltpu.make_async_copy(whole, band.at[pl.ds(0, slots * edge), pl.ds(0, edge)], arrived.at[k]).wait()

    def clear(k, carry):
        zero = jnp.zeros((edge, edge), kind)
        band[span(k, 1), pl.ds(0, edge)] = zero
        band[span(k, 1), pl.ds((slots + 1) * edge, edge)] = zero
        return carry

    lax.fori_loop(0, 2 * far + 2, clear, 0)
    band[span(2 * far + 1, 1), :] = jnp.zeros((edge, band.shape[1]), kind)

    def clear_square(r, carry):
        zero = jnp.zeros((edge, edge), kind)
        square[span(r, 1), pl.ds(0, edge)] = zero
        square[span(r, 1), pl.ds((wide + 1) * edge, edge)] = zero
        return carry

    lax.fori_loop(0, slots + 1, clear_square, 0)

    for r in range(slots):
        pltpu.make_async_copy(tables[0].at[pl.ds(0, NOTE)], notes.at[r], noted).wait()
    notes[slots] = jnp.zeros(notes.shape[1:], kind)
    spots = keep.shape[1]
    diagonal = lax.broadcasted_iota(jnp.int32, (spots, edge), 0) == lax.broadcasted_iota(jnp.int32, (spots, edge), 1)

    def spread(r, carry):
        line = notes[r].astype(jnp.float32)[:1]
        value = jnp.sum(jnp.where(diagonal, line, 0.0), axis=1, keepdims=True)
        keep[r] = jnp.broadcast_to(value, (spots, edge))
        return carry

    lax.fori_loop(0, slots + 1, spread, 0)

    for k in range(far):
        ready(k)

    def row_pair(pair, carry):
        r = 2 * pair
        ready(r + far)

        @pl.when(r + far + 1 <= 2 * far)
        def _():
            ready(r + far + 1)

        middle = jnp.where((r == reach) | (r + 1 == reach), 1, 0)
        for d in range(-far, far + 1, 2):
            low, high = max(-reach, d - reach), min(reach + 1, d + reach + 1)
            size = high - low + 1
            left = jnp.concatenate(
                [
                    band[span(r + reach, 1), pl.ds((low + reach + 1) * edge, size * edge)],
                    band[span(r + reach + 1, 1), pl.ds((low + reach) * edge, size * edge)],
                ],
                axis=0,
            )
            right = jnp.concatenate(
                [
                    band[span(r + reach + e, 1), pl.ds((d - e + reach + 1) * edge, 2 * edge)]
                    for e in range(low, high + 1)
                ],
                axis=0,
            )
            product = jnp.dot(left, right, preferred_element_type=jnp.float32)
            for i in range(2):
                u = d + far - i
                mask = jnp.concatenate(
                    [keep[r + i, pl.ds(min(max(u + j, 0), wide - 1), 1), :] for j in range(2)], axis=1
                )
                kept = product[i * edge : (i + 1) * edge] * mask
                square[span(r + i, 1), pl.ds((u + 1) * edge, 2 * edge)] = kept.astype(kind)
                if i == reach % 2:
                    own[middle, :, pl.ds((u + 1) * edge, 2 * edge)] = kept
        return carry

    lax.fori_loop(0, (slots + 1) // 2, row_pair, 0)

    for c in range(-far, far + 1, 2):
        low, high = max(-reach, c - far), min(reach, c + far + 1)
        left = band[span(far, 1), pl.ds((low + reach + 1) * edge, (high - low + 1) * edge)]
        right = jnp.concatenate(
            [square[span(r + reach, 1), pl.ds((c - r + far + 1) * edge, 2 * edge)] for r in range(low, high + 1)],
            axis=0,
        )
        cube = jnp.dot(left, right, preferred_element_type=jnp.float32)
        for j in range(2):
            u = c + far + j
            if u < wide:
                kept = own[1, :, pl.ds((u + 1) * edge, edge)]
                value = 3.0 * kept - 2.0 * cube[:, j * edge : (j + 1) * edge]
                out[u] = (keep[reach, pl.ds(u, 1), :] * value).astype(out.dtype)


def shards(density, pattern, filter_mask):
    slots, edge = density.shape[1], density.shape[2]
    wide = filter_mask.shape[1]
    reach = (slots - 1) // 2
    far = 2 * reach
    masked = density[0] * pattern[0][:, None, None].astype(density.dtype)
    note = jnp.zeros((NOTE, edge), density.dtype).at[0, :wide].set(filter_mask[0].astype(density.dtype))
    payload = jnp.concatenate([masked.reshape(slots * edge, edge), note], axis=0)
    half = -(-slots // 2) * edge
    pieces, place = window(payload, far, half)
    tables = [array for array, _, _ in pieces]
    layout = [(number, start) for _, number, start in pieces]
    smem = pl.BlockSpec(memory_space=pltpu.SMEM)
    result = pl.pallas_call(
        functools.partial(purify, reach, edge, layout),
        out_shape=jax.ShapeDtypeStruct((wide, edge, edge), density.dtype),
        in_specs=[smem] + [pl.BlockSpec(memory_space=pl.ANY)] * len(tables),
        out_specs=pl.BlockSpec(memory_space=pltpu.VMEM),
        scratch_shapes=[
            pltpu.VMEM(((2 * far + 2) * edge, (slots + 2) * edge), density.dtype),
            pltpu.VMEM(((slots + 1) * edge, (wide + 2) * edge), density.dtype),
            pltpu.VMEM((2, edge, (wide + 2) * edge), jnp.float32),
            pltpu.VMEM((slots + 1, NOTE, edge), density.dtype),
            pltpu.VMEM((slots + 1, -(-wide // 8) * 8, edge), jnp.float32),
            pltpu.SemaphoreType.DMA((2 * far + 1,)),
            pltpu.SemaphoreType.DMA,
        ],
        compiler_params=pltpu.CompilerParams(vmem_limit_bytes=56 * 2**20),
        cost_estimate=pl.CostEstimate(flops=17 * 10**9, bytes_accessed=15 * 2**20, transcendentals=0),
    )(place, *tables)
    return result[None]


def solution(mesh):
    in_specs = (P(AXES, None, None, None), P(AXES, None), P(AXES, None))
    out_specs = P(AXES, None, None, None)
    return jax.shard_map(shards, mesh=mesh, in_specs=in_specs, out_specs=out_specs, check_vma=False)
```

```python
import functools

import jax
import jax.numpy as jnp
from jax import lax
from jax.experimental import pallas as pl
from jax.experimental.pallas import tpu as pltpu
from jax.sharding import PartitionSpec as P

NOTE = 16
AXES = ("row", "col")


def cube(payload, count, half):
    def swap(value, mask):
        return lax.ppermute(value, AXES, [(i, i ^ mask) for i in range(count)])

    x, z1, z2, z3, core, y = 1, 2, 4, 6, 8, 16
    rows = {0: [payload]}

    def send(target, source, mask):
        rows[target] = [swap(piece, mask) for piece in rows[source]]

    def corner(z):
        rows[z | x | y] = [swap(rows[z | y][0][:half], x), swap(rows[z | x][0][half:], y)]

    send(x, 0, x)
    send(y, 0, y)
    send(z1, 0, z1)
    send(z3, 0, z3)
    corner(0)
    send(z1 | x, z1, x)
    send(z1 | y, z1, y)
    send(z2, z3, z1)
    send(z3 | x, z3, x)
    send(z3 | y, z3, y)
    send(z1 | x | y, x | y, z1)
    send(z3 | x | y, x | y, z3)
    send(z2 | x, z2, x)
    send(z2 | y, z2, y)
    corner(z2)
    for mask in list(rows):
        send(mask | core, mask, core)
    return rows


def window(payload, need, half):
    groups, width = lax.axis_size("row"), lax.axis_size("col")
    count = groups * width
    size = payload.shape[0]
    column = lax.axis_index("col")
    here = lax.axis_index("row") * width + column
    pieces, offsets = [], []
    if (groups, width) == (4, 8):
        for mask, arrays in sorted(cube(payload, count, half).items()):
            start = 0
            for array in arrays:
                pieces.append((array, 1, start))
                offsets.append((((here ^ mask) - here + count // 2) % count - count // 2)[None])
                start += array.shape[0]
    else:
        block = lax.all_gather(payload, "col", axis=0, tiled=True)
        pieces.append((block, width, 0))
        offsets.append(jnp.arange(width, dtype=jnp.int32) - column)
        for hop in range(1, -(-need // width) + 1):
            part = min(width, need - (hop - 1) * width)
            up = [(g, (g + hop) % groups) for g in range(groups)]
            down = [(g, (g - hop) % groups) for g in range(groups)]
            steps = jnp.arange(part, dtype=jnp.int32) - column
            pieces.append((lax.ppermute(block[(width - part) * size :], "row", up), part, 0))
            offsets.append(steps - (hop - 1) * width - part)
            pieces.append((lax.ppermute(block[: part * size], "row", down), part, 0))
            offsets.append(steps + hop * width)
    offsets = jnp.concatenate(offsets).astype(jnp.int32)
    return pieces, jnp.where(jnp.abs(offsets) <= need, offsets + need, -1)


def purify(reach, edge, layout, place, *refs):
    count = len(layout)
    tables, (out, band, square, own, notes, keep, arrived, noted) = refs[:count], refs[count:]
    far = 2 * reach
    slots, wide = 2 * reach + 1, 4 * reach + 1
    kind = band.dtype
    size = slots * edge + NOTE

    def span(first, n):
        first = first * edge
        return pl.ds(first if isinstance(first, int) else pl.multiple_of(first, edge), n * edge)

    base = 0
    for table, (number, start) in zip(tables, layout):
        held = table.shape[0] // number
        first, last = start // edge, min((start + held) // edge, slots)

        def fetch(j, carry, table=table, base=base, start=start, held=held, first=first, last=last):
            k = place[base + j]
            begin = j * held - start

            @pl.when(k >= 0)
            def _():
                def block(s, carry):
                    pltpu.make_async_copy(
                        table.at[pl.ds(pl.multiple_of(begin + s * edge, 16), edge)],
                        band.at[span(k, 1), span(s + 1, 1)],
                        arrived.at[k],
                    ).start()
                    return carry

                lax.fori_loop(first, last, block, 0)

                if start + held == size:

                    @pl.when((k >= reach) & (k <= 3 * reach))
                    def _():
                        pltpu.make_async_copy(
                            table.at[pl.ds(pl.multiple_of(begin + slots * edge, 16), NOTE)],
                            notes.at[k - reach],
                            noted,
                        ).start()

            return carry

        lax.fori_loop(0, number, fetch, 0)
        base += number

    def ready(k):
        whole = tables[0].at[pl.ds(0, slots * edge)]
        pltpu.make_async_copy(whole, band.at[pl.ds(0, slots * edge), pl.ds(0, edge)], arrived.at[k]).wait()

    def clear(k, carry):
        zero = jnp.zeros((edge, edge), kind)
        band[span(k, 1), pl.ds(0, edge)] = zero
        band[span(k, 1), pl.ds((slots + 1) * edge, edge)] = zero
        return carry

    lax.fori_loop(0, 2 * far + 2, clear, 0)
    band[span(2 * far + 1, 1), :] = jnp.zeros((edge, band.shape[1]), kind)

    def clear_square(r, carry):
        zero = jnp.zeros((edge, edge), kind)
        square[span(r, 1), pl.ds(0, edge)] = zero
        square[span(r, 1), pl.ds((wide + 1) * edge, edge)] = zero
        return carry

    lax.fori_loop(0, slots + 1, clear_square, 0)

    for r in range(slots):
        pltpu.make_async_copy(tables[0].at[pl.ds(0, NOTE)], notes.at[r], noted).wait()
    notes[slots] = jnp.zeros(notes.shape[1:], kind)
    spots = keep.shape[1]
    diagonal = lax.broadcasted_iota(jnp.int32, (spots, edge), 0) == lax.broadcasted_iota(jnp.int32, (spots, edge), 1)

    def spread(r, carry):
        line = notes[r].astype(jnp.float32)[:1]
        value = jnp.sum(jnp.where(diagonal, line, 0.0), axis=1, keepdims=True)
        keep[r] = jnp.broadcast_to(value, (spots, edge))
        return carry

    lax.fori_loop(0, slots + 1, spread, 0)

    for k in range(far):
        ready(k)

    def row_pair(pair, carry):
        r = 2 * pair
        ready(r + far)

        @pl.when(r + far + 1 <= 2 * far)
        def _():
            ready(r + far + 1)

        middle = jnp.where((r == reach) | (r + 1 == reach), 1, 0)
        for d in range(-far, far + 1, 2):
            low, high = max(-reach, d - reach), min(reach + 1, d + reach + 1)
            size = high - low + 1
            left = jnp.concatenate(
                [
                    band[span(r + reach, 1), pl.ds((low + reach + 1) * edge, size * edge)],
                    band[span(r + reach + 1, 1), pl.ds((low + reach) * edge, size * edge)],
                ],
                axis=0,
            )
            right = jnp.concatenate(
                [
                    band[span(r + reach + e, 1), pl.ds((d - e + reach + 1) * edge, 2 * edge)]
                    for e in range(low, high + 1)
                ],
                axis=0,
            )
            product = jnp.dot(left, right, preferred_element_type=jnp.float32)
            for i in range(2):
                u = d + far - i
                mask = jnp.concatenate(
                    [keep[r + i, pl.ds(min(max(u + j, 0), wide - 1), 1), :] for j in range(2)], axis=1
                )
                kept = product[i * edge : (i + 1) * edge] * mask
                square[span(r + i, 1), pl.ds((u + 1) * edge, 2 * edge)] = kept.astype(kind)
                if i == reach % 2:
                    own[middle, :, pl.ds((u + 1) * edge, 2 * edge)] = kept
        return carry

    lax.fori_loop(0, (slots + 1) // 2, row_pair, 0)

    for c in range(-far, far + 1, 2):
        low, high = max(-reach, c - far), min(reach, c + far + 1)
        left = band[span(far, 1), pl.ds((low + reach + 1) * edge, (high - low + 1) * edge)]
        right = jnp.concatenate(
            [square[span(r + reach, 1), pl.ds((c - r + far + 1) * edge, 2 * edge)] for r in range(low, high + 1)],
            axis=0,
        )
        cube = jnp.dot(left, right, preferred_element_type=jnp.float32)
        for j in range(2):
            u = c + far + j
            if u < wide:
                kept = own[1, :, pl.ds((u + 1) * edge, edge)]
                value = 3.0 * kept - 2.0 * cube[:, j * edge : (j + 1) * edge]
                out[u] = (keep[reach, pl.ds(u, 1), :] * value).astype(out.dtype)


def shards(density, pattern, filter_mask):
    slots, edge = density.shape[1], density.shape[2]
    wide = filter_mask.shape[1]
    reach = (slots - 1) // 2
    far = 2 * reach
    masked = density[0] * pattern[0][:, None, None].astype(density.dtype)
    note = jnp.zeros((NOTE, edge), density.dtype).at[0, :wide].set(filter_mask[0].astype(density.dtype))
    payload = jnp.concatenate([masked.reshape(slots * edge, edge), note], axis=0)
    half = -(-slots // 2) * edge
    pieces, place = window(payload, far, half)
    tables = [array for array, _, _ in pieces]
    layout = [(number, start) for _, number, start in pieces]
    smem = pl.BlockSpec(memory_space=pltpu.SMEM)
    result = pl.pallas_call(
        functools.partial(purify, reach, edge, layout),
        out_shape=jax.ShapeDtypeStruct((wide, edge, edge), density.dtype),
        in_specs=[smem] + [pl.BlockSpec(memory_space=pl.ANY)] * len(tables),
        out_specs=pl.BlockSpec(memory_space=pltpu.VMEM),
        scratch_shapes=[
            pltpu.VMEM(((2 * far + 2) * edge, (slots + 2) * edge), density.dtype),
            pltpu.VMEM(((slots + 1) * edge, (wide + 2) * edge), density.dtype),
            pltpu.VMEM((2, edge, (wide + 2) * edge), jnp.float32),
            pltpu.VMEM((slots + 1, NOTE, edge), density.dtype),
            pltpu.VMEM((slots + 1, -(-wide // 8) * 8, edge), jnp.float32),
            pltpu.SemaphoreType.DMA((2 * far + 1,)),
            pltpu.SemaphoreType.DMA,
        ],
        compiler_params=pltpu.CompilerParams(vmem_limit_bytes=56 * 2**20),
        cost_estimate=pl.CostEstimate(flops=17 * 10**9, bytes_accessed=15 * 2**20, transcendentals=0),
    )(place, *tables)
    return result[None]


def solution(mesh):
    in_specs = (P(AXES, None, None, None), P(AXES, None), P(AXES, None))
    out_specs = P(AXES, None, None, None)
    return jax.shard_map(shards, mesh=mesh, in_specs=in_specs, out_specs=out_specs, check_vma=False)
```

```python
import functools

import jax
import jax.numpy as jnp
from jax import lax
from jax.experimental import pallas as pl
from jax.experimental.pallas import tpu as pltpu
from jax.sharding import PartitionSpec as P

NOTE = 16
AXES = ("row", "col")


def cube(own, count, here):
    x, z1, z2, z3, core, y = 1, 2, 4, 6, 8, 16

    def inner(i):
        return (i // 2) % 4 in (1, 2)

    def swap(value, mask):
        return lax.ppermute(value, AXES, [(i, i ^ mask) for i in range(count)])

    def middle(value):
        return lax.ppermute(value, AXES, [(i, i ^ z3) for i in range(count) if inner(i)])

    def outward(value):
        return lax.ppermute(value, AXES, [(i, i ^ z1) for i in range(count) if inner(i)])

    within = ((here // 2) % 4 == 1) | ((here // 2) % 4 == 2)
    near, far = jnp.where(within, z3, z2), jnp.where(within, z2, z3)
    both = lax.optimization_barrier
    found = []

    def cross(*rows):
        arrays = [array for array, _ in rows]
        masks = [mask for _, mask in rows]
        found.extend((array, [mask]) for array, mask in rows)
        batch = swap(jnp.concatenate(arrays, axis=0) if len(arrays) > 1 else arrays[0], core)
        found.append((batch, [jnp.where(mask >= 0, mask | core, -1) for mask in masks]))
        return len(found) - 1

    def finish(spot, *arrays):
        batch, *arrays = both((found[spot][0],) + arrays)
        found[spot] = (batch, found[spot][1])
        return arrays

    x0, y0, f, b2 = swap(own, x), swap(own, y), swap(own, z1), middle(own)
    spot = cross((own, 0))
    x0, y0, f, b2 = finish(spot, x0, y0, f, b2)
    d0, yf, c3, b4 = swap(y0, x), swap(f, y), middle(f), outward(b2)
    spot = cross((x0, x), (y0, y), (f, z1))
    d0, yf, c3, b4, b2, f = finish(spot, d0, yf, c3, b4, b2, f)
    b = jnp.where(within, b2, b4)
    xb, yb, c5, db2 = swap(b, x), swap(b, y), outward(c3), middle(d0)
    spot = cross((d0, x | y), (yf, z1 | y), (b, near))
    xb, yb, c5, db2, c3, d0, f = finish(spot, xb, yb, c5, db2, c3, d0, f)
    c = jnp.where(within, c3, c5)
    xc, yc, df = swap(c, x), swap(c, y), swap(d0, z1)
    spot = cross((xb, near | x), (yb, near | y), (c, far))
    xc, yc, df, f, db2 = finish(spot, xc, yc, df, f, db2)
    xf, dc, db4 = swap(f, x), swap(xc, y), outward(db2)
    spot = cross((xc, far | x), (yc, far | y), (df, z1 | x | y), (db2, jnp.where(within, z3 | x | y, -1)))
    xf, dc, db4 = finish(spot, xf, dc, db4)
    cross((xf, z1 | x))
    cross((dc, far | x | y))
    cross((db4, jnp.where(within, -1, z2 | x | y)))
    return found


def window(payload, need):
    groups, width = lax.axis_size("row"), lax.axis_size("col")
    count = groups * width
    size = payload.shape[0]
    column = lax.axis_index("col")
    here = lax.axis_index("row") * width + column
    pieces, offsets = [], []
    if (groups, width) == (4, 8):
        for array, masks in cube(payload, count, here):
            pieces.append((array, len(masks)))
            for mask in masks:
                offset = ((here ^ mask) - here + count // 2) % count - count // 2
                offsets.append(jnp.where(mask >= 0, offset, need + 1)[None])
    else:
        block = lax.all_gather(payload, "col", axis=0, tiled=True)
        pieces.append((block, width))
        offsets.append(jnp.arange(width, dtype=jnp.int32) - column)
        for hop in range(1, -(-need // width) + 1):
            part = min(width, need - (hop - 1) * width)
            up = [(g, (g + hop) % groups) for g in range(groups)]
            down = [(g, (g - hop) % groups) for g in range(groups)]
            steps = jnp.arange(part, dtype=jnp.int32) - column
            pieces.append((lax.ppermute(block[(width - part) * size :], "row", up), part))
            offsets.append(steps - (hop - 1) * width - part)
            pieces.append((lax.ppermute(block[: part * size], "row", down), part))
            offsets.append(steps + hop * width)
    offsets = jnp.concatenate(offsets).astype(jnp.int32)
    return pieces, jnp.where(jnp.abs(offsets) <= need, offsets + need, -1)


def purify(reach, edge, layout, place, *refs):
    count = len(layout)
    tables, (out, band, square, own, notes, keep, arrived, noted) = refs[:count], refs[count:]
    far = 2 * reach
    slots, wide = 2 * reach + 1, 4 * reach + 1
    kind = band.dtype
    size = slots * edge + NOTE

    def span(first, n):
        first = first * edge
        return pl.ds(first if isinstance(first, int) else pl.multiple_of(first, edge), n * edge)

    base = 0
    for table, number in zip(tables, layout):

        def fetch(j, carry, table=table, base=base):
            k = place[base + j]
            begin = j * size

            @pl.when(k >= 0)
            def _():
                def block(s, carry):
                    pltpu.make_async_copy(
                        table.at[pl.ds(pl.multiple_of(begin + s * edge, 16), edge)],
                        band.at[span(k, 1), span(s + 1, 1)],
                        arrived.at[k],
                    ).start()
                    return carry

                lax.fori_loop(0, slots, block, 0)

                @pl.when((k >= reach) & (k <= 3 * reach))
                def _():
                    pltpu.make_async_copy(
                        table.at[pl.ds(pl.multiple_of(begin + slots * edge, 16), NOTE)], notes.at[k - reach], noted
                    ).start()

            return carry

        lax.fori_loop(0, number, fetch, 0)
        base += number

    def ready(k):
        whole = tables[0].at[pl.ds(0, slots * edge)]
        pltpu.make_async_copy(whole, band.at[pl.ds(0, slots * edge), pl.ds(0, edge)], arrived.at[k]).wait()

    def clear(k, carry):
        zero = jnp.zeros((edge, edge), kind)
        band[span(k, 1), pl.ds(0, edge)] = zero
        band[span(k, 1), pl.ds((slots + 1) * edge, edge)] = zero
        return carry

    lax.fori_loop(0, 2 * far + 2, clear, 0)
    band[span(2 * far + 1, 1), :] = jnp.zeros((edge, band.shape[1]), kind)

    def clear_square(r, carry):
        zero = jnp.zeros((edge, edge), kind)
        square[span(r, 1), pl.ds(0, edge)] = zero
        square[span(r, 1), pl.ds((wide + 1) * edge, edge)] = zero
        return carry

    lax.fori_loop(0, slots + 1, clear_square, 0)

    for r in range(slots):
        pltpu.make_async_copy(tables[0].at[pl.ds(0, NOTE)], notes.at[r], noted).wait()
    notes[slots] = jnp.zeros(notes.shape[1:], kind)
    spots = keep.shape[1]
    diagonal = lax.broadcasted_iota(jnp.int32, (spots, edge), 0) == lax.broadcasted_iota(jnp.int32, (spots, edge), 1)

    def spread(r, carry):
        line = notes[r].astype(jnp.float32)[:1]
        value = jnp.sum(jnp.where(diagonal, line, 0.0), axis=1, keepdims=True)
        keep[r] = jnp.broadcast_to(value, (spots, edge))
        return carry

    lax.fori_loop(0, slots + 1, spread, 0)

    for k in range(far):
        ready(k)

    def row_pair(pair, carry):
        r = 2 * pair
        ready(r + far)

        @pl.when(r + far + 1 <= 2 * far)
        def _():
            ready(r + far + 1)

        middle = jnp.where((r == reach) | (r + 1 == reach), 1, 0)
        for d in range(-far, far + 1, 2):
            low, high = max(-reach, d - reach), min(reach + 1, d + reach + 1)
            size = high - low + 1
            left = jnp.concatenate(
                [
                    band[span(r + reach, 1), pl.ds((low + reach + 1) * edge, size * edge)],
                    band[span(r + reach + 1, 1), pl.ds((low + reach) * edge, size * edge)],
                ],
                axis=0,
            )
            right = jnp.concatenate(
                [
                    band[span(r + reach + e, 1), pl.ds((d - e + reach + 1) * edge, 2 * edge)]
                    for e in range(low, high + 1)
                ],
                axis=0,
            )
            product = jnp.dot(left, right, preferred_element_type=jnp.float32)
            for i in range(2):
                u = d + far - i
                mask = jnp.concatenate(
                    [keep[r + i, pl.ds(min(max(u + j, 0), wide - 1), 1), :] for j in range(2)], axis=1
                )
                kept = product[i * edge : (i + 1) * edge] * mask
                square[span(r + i, 1), pl.ds((u + 1) * edge, 2 * edge)] = kept.astype(kind)
                if i == reach % 2:
                    own[middle, :, pl.ds((u + 1) * edge, 2 * edge)] = kept
        return carry

    lax.fori_loop(0, (slots + 1) // 2, row_pair, 0)

    for c in range(-far, far + 1, 2):
        low, high = max(-reach, c - far), min(reach, c + far + 1)
        left = band[span(far, 1), pl.ds((low + reach + 1) * edge, (high - low + 1) * edge)]
        right = jnp.concatenate(
            [square[span(r + reach, 1), pl.ds((c - r + far + 1) * edge, 2 * edge)] for r in range(low, high + 1)],
            axis=0,
        )
        cube = jnp.dot(left, right, preferred_element_type=jnp.float32)
        for j in range(2):
            u = c + far + j
            if u < wide:
                kept = own[1, :, pl.ds((u + 1) * edge, edge)]
                value = 3.0 * kept - 2.0 * cube[:, j * edge : (j + 1) * edge]
                out[u] = (keep[reach, pl.ds(u, 1), :] * value).astype(out.dtype)


def shards(density, pattern, filter_mask):
    slots, edge = density.shape[1], density.shape[2]
    wide = filter_mask.shape[1]
    reach = (slots - 1) // 2
    far = 2 * reach
    masked = density[0] * pattern[0][:, None, None].astype(density.dtype)
    note = jnp.zeros((NOTE, edge), density.dtype).at[0, :wide].set(filter_mask[0].astype(density.dtype))
    payload = jnp.concatenate([masked.reshape(slots * edge, edge), note], axis=0)
    pieces, place = window(payload, far)
    tables = [array for array, _ in pieces]
    layout = [number for _, number in pieces]
    smem = pl.BlockSpec(memory_space=pltpu.SMEM)
    result = pl.pallas_call(
        functools.partial(purify, reach, edge, layout),
        out_shape=jax.ShapeDtypeStruct((wide, edge, edge), density.dtype),
        in_specs=[smem] + [pl.BlockSpec(memory_space=pl.ANY)] * len(tables),
        out_specs=pl.BlockSpec(memory_space=pltpu.VMEM),
        scratch_shapes=[
            pltpu.VMEM(((2 * far + 2) * edge, (slots + 2) * edge), density.dtype),
            pltpu.VMEM(((slots + 1) * edge, (wide + 2) * edge), density.dtype),
            pltpu.VMEM((2, edge, (wide + 2) * edge), jnp.float32),
            pltpu.VMEM((slots + 1, NOTE, edge), density.dtype),
            pltpu.VMEM((slots + 1, -(-wide // 8) * 8, edge), jnp.float32),
            pltpu.SemaphoreType.DMA((2 * far + 1,)),
            pltpu.SemaphoreType.DMA,
        ],
        compiler_params=pltpu.CompilerParams(vmem_limit_bytes=56 * 2**20),
        cost_estimate=pl.CostEstimate(flops=17 * 10**9, bytes_accessed=15 * 2**20, transcendentals=0),
    )(place, *tables)
    return result[None]


def solution(mesh):
    in_specs = (P(AXES, None, None, None), P(AXES, None), P(AXES, None))
    out_specs = P(AXES, None, None, None)
    return jax.shard_map(shards, mesh=mesh, in_specs=in_specs, out_specs=out_specs, check_vma=False)
```

```python
import functools

import jax
import jax.numpy as jnp
from jax import lax
from jax.experimental import pallas as pl
from jax.experimental.pallas import tpu as pltpu
from jax.sharding import PartitionSpec as P

NOTE = 16
AXES = ("row", "col")


def cube(own, count, here):
    x, z1, z2, z3, core, y = 1, 2, 4, 6, 8, 16

    def inner(i):
        return (i // 2) % 4 in (1, 2)

    def swap(value, mask):
        return lax.ppermute(value, AXES, [(i, i ^ mask) for i in range(count)])

    def middle(value):
        return lax.ppermute(value, AXES, [(i, i ^ z3) for i in range(count) if inner(i)])

    def outward(value):
        return lax.ppermute(value, AXES, [(i, i ^ z1) for i in range(count) if inner(i)])

    within = ((here // 2) % 4 == 1) | ((here // 2) % 4 == 2)
    near, far = jnp.where(within, z3, z2), jnp.where(within, z2, z3)
    both = lax.optimization_barrier
    found = []

    def cross(*rows):
        rows = [(array, mask if isinstance(mask, tuple) else (mask,)) for array, mask in rows]
        arrays = [array for array, _ in rows]
        masks = [mask for _, group in rows for mask in group]
        found.extend(rows)
        batch = swap(jnp.concatenate(arrays, axis=0) if len(arrays) > 1 else arrays[0], core)
        found.append((batch, [jnp.where(mask >= 0, mask | core, -1) for mask in masks]))
        return len(found) - 1

    def finish(spot, *arrays):
        batch, *arrays = both((found[spot][0],) + arrays)
        found[spot] = (batch, found[spot][1])
        return arrays

    x0, y0, d0, f, b2 = swap(own, x), swap(own, y), swap(own, x | y), swap(own, z1), middle(own)
    f, b2 = both((f, b2))
    c3, b4 = middle(f), outward(b2)
    own, x0, y0, d0, f, b2, c3, b4 = both((own, x0, y0, d0, f, b2, c3, b4))
    b = jnp.where(within, b2, b4)
    pair = jnp.concatenate([f, b], axis=0)
    xfb, yfb, db2 = swap(pair, x), swap(pair, y), middle(d0)
    across = swap(jnp.concatenate([c3, d0], axis=0), z1)
    spot = cross((own, 0), (x0, x), (y0, y), (d0, x | y), (f, z1), (b, near))
    xfb, yfb, db2, across = finish(spot, xfb, yfb, db2, across)
    size = own.shape[0]
    c, df = jnp.where(within, c3, across[:size]), across[size:]
    xc, yc, db4 = swap(c, x), swap(c, y), outward(db2)
    spot = cross(
        (c, far),
        (xfb, (z1 | x, near | x)),
        (yfb, (z1 | y, near | y)),
        (df, z1 | x | y),
        (db2, jnp.where(within, z3 | x | y, -1)),
    )
    xc, yc, db4 = finish(spot, xc, yc, db4)
    half = size // 2 // 16 * 16
    first, second = swap(yc[:half], x), swap(xc[half:], y)
    spots = [cross((xc, far | x)), cross((yc, far | y)), cross((db4, jnp.where(within, -1, z2 | x | y)))]
    first, second = finish(spots[0], first, second)
    cross((jnp.concatenate([first, second], axis=0), far | x | y))
    return found


def window(payload, need):
    groups, width = lax.axis_size("row"), lax.axis_size("col")
    count = groups * width
    size = payload.shape[0]
    column = lax.axis_index("col")
    here = lax.axis_index("row") * width + column
    pieces, offsets = [], []
    if (groups, width) == (4, 8):
        for array, masks in cube(payload, count, here):
            pieces.append((array, len(masks)))
            for mask in masks:
                offset = ((here ^ mask) - here + count // 2) % count - count // 2
                offsets.append(jnp.where(mask >= 0, offset, need + 1)[None])
    else:
        block = lax.all_gather(payload, "col", axis=0, tiled=True)
        pieces.append((block, width))
        offsets.append(jnp.arange(width, dtype=jnp.int32) - column)
        for hop in range(1, -(-need // width) + 1):
            part = min(width, need - (hop - 1) * width)
            up = [(g, (g + hop) % groups) for g in range(groups)]
            down = [(g, (g - hop) % groups) for g in range(groups)]
            steps = jnp.arange(part, dtype=jnp.int32) - column
            pieces.append((lax.ppermute(block[(width - part) * size :], "row", up), part))
            offsets.append(steps - (hop - 1) * width - part)
            pieces.append((lax.ppermute(block[: part * size], "row", down), part))
            offsets.append(steps + hop * width)
    offsets = jnp.concatenate(offsets).astype(jnp.int32)
    return pieces, jnp.where(jnp.abs(offsets) <= need, offsets + need, -1)


def purify(reach, edge, layout, place, *refs):
    count = len(layout)
    tables, (out, band, square, own, notes, keep, arrived, noted) = refs[:count], refs[count:]
    far = 2 * reach
    slots, wide = 2 * reach + 1, 4 * reach + 1
    kind = band.dtype
    size = slots * edge + NOTE

    def span(first, n):
        first = first * edge
        return pl.ds(first if isinstance(first, int) else pl.multiple_of(first, edge), n * edge)

    base = 0
    for table, number in zip(tables, layout):

        def fetch(j, carry, table=table, base=base):
            k = place[base + j]
            begin = j * size

            @pl.when(k >= 0)
            def _():
                def block(s, carry):
                    pltpu.make_async_copy(
                        table.at[pl.ds(pl.multiple_of(begin + s * edge, 16), edge)],
                        band.at[span(k, 1), span(s + 1, 1)],
                        arrived.at[k],
                    ).start()
                    return carry

                lax.fori_loop(0, slots, block, 0)

                @pl.when((k >= reach) & (k <= 3 * reach))
                def _():
                    pltpu.make_async_copy(
                        table.at[pl.ds(pl.multiple_of(begin + slots * edge, 16), NOTE)], notes.at[k - reach], noted
                    ).start()

            return carry

        lax.fori_loop(0, number, fetch, 0)
        base += number

    def ready(k):
        whole = tables[0].at[pl.ds(0, slots * edge)]
        pltpu.make_async_copy(whole, band.at[pl.ds(0, slots * edge), pl.ds(0, edge)], arrived.at[k]).wait()

    def clear(k, carry):
        zero = jnp.zeros((edge, edge), kind)
        band[span(k, 1), pl.ds(0, edge)] = zero
        band[span(k, 1), pl.ds((slots + 1) * edge, edge)] = zero
        return carry

    lax.fori_loop(0, 2 * far + 2, clear, 0)
    band[span(2 * far + 1, 1), :] = jnp.zeros((edge, band.shape[1]), kind)

    def clear_square(r, carry):
        zero = jnp.zeros((edge, edge), kind)
        square[span(r, 1), pl.ds(0, edge)] = zero
        square[span(r, 1), pl.ds((wide + 1) * edge, edge)] = zero
        return carry

    lax.fori_loop(0, slots + 1, clear_square, 0)

    for r in range(slots):
        pltpu.make_async_copy(tables[0].at[pl.ds(0, NOTE)], notes.at[r], noted).wait()
    notes[slots] = jnp.zeros(notes.shape[1:], kind)
    spots = keep.shape[1]
    diagonal = lax.broadcasted_iota(jnp.int32, (spots, edge), 0) == lax.broadcasted_iota(jnp.int32, (spots, edge), 1)

    def spread(r, carry):
        line = notes[r].astype(jnp.float32)[:1]
        value = jnp.sum(jnp.where(diagonal, line, 0.0), axis=1, keepdims=True)
        keep[r] = jnp.broadcast_to(value, (spots, edge))
        return carry

    lax.fori_loop(0, slots + 1, spread, 0)

    for k in range(far):
        ready(k)

    def row_pair(pair, carry):
        r = 2 * pair
        ready(r + far)

        @pl.when(r + far + 1 <= 2 * far)
        def _():
            ready(r + far + 1)

        middle = jnp.where((r == reach) | (r + 1 == reach), 1, 0)
        for d in range(-far, far + 1, 2):
            low, high = max(-reach, d - reach), min(reach + 1, d + reach + 1)
            size = high - low + 1
            left = jnp.concatenate(
                [
                    band[span(r + reach, 1), pl.ds((low + reach + 1) * edge, size * edge)],
                    band[span(r + reach + 1, 1), pl.ds((low + reach) * edge, size * edge)],
                ],
                axis=0,
            )
            right = jnp.concatenate(
                [
                    band[span(r + reach + e, 1), pl.ds((d - e + reach + 1) * edge, 2 * edge)]
                    for e in range(low, high + 1)
                ],
                axis=0,
            )
            product = jnp.dot(left, right, preferred_element_type=jnp.float32)
            for i in range(2):
                u = d + far - i
                mask = jnp.concatenate(
                    [keep[r + i, pl.ds(min(max(u + j, 0), wide - 1), 1), :] for j in range(2)], axis=1
                )
                kept = product[i * edge : (i + 1) * edge] * mask
                square[span(r + i, 1), pl.ds((u + 1) * edge, 2 * edge)] = kept.astype(kind)
                if i == reach % 2:
                    own[middle, :, pl.ds((u + 1) * edge, 2 * edge)] = kept
        return carry

    lax.fori_loop(0, (slots + 1) // 2, row_pair, 0)

    for c in range(-far, far + 1, 2):
        low, high = max(-reach, c - far), min(reach, c + far + 1)
        left = band[span(far, 1), pl.ds((low + reach + 1) * edge, (high - low + 1) * edge)]
        right = jnp.concatenate(
            [square[span(r + reach, 1), pl.ds((c - r + far + 1) * edge, 2 * edge)] for r in range(low, high + 1)],
            axis=0,
        )
        cube = jnp.dot(left, right, preferred_element_type=jnp.float32)
        for j in range(2):
            u = c + far + j
            if u < wide:
                kept = own[1, :, pl.ds((u + 1) * edge, edge)]
                value = 3.0 * kept - 2.0 * cube[:, j * edge : (j + 1) * edge]
                out[u] = (keep[reach, pl.ds(u, 1), :] * value).astype(out.dtype)


def shards(density, pattern, filter_mask):
    slots, edge = density.shape[1], density.shape[2]
    wide = filter_mask.shape[1]
    reach = (slots - 1) // 2
    far = 2 * reach
    masked = density[0] * pattern[0][:, None, None].astype(density.dtype)
    note = jnp.zeros((NOTE, edge), density.dtype).at[0, :wide].set(filter_mask[0].astype(density.dtype))
    payload = jnp.concatenate([masked.reshape(slots * edge, edge), note], axis=0)
    pieces, place = window(payload, far)
    tables = [array for array, _ in pieces]
    layout = [number for _, number in pieces]
    smem = pl.BlockSpec(memory_space=pltpu.SMEM)
    result = pl.pallas_call(
        functools.partial(purify, reach, edge, layout),
        out_shape=jax.ShapeDtypeStruct((wide, edge, edge), density.dtype),
        in_specs=[smem] + [pl.BlockSpec(memory_space=pl.ANY)] * len(tables),
        out_specs=pl.BlockSpec(memory_space=pltpu.VMEM),
        scratch_shapes=[
            pltpu.VMEM(((2 * far + 2) * edge, (slots + 2) * edge), density.dtype),
            pltpu.VMEM(((slots + 1) * edge, (wide + 2) * edge), density.dtype),
            pltpu.VMEM((2, edge, (wide + 2) * edge), jnp.float32),
            pltpu.VMEM((slots + 1, NOTE, edge), density.dtype),
            pltpu.VMEM((slots + 1, -(-wide // 8) * 8, edge), jnp.float32),
            pltpu.SemaphoreType.DMA((2 * far + 1,)),
            pltpu.SemaphoreType.DMA,
        ],
        compiler_params=pltpu.CompilerParams(vmem_limit_bytes=56 * 2**20),
        cost_estimate=pl.CostEstimate(flops=17 * 10**9, bytes_accessed=15 * 2**20, transcendentals=0),
    )(place, *tables)
    return result[None]


def solution(mesh):
    in_specs = (P(AXES, None, None, None), P(AXES, None), P(AXES, None))
    out_specs = P(AXES, None, None, None)
    return jax.shard_map(shards, mesh=mesh, in_specs=in_specs, out_specs=out_specs, check_vma=False)
```

```python
import functools

import jax
import jax.numpy as jnp
from jax import lax
from jax.experimental import pallas as pl
from jax.experimental.pallas import tpu as pltpu
from jax.sharding import PartitionSpec as P

NOTE = 16
AXES = ("row", "col")


def cube(own, count, here, cut):
    x, z1, z2, z3, core, y = 1, 2, 4, 6, 8, 16
    full = own.shape[0]
    found = []

    def swap(value, mask):
        return lax.ppermute(value, AXES, [(i, i ^ mask) for i in range(count)])

    def whole(*masks):
        return [(mask, 0, full) for mask in masks]

    def cross(*items):
        arrays = [array for array, _ in items]
        batch = swap(jnp.concatenate(arrays, axis=0) if len(arrays) > 1 else arrays[0], core)
        found.extend(items)
        found.append((batch, [(mask | core, start, size) for _, parts in items for mask, start, size in parts]))
        return len(found) - 1

    def finish(spot, *arrays):
        batch, *arrays = lax.optimization_barrier((found[spot][0],) + arrays)
        found[spot] = (batch, found[spot][1])
        return arrays

    x0, y0, d0, f1, f3 = (swap(own, mask) for mask in (x, y, x | y, z1, z3))
    own, x0, y0, d0, f1, f3 = lax.optimization_barrier((own, x0, y0, d0, f1, f3))
    pair = jnp.concatenate([f1, f3], axis=0)
    xp, yp, f2, d2 = swap(pair, x), swap(pair, y), swap(f3, z1), swap(d0, z2)
    spot = cross(
        (own, whole(0)), (x0, whole(x)), (y0, whole(y)), (d0, whole(x | y)), (f1, whole(z1)), (f3, whole(z3))
    )
    xp, yp, f2, d2, d0 = finish(spot, xp, yp, f2, d2, d0)
    xl = swap(jnp.concatenate([f2, yp[full : full + cut]], axis=0), x)
    yl = swap(jnp.concatenate([f2, xp[full + cut :]], axis=0), y)
    d1 = swap(d0, z1)
    spot = cross(
        (f2, whole(z2)), (d2, whole(z2 | x | y)), (xp, whole(z1 | x, z3 | x)), (yp, whole(z1 | y, z3 | y))
    )
    xl, yl, d1 = finish(spot, xl, yl, d1)
    cross((xl, [(z2 | x, 0, full), (z3 | x | y, 0, cut)]))
    cross((yl, [(z2 | y, 0, full), (z3 | x | y, cut, full - cut)]))
    cross((d1, whole(z1 | x | y)))
    return found


def window(payload, need, cut):
    groups, width = lax.axis_size("row"), lax.axis_size("col")
    count = groups * width
    size = payload.shape[0]
    column = lax.axis_index("col")
    here = lax.axis_index("row") * width + column
    pieces, offsets = [], []
    if (groups, width) == (4, 8):
        for array, parts in cube(payload, count, here, cut):
            pieces.append((array, [(start, rows) for _, start, rows in parts]))
            for mask, _, _ in parts:
                offsets.append((((here ^ mask) - here + count // 2) % count - count // 2)[None])
    else:
        block = lax.all_gather(payload, "col", axis=0, tiled=True)
        pieces.append((block, [(0, size)] * width))
        offsets.append(jnp.arange(width, dtype=jnp.int32) - column)
        for hop in range(1, -(-need // width) + 1):
            part = min(width, need - (hop - 1) * width)
            up = [(g, (g + hop) % groups) for g in range(groups)]
            down = [(g, (g - hop) % groups) for g in range(groups)]
            steps = jnp.arange(part, dtype=jnp.int32) - column
            pieces.append((lax.ppermute(block[(width - part) * size :], "row", up), [(0, size)] * part))
            offsets.append(steps - (hop - 1) * width - part)
            pieces.append((lax.ppermute(block[: part * size], "row", down), [(0, size)] * part))
            offsets.append(steps + hop * width)
    offsets = jnp.concatenate(offsets).astype(jnp.int32)
    return pieces, jnp.where(jnp.abs(offsets) <= need, offsets + need, -1)


def purify(reach, edge, layout, place, *refs):
    count = len(layout)
    tables, (out, band, square, own, notes, keep, arrived, noted) = refs[:count], refs[count:]
    far = 2 * reach
    slots, wide = 2 * reach + 1, 4 * reach + 1
    pitch = slots + 2
    kind = band.dtype

    def span(first, n):
        first = first * edge
        return pl.ds(first if isinstance(first, int) else pl.multiple_of(first, edge), n * edge)

    base = 0
    for table, parts in zip(tables, layout):
        begin = 0
        for start, size in parts:
            k = place[base]
            body = min(size, slots * edge - start)

            @pl.when(k >= 0)
            def _(table=table, begin=begin, start=start, size=size, body=body, k=k):
                pltpu.make_async_copy(
                    table.at[pl.ds(begin, body)],
                    band.at[pl.ds(pl.multiple_of((k * pitch + 1) * edge + start, edge), body)],
                    arrived.at[k],
                ).start()
                if size > body:

                    @pl.when((k >= reach) & (k <= 3 * reach))
                    def _():
                        pltpu.make_async_copy(
                            table.at[pl.ds(begin + body, NOTE)], notes.at[k - reach], noted
                        ).start()

            begin += size
            base += 1

    def ready(k):
        body = pl.ds(0, slots * edge)
        pltpu.make_async_copy(tables[0].at[body], band.at[body], arrived.at[k]).wait()

    def clear(k, carry):
        zero = jnp.zeros((edge, edge), kind)
        band[span(k * pitch, 1), :] = zero
        band[span(k * pitch + slots + 1, 1), :] = zero
        return carry

    lax.fori_loop(0, 2 * far + 2, clear, 0)

    def clear_last(s, carry):
        band[span((2 * far + 1) * pitch + s, 1), :] = jnp.zeros((edge, edge), kind)
        return carry

    lax.fori_loop(1, slots + 1, clear_last, 0)

    def clear_square(r, carry):
        zero = jnp.zeros((edge, edge), kind)
        square[span(r, 1), pl.ds(0, edge)] = zero
        square[span(r, 1), pl.ds((wide + 1) * edge, edge)] = zero
        return carry

    lax.fori_loop(0, slots + 1, clear_square, 0)

    for r in range(slots):
        pltpu.make_async_copy(tables[0].at[pl.ds(0, NOTE)], notes.at[r], noted).wait()
    notes[slots] = jnp.zeros(notes.shape[1:], kind)
    spots = keep.shape[1]
    diagonal = lax.broadcasted_iota(jnp.int32, (spots, edge), 0) == lax.broadcasted_iota(jnp.int32, (spots, edge), 1)

    def spread(r, carry):
        line = notes[r].astype(jnp.float32)[:1]
        value = jnp.sum(jnp.where(diagonal, line, 0.0), axis=1, keepdims=True)
        keep[r] = jnp.broadcast_to(value, (spots, edge))
        return carry

    lax.fori_loop(0, slots + 1, spread, 0)

    for k in range(far):
        ready(k)

    def strip(k, first, n):
        return jnp.concatenate([band[span(k * pitch + first + s, 1), :] for s in range(n)], axis=1)

    def row_pair(pair, carry):
        r = 2 * pair
        ready(r + far)

        @pl.when(r + far + 1 <= 2 * far)
        def _():
            ready(r + far + 1)

        middle = jnp.where((r == reach) | (r + 1 == reach), 1, 0)
        for d in range(-far, far + 1, 2):
            low, high = max(-reach, d - reach), min(reach + 1, d + reach + 1)
            size = high - low + 1
            left = jnp.concatenate(
                [strip(r + reach, low + reach + 1, size), strip(r + reach + 1, low + reach, size)], axis=0
            )
            right = jnp.concatenate(
                [strip(r + reach + e, d - e + reach + 1, 2) for e in range(low, high + 1)], axis=0
            )
            product = jnp.dot(left, right, preferred_element_type=jnp.float32)
            for i in range(2):
                u = d + far - i
                mask = jnp.concatenate(
                    [keep[r + i, pl.ds(min(max(u + j, 0), wide - 1), 1), :] for j in range(2)], axis=1
                )
                kept = product[i * edge : (i + 1) * edge] * mask
                square[span(r + i, 1), pl.ds((u + 1) * edge, 2 * edge)] = kept.astype(kind)
                if i == reach % 2:
                    own[middle, :, pl.ds((u + 1) * edge, 2 * edge)] = kept
        return carry

    lax.fori_loop(0, (slots + 1) // 2, row_pair, 0)

    for c in range(-far, far + 1, 2):
        low, high = max(-reach, c - far), min(reach, c + far + 1)
        left = strip(far, low + reach + 1, high - low + 1)
        right = jnp.concatenate(
            [square[span(r + reach, 1), pl.ds((c - r + far + 1) * edge, 2 * edge)] for r in range(low, high + 1)],
            axis=0,
        )
        cube = jnp.dot(left, right, preferred_element_type=jnp.float32)
        for j in range(2):
            u = c + far + j
            if u < wide:
                kept = own[1, :, pl.ds((u + 1) * edge, edge)]
                value = 3.0 * kept - 2.0 * cube[:, j * edge : (j + 1) * edge]
                out[u] = (keep[reach, pl.ds(u, 1), :] * value).astype(out.dtype)


def pack(pattern, filter_mask, density, payload):
    slots, edge = density.shape[0], density.shape[1]
    for s in range(slots):
        scale = pattern[0, s].astype(jnp.float32)
        payload[s * edge : (s + 1) * edge] = (density[s].astype(jnp.float32) * scale).astype(payload.dtype)
    lane = lax.broadcasted_iota(jnp.int32, (NOTE, edge), 1)
    note = jnp.zeros((NOTE, edge), jnp.float32)
    for u in range(filter_mask.shape[1]):
        note = jnp.where(lane == u, filter_mask[0, u].astype(jnp.float32), note)
    payload[slots * edge :] = note.astype(payload.dtype)


def shards(density, pattern, filter_mask):
    slots, edge = density.shape[1], density.shape[2]
    wide = filter_mask.shape[1]
    reach = (slots - 1) // 2
    far = 2 * reach
    smem, vmem = pl.BlockSpec(memory_space=pltpu.SMEM), pl.BlockSpec(memory_space=pltpu.VMEM)
    payload = pl.pallas_call(
        pack,
        out_shape=jax.ShapeDtypeStruct((slots * edge + NOTE, edge), density.dtype),
        in_specs=[smem, smem, vmem],
        out_specs=vmem,
    )(pattern, filter_mask, density[0])
    pieces, place = window(payload, far, (slots + 1) // 2 * edge)
    tables = [array for array, _ in pieces]
    layout = [parts for _, parts in pieces]
    result = pl.pallas_call(
        functools.partial(purify, reach, edge, layout),
        out_shape=jax.ShapeDtypeStruct((wide, edge, edge), density.dtype),
        in_specs=[smem] + [pl.BlockSpec(memory_space=pl.ANY)] * len(tables),
        out_specs=vmem,
        scratch_shapes=[
            pltpu.VMEM(((2 * far + 2) * (slots + 2) * edge, edge), density.dtype),
            pltpu.VMEM(((slots + 1) * edge, (wide + 2) * edge), density.dtype),
            pltpu.VMEM((2, edge, (wide + 2) * edge), jnp.float32),
            pltpu.VMEM((slots + 1, NOTE, edge), density.dtype),
            pltpu.VMEM((slots + 1, -(-wide // 8) * 8, edge), jnp.float32),
            pltpu.SemaphoreType.DMA((2 * far + 1,)),
            pltpu.SemaphoreType.DMA,
        ],
        compiler_params=pltpu.CompilerParams(vmem_limit_bytes=56 * 2**20),
        cost_estimate=pl.CostEstimate(flops=17 * 10**9, bytes_accessed=15 * 2**20, transcendentals=0),
    )(place, *tables)
    return result[None]


def solution(mesh):
    in_specs = (P(AXES, None, None, None), P(AXES, None), P(AXES, None))
    out_specs = P(AXES, None, None, None)
    return jax.shard_map(shards, mesh=mesh, in_specs=in_specs, out_specs=out_specs, check_vma=False)
```

```python
import functools

import jax
import jax.numpy as jnp
from jax import lax
from jax.experimental import pallas as pl
from jax.experimental.pallas import tpu as pltpu
from jax.sharding import PartitionSpec as P

NOTE = 16
QUAD = 4
AXES = ("row", "col")


def cube(own, count, here, cut):
    x, z1, z2, z3, core, y = 1, 2, 4, 6, 8, 16
    full = own.shape[0]
    found = []

    def swap(value, mask):
        return lax.ppermute(value, AXES, [(i, i ^ mask) for i in range(count)])

    def whole(*masks):
        return [(mask, 0, full) for mask in masks]

    def cross(*items):
        arrays = [array for array, _ in items]
        batch = swap(jnp.concatenate(arrays, axis=0) if len(arrays) > 1 else arrays[0], core)
        found.extend(items)
        found.append((batch, [(mask | core, start, size) for _, parts in items for mask, start, size in parts]))
        return len(found) - 1

    def finish(spot, *arrays):
        batch, *arrays = lax.optimization_barrier((found[spot][0],) + arrays)
        found[spot] = (batch, found[spot][1])
        return arrays

    x0, y0, d0, f1, f3 = (swap(own, mask) for mask in (x, y, x | y, z1, z3))
    own, x0, y0, d0, f1, f3 = lax.optimization_barrier((own, x0, y0, d0, f1, f3))
    pair = jnp.concatenate([f1, f3], axis=0)
    xp, yp, f2, d2 = swap(pair, x), swap(pair, y), swap(f3, z1), swap(d0, z2)
    spot = cross(
        (own, whole(0)), (x0, whole(x)), (y0, whole(y)), (d0, whole(x | y)), (f1, whole(z1)), (f3, whole(z3))
    )
    xp, yp, f2, d2, d0 = finish(spot, xp, yp, f2, d2, d0)
    xl = swap(jnp.concatenate([f2, yp[full : full + cut]], axis=0), x)
    yl = swap(jnp.concatenate([f2, xp[full + cut :]], axis=0), y)
    d1 = swap(d0, z1)
    spots = [cross((xp, whole(z1 | x, z3 | x))), cross((yp, whole(z1 | y, z3 | y)))]
    xl, yl, d1, f2, d2 = finish(spots[0], *finish(spots[1], xl, yl, d1, f2, d2))
    cross((xl, [(z2 | x, 0, full), (z3 | x | y, 0, cut)]))
    cross((yl, [(z2 | y, 0, full), (z3 | x | y, cut, full - cut)]))
    for item in ((f2, whole(z2)), (d2, whole(z2 | x | y)), (d1, whole(z1 | x | y))):
        cross(item)
    return found


def window(payload, need, cut):
    groups, width = lax.axis_size("row"), lax.axis_size("col")
    count = groups * width
    size = payload.shape[0]
    column = lax.axis_index("col")
    here = lax.axis_index("row") * width + column
    pieces, offsets = [], []
    if (groups, width) == (4, 8):
        for array, parts in cube(payload, count, here, cut):
            pieces.append((array, [(start, rows) for _, start, rows in parts]))
            for mask, _, _ in parts:
                offsets.append((((here ^ mask) - here + count // 2) % count - count // 2)[None])
    else:
        block = lax.all_gather(payload, "col", axis=0, tiled=True)
        pieces.append((block, [(0, size)] * width))
        offsets.append(jnp.arange(width, dtype=jnp.int32) - column)
        for hop in range(1, -(-need // width) + 1):
            part = min(width, need - (hop - 1) * width)
            up = [(g, (g + hop) % groups) for g in range(groups)]
            down = [(g, (g - hop) % groups) for g in range(groups)]
            steps = jnp.arange(part, dtype=jnp.int32) - column
            pieces.append((lax.ppermute(block[(width - part) * size :], "row", up), [(0, size)] * part))
            offsets.append(steps - (hop - 1) * width - part)
            pieces.append((lax.ppermute(block[: part * size], "row", down), [(0, size)] * part))
            offsets.append(steps + hop * width)
    offsets = jnp.concatenate(offsets).astype(jnp.int32)
    return pieces, jnp.where(jnp.abs(offsets) <= need, offsets + need, -1)


def purify(reach, edge, layout, place, *refs):
    count = len(layout)
    tables, (out, band, square, own, notes, keep, arrived, noted) = refs[:count], refs[count:]
    far = 2 * reach
    slots, wide = 2 * reach + 1, 4 * reach + 1
    pitch = slots
    kind = band.dtype

    def span(first, n):
        first = first * edge
        return pl.ds(first if isinstance(first, int) else pl.multiple_of(first, edge), n * edge)

    base = 0
    for table, parts in zip(tables, layout):
        begin = 0
        for start, size in parts:
            k = place[base]
            body = min(size, slots * edge - start)

            @pl.when(k >= 0)
            def _(table=table, begin=begin, start=start, size=size, body=body, k=k):
                pltpu.make_async_copy(
                    table.at[pl.ds(begin, body)],
                    band.at[pl.ds(pl.multiple_of(k * pitch * edge + start, edge), body)],
                    arrived.at[k],
                ).start()
                if size > body:

                    @pl.when((k >= reach) & (k <= 3 * reach))
                    def _():
                        pltpu.make_async_copy(
                            table.at[pl.ds(begin + body, NOTE)], notes.at[k - reach], noted
                        ).start()

            begin += size
            base += 1

    def ready(k):
        body = pl.ds(0, slots * edge)
        pltpu.make_async_copy(tables[0].at[body], band.at[body], arrived.at[k]).wait()

    zero = jnp.zeros((edge, edge), kind)

    def clear(s, carry):
        band[span((2 * far + 1) * pitch + s, 1), :] = zero
        return carry

    lax.fori_loop(0, slots, clear, 0)

    for r in range(slots):
        pltpu.make_async_copy(tables[0].at[pl.ds(0, NOTE)], notes.at[r], noted).wait()
    notes[slots] = jnp.zeros(notes.shape[1:], kind)
    spots = keep.shape[1]
    diagonal = lax.broadcasted_iota(jnp.int32, (spots, edge), 0) == lax.broadcasted_iota(jnp.int32, (spots, edge), 1)

    def spread(r, carry):
        line = notes[r].astype(jnp.float32)[:1]
        value = jnp.sum(jnp.where(diagonal, line, 0.0), axis=1, keepdims=True)
        keep[r] = jnp.broadcast_to(value, (spots, edge))
        return carry

    lax.fori_loop(0, slots + 1, spread, 0)

    for k in range(far):
        ready(k)

    def strip(k, first, n):
        return jnp.concatenate(
            [band[span(k * pitch + s, 1), :] if 0 <= s < slots else zero for s in range(first, first + n)], axis=1
        )

    def square_strip(r, first, n):
        return jnp.concatenate(
            [
                square[r * edge : (r + 1) * edge, u * edge : (u + 1) * edge] if 0 <= u < wide else zero
                for u in range(first, first + n)
            ],
            axis=1,
        )

    def row_quad(quad, carry):
        r = QUAD * quad
        for i in range(QUAD):
            k = r + far + i

            @pl.when(k <= 2 * far)
            def _(k=k):
                ready(k)

        middle = jnp.where(quad == reach // QUAD, 1, 0)
        for d in range(-far, far + QUAD, 2):
            low, high = max(-reach, d - reach), min(reach + QUAD - 1, d + reach + 1)
            size = high - low + 1
            left = jnp.concatenate([strip(r + reach + i, low + reach - i, size) for i in range(QUAD)], axis=0)
            right = jnp.concatenate([strip(r + reach + e, d - e + reach, 2) for e in range(low, high + 1)], axis=0)
            product = jnp.dot(left, right, preferred_element_type=jnp.float32)
            for i in range(QUAD):
                for j in range(2):
                    u = d + far - i + j
                    if 0 <= u < wide:
                        kept = product[i * edge : (i + 1) * edge, j * edge : (j + 1) * edge]
                        kept = kept * keep[r + i, u : u + 1, :]
                        square[span(r + i, 1), u * edge : (u + 1) * edge] = kept.astype(kind)
                        if i == reach % QUAD:
                            own[middle, :, u * edge : (u + 1) * edge] = kept
        return carry

    lax.fori_loop(0, (slots + 1) // QUAD, row_quad, 0)

    for c in range(-far, far + 1, QUAD):
        low, high = max(-reach, c - far), min(reach, c + far + QUAD - 1)
        left = strip(far, low + reach, high - low + 1)
        right = jnp.concatenate(
            [square_strip(r + reach, c - r + far, QUAD) for r in range(low, high + 1)], axis=0
        )
        cube = jnp.dot(left, right, preferred_element_type=jnp.float32)
        for j in range(QUAD):
            u = c + far + j
            if u < wide:
                value = 3.0 * own[1, :, u * edge : (u + 1) * edge] - 2.0 * cube[:, j * edge : (j + 1) * edge]
                out[u] = (keep[reach, u : u + 1, :] * value).astype(out.dtype)


def pack(pattern, filter_mask, density, payload):
    slots, edge = density.shape[0], density.shape[1]
    for s in range(slots):
        scale = pattern[0, s].astype(jnp.float32)
        payload[s * edge : (s + 1) * edge] = (density[s].astype(jnp.float32) * scale).astype(payload.dtype)
    lane = lax.broadcasted_iota(jnp.int32, (NOTE, edge), 1)
    note = jnp.zeros((NOTE, edge), jnp.float32)
    for u in range(filter_mask.shape[1]):
        note = jnp.where(lane == u, filter_mask[0, u].astype(jnp.float32), note)
    payload[slots * edge :] = note.astype(payload.dtype)


def shards(density, pattern, filter_mask):
    slots, edge = density.shape[1], density.shape[2]
    wide = filter_mask.shape[1]
    reach = (slots - 1) // 2
    far = 2 * reach
    smem, vmem = pl.BlockSpec(memory_space=pltpu.SMEM), pl.BlockSpec(memory_space=pltpu.VMEM)
    payload = pl.pallas_call(
        pack,
        out_shape=jax.ShapeDtypeStruct((slots * edge + NOTE, edge), density.dtype),
        in_specs=[smem, smem, vmem],
        out_specs=vmem,
    )(pattern, filter_mask, density[0])
    pieces, place = window(payload, far, (slots + 1) // 2 * edge)
    tables = [array for array, _ in pieces]
    layout = [parts for _, parts in pieces]
    result = pl.pallas_call(
        functools.partial(purify, reach, edge, layout),
        out_shape=jax.ShapeDtypeStruct((wide, edge, edge), density.dtype),
        in_specs=[smem] + [pl.BlockSpec(memory_space=pl.ANY)] * len(tables),
        out_specs=vmem,
        scratch_shapes=[
            pltpu.VMEM(((2 * far + 2) * slots * edge, edge), density.dtype),
            pltpu.VMEM(((slots + 1) * edge, wide * edge), density.dtype),
            pltpu.VMEM((2, edge, wide * edge), jnp.float32),
            pltpu.VMEM((slots + 1, NOTE, edge), density.dtype),
            pltpu.VMEM((slots + 1, -(-wide // 8) * 8, edge), jnp.float32),
            pltpu.SemaphoreType.DMA((2 * far + 1,)),
            pltpu.SemaphoreType.DMA,
        ],
        compiler_params=pltpu.CompilerParams(vmem_limit_bytes=40 * 2**20),
        cost_estimate=pl.CostEstimate(flops=17 * 10**9, bytes_accessed=15 * 2**20, transcendentals=0),
    )(place, *tables)
    return result[None]


def solution(mesh):
    in_specs = (P(AXES, None, None, None), P(AXES, None), P(AXES, None))
    out_specs = P(AXES, None, None, None)
    return jax.shard_map(shards, mesh=mesh, in_specs=in_specs, out_specs=out_specs, check_vma=False)
```

```python
import functools

import jax
import jax.numpy as jnp
import numpy as np
from jax import lax
from jax.experimental import pallas as pl
from jax.experimental.pallas import tpu as pltpu
from jax.sharding import PartitionSpec as P

NOTE = 16
GROUP = 2
WIDTH = 4
AXES = ("row", "col")


def cube(own, count, cut):
    x, z1, z2, z3, core, y = 1, 2, 4, 6, 8, 16
    full = own.shape[0]
    found = []

    def swap(value, mask):
        return lax.ppermute(value, AXES, [(i, i ^ mask) for i in range(count)])

    def whole(*masks):
        return [(mask, 0, full) for mask in masks]

    def cross(*items):
        arrays = [array for array, _ in items]
        batch = swap(jnp.concatenate(arrays, axis=0) if len(arrays) > 1 else arrays[0], core)
        found.extend(items)
        found.append((batch, [(mask | core, start, size) for _, parts in items for mask, start, size in parts]))
        return len(found) - 1

    def finish(spot, *arrays):
        batch, *arrays = lax.optimization_barrier((found[spot][0],) + arrays)
        found[spot] = (batch, found[spot][1])
        return arrays

    x0, y0, d0, f1, f3 = (swap(own, mask) for mask in (x, y, x | y, z1, z3))
    pair = jnp.concatenate([f1, f3], axis=0)
    xp, yp, f2, d2 = swap(pair, x), swap(pair, y), swap(f3, z1), swap(d0, z2)
    spot = cross(
        (own, whole(0)), (x0, whole(x)), (y0, whole(y)), (d0, whole(x | y)), (f1, whole(z1)), (f3, whole(z3))
    )
    xp, yp, f2, d0 = finish(spot, xp, yp, f2, d0)
    xl = swap(jnp.concatenate([f2, yp[full : full + cut]], axis=0), x)
    yl = swap(jnp.concatenate([f2, xp[full + cut :]], axis=0), y)
    d1 = swap(d0, z1)
    spots = [cross((xp, whole(z1 | x, z3 | x))), cross((yp, whole(z1 | y, z3 | y)))]
    xl, yl, d1, f2, d2 = finish(spots[0], *finish(spots[1], xl, yl, d1, f2, d2))
    cross((xl, [(z2 | x, 0, full), (z3 | x | y, 0, cut)]))
    cross((yl, [(z2 | y, 0, full), (z3 | x | y, cut, full - cut)]))
    for item in ((f2, whole(z2)), (d2, whole(z2 | x | y)), (d1, whole(z1 | x | y))):
        cross(item)
    return found


def window(payload, need, cut):
    groups, width = lax.axis_size("row"), lax.axis_size("col")
    count = groups * width
    size = payload.shape[0]
    column = lax.axis_index("col")
    here = lax.axis_index("row") * width + column
    if (groups, width) == (4, 8):
        found = cube(payload, count, cut)
        pieces = [(array, [(start, rows) for _, start, rows in parts]) for array, parts in found]
        masks = np.array([mask for _, parts in found for mask, _, _ in parts])
        device = np.arange(count)[:, None]
        offsets = jnp.asarray((((device ^ masks) - device + count // 2) % count - count // 2).astype(np.int32))[here]
    else:
        pieces, offsets = [], []
        block = lax.all_gather(payload, "col", axis=0, tiled=True)
        pieces.append((block, [(0, size)] * width))
        offsets.append(jnp.arange(width, dtype=jnp.int32) - column)
        for hop in range(1, -(-need // width) + 1):
            part = min(width, need - (hop - 1) * width)
            up = [(g, (g + hop) % groups) for g in range(groups)]
            down = [(g, (g - hop) % groups) for g in range(groups)]
            steps = jnp.arange(part, dtype=jnp.int32) - column
            pieces.append((lax.ppermute(block[(width - part) * size :], "row", up), [(0, size)] * part))
            offsets.append(steps - (hop - 1) * width - part)
            pieces.append((lax.ppermute(block[: part * size], "row", down), [(0, size)] * part))
            offsets.append(steps + hop * width)
        offsets = jnp.concatenate(offsets).astype(jnp.int32)
    return pieces, jnp.where(jnp.abs(offsets) <= need, offsets + need, -1)


def purify(reach, edge, layout, place, *refs):
    count = len(layout)
    tables, (out, band, square, own, notes, keep, arrived, noted) = refs[:count], refs[count:]
    far = 2 * reach
    slots, wide = 2 * reach + 1, 4 * reach + 1
    pitch = slots
    kind = band.dtype

    def span(first, n):
        first = first * edge
        return pl.ds(first if isinstance(first, int) else pl.multiple_of(first, edge), n * edge)

    base = 0
    for table, parts in zip(tables, layout):
        begin = 0
        for start, size in parts:
            k = place[base]
            body = min(size, slots * edge - start)

            @pl.when(k >= 0)
            def _(table=table, begin=begin, start=start, size=size, body=body, k=k):
                pltpu.make_async_copy(
                    table.at[pl.ds(begin, body)],
                    band.at[pl.ds(pl.multiple_of(k * pitch * edge + start, edge), body)],
                    arrived.at[k],
                ).start()
                if size > body:

                    @pl.when((k >= reach) & (k <= 3 * reach))
                    def _():
                        pltpu.make_async_copy(
                            table.at[pl.ds(begin + body, NOTE)], notes.at[k - reach], noted
                        ).start()

            begin += size
            base += 1

    def ready(k):
        body = pl.ds(0, slots * edge)
        pltpu.make_async_copy(tables[0].at[body], band.at[body], arrived.at[k]).wait()

    zero = jnp.zeros((edge, edge), kind)

    def clear(s, carry):
        band[span((2 * far + 1) * pitch + s, 1), :] = zero
        return carry

    lax.fori_loop(0, slots, clear, 0)

    for r in range(slots):
        pltpu.make_async_copy(tables[0].at[pl.ds(0, NOTE)], notes.at[r], noted).wait()
    notes[slots] = jnp.zeros(notes.shape[1:], kind)
    spots = keep.shape[1]
    diagonal = lax.broadcasted_iota(jnp.int32, (spots, edge), 0) == lax.broadcasted_iota(jnp.int32, (spots, edge), 1)

    def spread(r, carry):
        line = notes[r].astype(jnp.float32)[:1]
        value = jnp.sum(jnp.where(diagonal, line, 0.0), axis=1, keepdims=True)
        keep[r] = jnp.broadcast_to(value, (spots, edge))
        return carry

    lax.fori_loop(0, slots + 1, spread, 0)

    for k in range(far):
        ready(k)

    def strip(k, first, n):
        return jnp.concatenate(
            [band[span(k * pitch + s, 1), :] if 0 <= s < slots else zero for s in range(first, first + n)], axis=1
        )

    def square_strip(r, first, n):
        return jnp.concatenate(
            [
                square[r * edge : (r + 1) * edge, u * edge : (u + 1) * edge] if 0 <= u < wide else zero
                for u in range(first, first + n)
            ],
            axis=1,
        )

    def row_group(group, carry):
        r = GROUP * group
        for i in range(GROUP):
            k = r + far + i

            @pl.when(k <= 2 * far)
            def _(k=k):
                ready(k)

        middle = jnp.where(group == reach // GROUP, 1, 0)
        for d in range(-far, far + GROUP, 2):
            low, high = max(-reach, d - reach), min(reach + GROUP - 1, d + reach + 1)
            size = high - low + 1
            left = jnp.concatenate([strip(r + reach + i, low + reach - i, size) for i in range(GROUP)], axis=0)
            right = jnp.concatenate([strip(r + reach + e, d - e + reach, 2) for e in range(low, high + 1)], axis=0)
            product = jnp.dot(left, right, preferred_element_type=jnp.float32)
            for i in range(GROUP):
                for j in range(2):
                    u = d + far - i + j
                    if 0 <= u < wide:
                        kept = product[i * edge : (i + 1) * edge, j * edge : (j + 1) * edge]
                        kept = kept * keep[r + i, u : u + 1, :]
                        square[span(r + i, 1), u * edge : (u + 1) * edge] = kept.astype(kind)
                        if i == reach % GROUP:
                            own[middle, :, u * edge : (u + 1) * edge] = kept
        return carry

    lax.fori_loop(0, (slots + 1) // GROUP, row_group, 0)

    for c in range(-far, far + 1, WIDTH):
        low, high = max(-reach, c - far), min(reach, c + far + WIDTH - 1)
        left = strip(far, low + reach, high - low + 1)
        right = jnp.concatenate(
            [square_strip(r + reach, c - r + far, WIDTH) for r in range(low, high + 1)], axis=0
        )
        cube = jnp.dot(left, right, preferred_element_type=jnp.float32)
        for j in range(WIDTH):
            u = c + far + j
            if u < wide:
                value = 3.0 * own[1, :, u * edge : (u + 1) * edge] - 2.0 * cube[:, j * edge : (j + 1) * edge]
                out[u] = (keep[reach, u : u + 1, :] * value).astype(out.dtype)


def pack(pattern, filter_mask, density, payload):
    slots, edge = density.shape[0], density.shape[1]
    for s in range(slots):
        scale = pattern[0, s].astype(jnp.float32)
        payload[s * edge : (s + 1) * edge] = (density[s].astype(jnp.float32) * scale).astype(payload.dtype)
    lane = lax.broadcasted_iota(jnp.int32, (NOTE, edge), 1)
    note = jnp.zeros((NOTE, edge), jnp.float32)
    for u in range(filter_mask.shape[1]):
        note = jnp.where(lane == u, filter_mask[0, u].astype(jnp.float32), note)
    payload[slots * edge :] = note.astype(payload.dtype)


def shards(density, pattern, filter_mask):
    slots, edge = density.shape[1], density.shape[2]
    wide = filter_mask.shape[1]
    reach = (slots - 1) // 2
    far = 2 * reach
    smem, vmem = pl.BlockSpec(memory_space=pltpu.SMEM), pl.BlockSpec(memory_space=pltpu.VMEM)
    payload = pl.pallas_call(
        pack,
        out_shape=jax.ShapeDtypeStruct((slots * edge + NOTE, edge), density.dtype),
        in_specs=[smem, smem, vmem],
        out_specs=vmem,
    )(pattern, filter_mask, density[0])
    pieces, place = window(payload, far, (slots + 1) // 2 * edge)
    tables = [array for array, _ in pieces]
    layout = [parts for _, parts in pieces]
    result = pl.pallas_call(
        functools.partial(purify, reach, edge, layout),
        out_shape=jax.ShapeDtypeStruct((wide, edge, edge), density.dtype),
        in_specs=[smem] + [pl.BlockSpec(memory_space=pl.ANY)] * len(tables),
        out_specs=vmem,
        scratch_shapes=[
            pltpu.VMEM(((2 * far + 2) * slots * edge, edge), density.dtype),
            pltpu.VMEM(((slots + 1) * edge, wide * edge), density.dtype),
            pltpu.VMEM((2, edge, wide * edge), jnp.float32),
            pltpu.VMEM((slots + 1, NOTE, edge), density.dtype),
            pltpu.VMEM((slots + 1, -(-wide // 8) * 8, edge), jnp.float32),
            pltpu.SemaphoreType.DMA((2 * far + 1,)),
            pltpu.SemaphoreType.DMA,
        ],
        compiler_params=pltpu.CompilerParams(vmem_limit_bytes=56 * 2**20),
        cost_estimate=pl.CostEstimate(flops=17 * 10**9, bytes_accessed=15 * 2**20, transcendentals=0),
    )(place, *tables)
    return result[None]


def solution(mesh):
    in_specs = (P(AXES, None, None, None), P(AXES, None), P(AXES, None))
    out_specs = P(AXES, None, None, None)
    return jax.shard_map(shards, mesh=mesh, in_specs=in_specs, out_specs=out_specs, check_vma=False)
```

```python
import functools

import jax
import jax.numpy as jnp
import numpy as np
from jax import lax
from jax.experimental import pallas as pl
from jax.experimental.pallas import tpu as pltpu
from jax.sharding import PartitionSpec as P

NOTE = 16
GROUP = 2
WIDTH = 4
AXES = ("row", "col")


def cube(own, count, cut):
    x, z1, z2, z3, core, y = 1, 2, 4, 6, 8, 16
    full = own.shape[0]
    found = []

    def swap(value, mask):
        return lax.ppermute(value, AXES, [(i, i ^ mask) for i in range(count)])

    def whole(*masks):
        return [(mask, 0, full) for mask in masks]

    def cross(*items):
        arrays = [array for array, _ in items]
        batch = swap(jnp.concatenate(arrays, axis=0) if len(arrays) > 1 else arrays[0], core)
        found.extend(items)
        found.append((batch, [(mask | core, start, size) for _, parts in items for mask, start, size in parts]))
        return len(found) - 1

    def finish(spot, *arrays):
        batch, *arrays = lax.optimization_barrier((found[spot][0],) + arrays)
        found[spot] = (batch, found[spot][1])
        return arrays

    x0, y0, d0, f1, f3 = (swap(own, mask) for mask in (x, y, x | y, z1, z3))
    pair = jnp.concatenate([f1, f3], axis=0)
    xp, yp, f2, d2 = swap(pair, x), swap(pair, y), swap(f3, z1), swap(d0, z2)
    spot = cross(
        (own, whole(0)), (x0, whole(x)), (y0, whole(y)), (d0, whole(x | y)), (f1, whole(z1)), (f3, whole(z3))
    )
    xp, yp, f2, d0 = finish(spot, xp, yp, f2, d0)
    xl = swap(jnp.concatenate([f2, yp[full : full + cut]], axis=0), x)
    yl = swap(jnp.concatenate([f2, xp[full + cut :]], axis=0), y)
    d1 = swap(d0, z1)
    spots = [cross((xp, whole(z1 | x, z3 | x))), cross((yp, whole(z1 | y, z3 | y)))]
    xl, yl, d1, f2, d2 = finish(spots[0], *finish(spots[1], xl, yl, d1, f2, d2))
    cross((xl, [(z2 | x, 0, full), (z3 | x | y, 0, cut)]))
    cross((yl, [(z2 | y, 0, full), (z3 | x | y, cut, full - cut)]))
    for item in ((f2, whole(z2)), (d2, whole(z2 | x | y)), (d1, whole(z1 | x | y))):
        cross(item)
    return found


def window(payload, need, cut):
    groups, width = lax.axis_size("row"), lax.axis_size("col")
    count = groups * width
    size = payload.shape[0]
    column = lax.axis_index("col")
    here = lax.axis_index("row") * width + column
    if (groups, width) == (4, 8):
        found = cube(payload, count, cut)
        pieces = [(array, [(start, rows) for _, start, rows in parts]) for array, parts in found]
        masks = np.array([mask for _, parts in found for mask, _, _ in parts])
        device = np.arange(count)[:, None]
        offsets = jnp.asarray((((device ^ masks) - device + count // 2) % count - count // 2).astype(np.int32))[here]
    else:
        pieces, offsets = [], []
        block = lax.all_gather(payload, "col", axis=0, tiled=True)
        pieces.append((block, [(0, size)] * width))
        offsets.append(jnp.arange(width, dtype=jnp.int32) - column)
        for hop in range(1, -(-need // width) + 1):
            part = min(width, need - (hop - 1) * width)
            up = [(g, (g + hop) % groups) for g in range(groups)]
            down = [(g, (g - hop) % groups) for g in range(groups)]
            steps = jnp.arange(part, dtype=jnp.int32) - column
            pieces.append((lax.ppermute(block[(width - part) * size :], "row", up), [(0, size)] * part))
            offsets.append(steps - (hop - 1) * width - part)
            pieces.append((lax.ppermute(block[: part * size], "row", down), [(0, size)] * part))
            offsets.append(steps + hop * width)
        offsets = jnp.concatenate(offsets).astype(jnp.int32)
    return pieces, jnp.where(jnp.abs(offsets) <= need, offsets + need, -1)


def purify(reach, edge, layout, place, *refs):
    count = len(layout)
    tables, (out, band, square, own, result, arrived, left_out) = refs[:count], refs[count:]
    far = 2 * reach
    slots, wide = 2 * reach + 1, 4 * reach + 1
    pitch = slots * edge + NOTE
    kind = band.dtype

    base = 0
    for table, parts in zip(tables, layout):
        begin = 0
        for start, size in parts:
            k = place[base]

            @pl.when(k >= 0)
            def _(table=table, begin=begin, start=start, size=size, k=k):
                pltpu.make_async_copy(
                    table.at[pl.ds(begin, size)],
                    band.at[pl.ds(pl.multiple_of(k * pitch + start, NOTE), size)],
                    arrived.at[k],
                ).start()

            begin += size
            base += 1

    def ready(k):
        row = pl.ds(0, pitch)
        pltpu.make_async_copy(tables[0].at[row], band.at[row], arrived.at[k]).wait()

    zero = jnp.zeros((edge, edge), kind)

    def block(k, s):
        return band[pl.ds(pl.multiple_of(k * pitch + s * edge, NOTE), edge), :]

    def clear(s, carry):
        band[pl.ds(pl.multiple_of((2 * far + 1) * pitch + s * edge, NOTE), edge), :] = zero
        return carry

    lax.fori_loop(0, slots, clear, 0)
    band[(2 * far + 1) * pitch + slots * edge :, :] = jnp.zeros((NOTE, edge), kind)

    spots = -(-wide // 8) * 8
    diagonal = lax.broadcasted_iota(jnp.int32, (spots, edge), 0) == lax.broadcasted_iota(jnp.int32, (spots, edge), 1)

    def masks(k):
        line = band[pl.ds(pl.multiple_of(k * pitch + slots * edge, NOTE), NOTE), :].astype(jnp.float32)[:1]
        value = jnp.sum(jnp.where(diagonal, line, 0.0), axis=1, keepdims=True)
        return jnp.broadcast_to(value, (spots, edge))

    def strip(k, first, n):
        return jnp.concatenate(
            [block(k, s) if 0 <= s < slots else zero for s in range(first, first + n)], axis=1
        )

    def square_strip(r, first, n):
        return jnp.concatenate(
            [
                square[r * edge : (r + 1) * edge, u * edge : (u + 1) * edge] if 0 <= u < wide else zero
                for u in range(first, first + n)
            ],
            axis=1,
        )

    for k in range(far):
        ready(k)

    def row_group(group, carry):
        r = GROUP * group
        for i in range(GROUP):
            k = r + far + i

            @pl.when(k <= 2 * far)
            def _(k=k):
                ready(k)

        middle = jnp.where(group == reach // GROUP, 1, 0)
        keep = [masks(r + reach + i) for i in range(GROUP)]
        for d in range(-far, far + GROUP, 2):
            low, high = max(-reach, d - reach), min(reach + GROUP - 1, d + reach + 1)
            size = high - low + 1
            left = jnp.concatenate([strip(r + reach + i, low + reach - i, size) for i in range(GROUP)], axis=0)
            right = jnp.concatenate([strip(r + reach + e, d - e + reach, 2) for e in range(low, high + 1)], axis=0)
            product = jnp.dot(left, right, preferred_element_type=jnp.float32)
            for i in range(GROUP):
                for j in range(2):
                    u = d + far - i + j
                    if 0 <= u < wide:
                        kept = product[i * edge : (i + 1) * edge, j * edge : (j + 1) * edge]
                        kept = kept * keep[i][u : u + 1, :]
                        rows = pl.ds(pl.multiple_of((r + i) * edge, edge), edge)
                        square[rows, u * edge : (u + 1) * edge] = kept.astype(kind)
                        if i == reach % GROUP:
                            own[middle, :, u * edge : (u + 1) * edge] = kept
        return carry

    lax.fori_loop(0, (slots + 1) // GROUP, row_group, 0)

    keep = masks(far)
    copies = []
    for c in range(-far, far + 1, WIDTH):
        low, high = max(-reach, c - far), min(reach, c + far + WIDTH - 1)
        left = strip(far, low + reach, high - low + 1)
        right = jnp.concatenate(
            [square_strip(r + reach, c - r + far, WIDTH) for r in range(low, high + 1)], axis=0
        )
        cube = jnp.dot(left, right, preferred_element_type=jnp.float32)
        first, last = c + far, min(c + far + WIDTH, wide)
        for u in range(first, last):
            j = u - first
            value = 3.0 * own[1, :, u * edge : (u + 1) * edge] - 2.0 * cube[:, j * edge : (j + 1) * edge]
            result[u] = (keep[u : u + 1, :] * value).astype(out.dtype)
        copies.append(
            pltpu.make_async_copy(
                result.at[pl.ds(first, last - first)], out.at[pl.ds(first, last - first)], left_out.at[len(copies)]
            )
        )
        copies[-1].start()
    for copy in copies:
        copy.wait()


def pack(pattern, filter_mask, density, payload):
    slots, edge = density.shape[0], density.shape[1]
    for s in range(slots):
        scale = pattern[0, s].astype(jnp.float32)
        payload[s * edge : (s + 1) * edge] = (density[s].astype(jnp.float32) * scale).astype(payload.dtype)
    lane = lax.broadcasted_iota(jnp.int32, (NOTE, edge), 1)
    note = jnp.zeros((NOTE, edge), jnp.float32)
    for u in range(filter_mask.shape[1]):
        note = jnp.where(lane == u, filter_mask[0, u].astype(jnp.float32), note)
    payload[slots * edge :] = note.astype(payload.dtype)


def shards(density, pattern, filter_mask):
    slots, edge = density.shape[1], density.shape[2]
    wide = filter_mask.shape[1]
    reach = (slots - 1) // 2
    far = 2 * reach
    smem, vmem = pl.BlockSpec(memory_space=pltpu.SMEM), pl.BlockSpec(memory_space=pltpu.VMEM)
    payload = pl.pallas_call(
        pack,
        out_shape=jax.ShapeDtypeStruct((slots * edge + NOTE, edge), density.dtype),
        in_specs=[smem, smem, vmem],
        out_specs=vmem,
    )(pattern, filter_mask, density[0])
    pieces, place = window(payload, far, (slots + 1) // 2 * edge)
    tables = [array for array, _ in pieces]
    layout = [parts for _, parts in pieces]
    result = pl.pallas_call(
        functools.partial(purify, reach, edge, layout),
        out_shape=jax.ShapeDtypeStruct((wide, edge, edge), density.dtype),
        in_specs=[smem] + [pl.BlockSpec(memory_space=pl.ANY)] * len(tables),
        out_specs=pl.BlockSpec(memory_space=pl.ANY),
        scratch_shapes=[
            pltpu.VMEM(((2 * far + 2) * (slots * edge + NOTE), edge), density.dtype),
            pltpu.VMEM(((slots + 1) * edge, wide * edge), density.dtype),
            pltpu.VMEM((2, edge, wide * edge), jnp.float32),
            pltpu.VMEM((wide, edge, edge), density.dtype),
            pltpu.SemaphoreType.DMA((2 * far + 1,)),
            pltpu.SemaphoreType.DMA((-(-wide // WIDTH),)),
        ],
        compiler_params=pltpu.CompilerParams(vmem_limit_bytes=56 * 2**20),
        cost_estimate=pl.CostEstimate(flops=17 * 10**9, bytes_accessed=15 * 2**20, transcendentals=0),
    )(place, *tables)
    return result[None]


def solution(mesh):
    in_specs = (P(AXES, None, None, None), P(AXES, None), P(AXES, None))
    out_specs = P(AXES, None, None, None)
    return jax.shard_map(shards, mesh=mesh, in_specs=in_specs, out_specs=out_specs, check_vma=False)
```

```python
import functools

import jax
import jax.numpy as jnp
import numpy as np
from jax import lax
from jax.experimental import pallas as pl
from jax.experimental.pallas import tpu as pltpu
from jax.sharding import PartitionSpec as P

NOTE = 16
GROUP = 1
WIDTH = 4
AXES = ("row", "col")


def cube(own, count, cut):
    x, z1, z2, z3, core, y = 1, 2, 4, 6, 8, 16
    full = own.shape[0]
    found = []

    def swap(value, mask):
        return lax.ppermute(value, AXES, [(i, i ^ mask) for i in range(count)])

    def whole(*masks):
        return [(mask, 0, full) for mask in masks]

    def cross(*items):
        arrays = [array for array, _ in items]
        batch = swap(jnp.concatenate(arrays, axis=0) if len(arrays) > 1 else arrays[0], core)
        found.extend(items)
        found.append((batch, [(mask | core, start, size) for _, parts in items for mask, start, size in parts]))
        return len(found) - 1

    def finish(spot, *arrays):
        batch, *arrays = lax.optimization_barrier((found[spot][0],) + arrays)
        found[spot] = (batch, found[spot][1])
        return arrays

    x0, y0, d0, f1, f3 = (swap(own, mask) for mask in (x, y, x | y, z1, z3))
    pair = jnp.concatenate([f1, f3], axis=0)
    xp, yp, f2, d2 = swap(pair, x), swap(pair, y), swap(f3, z1), swap(d0, z2)
    spot = cross(
        (own, whole(0)), (x0, whole(x)), (y0, whole(y)), (d0, whole(x | y)), (f1, whole(z1)), (f3, whole(z3))
    )
    xp, yp, f2, d0 = finish(spot, xp, yp, f2, d0)
    xl = swap(jnp.concatenate([f2, yp[full : full + cut]], axis=0), x)
    yl = swap(jnp.concatenate([f2, xp[full + cut :]], axis=0), y)
    d1 = swap(d0, z1)
    spots = [cross((xp, whole(z1 | x, z3 | x))), cross((yp, whole(z1 | y, z3 | y)))]
    xl, yl, d1, f2, d2 = finish(spots[0], *finish(spots[1], xl, yl, d1, f2, d2))
    cross((xl, [(z2 | x, 0, full), (z3 | x | y, 0, cut)]))
    cross((yl, [(z2 | y, 0, full), (z3 | x | y, cut, full - cut)]))
    for item in ((f2, whole(z2)), (d2, whole(z2 | x | y)), (d1, whole(z1 | x | y))):
        cross(item)
    return found


def window(payload, need, cut):
    groups, width = lax.axis_size("row"), lax.axis_size("col")
    count = groups * width
    size = payload.shape[0]
    column = lax.axis_index("col")
    here = lax.axis_index("row") * width + column
    if (groups, width) == (4, 8):
        found = cube(payload, count, cut)
        pieces = [(array, [(start, rows) for _, start, rows in parts]) for array, parts in found]
        masks = np.array([mask for _, parts in found for mask, _, _ in parts])
        device = np.arange(count)[:, None]
        offsets = jnp.asarray((((device ^ masks) - device + count // 2) % count - count // 2).astype(np.int32))[here]
    else:
        pieces, offsets = [], []
        block = lax.all_gather(payload, "col", axis=0, tiled=True)
        pieces.append((block, [(0, size)] * width))
        offsets.append(jnp.arange(width, dtype=jnp.int32) - column)
        for hop in range(1, -(-need // width) + 1):
            part = min(width, need - (hop - 1) * width)
            up = [(g, (g + hop) % groups) for g in range(groups)]
            down = [(g, (g - hop) % groups) for g in range(groups)]
            steps = jnp.arange(part, dtype=jnp.int32) - column
            pieces.append((lax.ppermute(block[(width - part) * size :], "row", up), [(0, size)] * part))
            offsets.append(steps - (hop - 1) * width - part)
            pieces.append((lax.ppermute(block[: part * size], "row", down), [(0, size)] * part))
            offsets.append(steps + hop * width)
        offsets = jnp.concatenate(offsets).astype(jnp.int32)
    return pieces, jnp.where(jnp.abs(offsets) <= need, offsets + need, -1)


def purify(reach, edge, layout, place, *refs):
    count = len(layout)
    tables, (out, band, square, own, result, arrived, left_out) = refs[:count], refs[count:]
    far = 2 * reach
    slots, wide = 2 * reach + 1, 4 * reach + 1
    pitch = slots * edge + NOTE
    kind = band.dtype

    base = 0
    for table, parts in zip(tables, layout):
        begin = 0
        for start, size in parts:
            k = place[base]

            @pl.when(k >= 0)
            def _(table=table, begin=begin, start=start, size=size, k=k):
                pltpu.make_async_copy(
                    table.at[pl.ds(begin, size)],
                    band.at[pl.ds(pl.multiple_of(k * pitch + start, NOTE), size)],
                    arrived.at[k],
                ).start()

            begin += size
            base += 1

    def ready(k):
        row = pl.ds(0, pitch)
        pltpu.make_async_copy(tables[0].at[row], band.at[row], arrived.at[k]).wait()

    zero = jnp.zeros((edge, edge), kind)

    def block(k, s):
        return band[pl.ds(pl.multiple_of(k * pitch + s * edge, NOTE), edge), :]

    def clear(s, carry):
        band[pl.ds(pl.multiple_of((2 * far + 1) * pitch + s * edge, NOTE), edge), :] = zero
        return carry

    lax.fori_loop(0, slots, clear, 0)
    band[(2 * far + 1) * pitch + slots * edge :, :] = jnp.zeros((NOTE, edge), kind)

    spots = -(-wide // 8) * 8
    diagonal = lax.broadcasted_iota(jnp.int32, (spots, edge), 0) == lax.broadcasted_iota(jnp.int32, (spots, edge), 1)

    def masks(k):
        line = band[pl.ds(pl.multiple_of(k * pitch + slots * edge, NOTE), NOTE), :].astype(jnp.float32)[:1]
        value = jnp.sum(jnp.where(diagonal, line, 0.0), axis=1, keepdims=True)
        return jnp.broadcast_to(value, (spots, edge))

    def strip(k, first, n):
        return jnp.concatenate(
            [block(k, s) if 0 <= s < slots else zero for s in range(first, first + n)], axis=1
        )

    def square_strip(r, first, n):
        return jnp.concatenate(
            [
                square[r * edge : (r + 1) * edge, u * edge : (u + 1) * edge] if 0 <= u < wide else zero
                for u in range(first, first + n)
            ],
            axis=1,
        )

    for k in range(far):
        ready(k)

    def row_group(group, carry):
        r = GROUP * group
        for i in range(GROUP):
            k = r + far + i

            @pl.when(k <= 2 * far)
            def _(k=k):
                ready(k)

        middle = jnp.where(group == reach // GROUP, 1, 0)
        keep = [masks(r + reach + i) for i in range(GROUP)]
        for d in range(-far, far + GROUP, 2):
            low, high = max(-reach, d - reach), min(reach + GROUP - 1, d + reach + 1)
            size = high - low + 1
            left = jnp.concatenate([strip(r + reach + i, low + reach - i, size) for i in range(GROUP)], axis=0)
            right = jnp.concatenate([strip(r + reach + e, d - e + reach, 2) for e in range(low, high + 1)], axis=0)
            product = jnp.dot(left, right, preferred_element_type=jnp.float32)
            for i in range(GROUP):
                for j in range(2):
                    u = d + far - i + j
                    if 0 <= u < wide:
                        kept = product[i * edge : (i + 1) * edge, j * edge : (j + 1) * edge]
                        kept = kept * keep[i][u : u + 1, :]
                        rows = pl.ds(pl.multiple_of((r + i) * edge, edge), edge)
                        square[rows, u * edge : (u + 1) * edge] = kept.astype(kind)
                        if i == reach % GROUP:
                            own[middle, :, u * edge : (u + 1) * edge] = kept
        return carry

    lax.fori_loop(0, -(-slots // GROUP), row_group, 0)

    keep = masks(far)
    copies = []
    for c in range(-far, far + 1, WIDTH):
        low, high = max(-reach, c - far), min(reach, c + far + WIDTH - 1)
        left = strip(far, low + reach, high - low + 1)
        right = jnp.concatenate(
            [square_strip(r + reach, c - r + far, WIDTH) for r in range(low, high + 1)], axis=0
        )
        cube = jnp.dot(left, right, preferred_element_type=jnp.float32)
        first, last = c + far, min(c + far + WIDTH, wide)
        for u in range(first, last):
            j = u - first
            value = 3.0 * own[1, :, u * edge : (u + 1) * edge] - 2.0 * cube[:, j * edge : (j + 1) * edge]
            result[u] = (keep[u : u + 1, :] * value).astype(out.dtype)
        copies.append(
            pltpu.make_async_copy(
                result.at[pl.ds(first, last - first)], out.at[pl.ds(first, last - first)], left_out.at[len(copies)]
            )
        )
        copies[-1].start()
    for copy in copies:
        copy.wait()


def pack(pattern, filter_mask, density, payload):
    slots, edge = density.shape[0], density.shape[1]
    for s in range(slots):
        scale = pattern[0, s].astype(jnp.float32)
        payload[s * edge : (s + 1) * edge] = (density[s].astype(jnp.float32) * scale).astype(payload.dtype)
    lane = lax.broadcasted_iota(jnp.int32, (NOTE, edge), 1)
    note = jnp.zeros((NOTE, edge), jnp.float32)
    for u in range(filter_mask.shape[1]):
        note = jnp.where(lane == u, filter_mask[0, u].astype(jnp.float32), note)
    payload[slots * edge :] = note.astype(payload.dtype)


def shards(density, pattern, filter_mask):
    slots, edge = density.shape[1], density.shape[2]
    wide = filter_mask.shape[1]
    reach = (slots - 1) // 2
    far = 2 * reach
    smem, vmem = pl.BlockSpec(memory_space=pltpu.SMEM), pl.BlockSpec(memory_space=pltpu.VMEM)
    payload = pl.pallas_call(
        pack,
        out_shape=jax.ShapeDtypeStruct((slots * edge + NOTE, edge), density.dtype),
        in_specs=[smem, smem, vmem],
        out_specs=vmem,
    )(pattern, filter_mask, density[0])
    pieces, place = window(payload, far, (slots + 1) // 2 * edge)
    tables = [array for array, _ in pieces]
    layout = [parts for _, parts in pieces]
    result = pl.pallas_call(
        functools.partial(purify, reach, edge, layout),
        out_shape=jax.ShapeDtypeStruct((wide, edge, edge), density.dtype),
        in_specs=[smem] + [pl.BlockSpec(memory_space=pl.ANY)] * len(tables),
        out_specs=pl.BlockSpec(memory_space=pl.ANY),
        scratch_shapes=[
            pltpu.VMEM(((2 * far + 2) * (slots * edge + NOTE), edge), density.dtype),
            pltpu.VMEM(((slots + 1) * edge, wide * edge), density.dtype),
            pltpu.VMEM((2, edge, wide * edge), jnp.float32),
            pltpu.VMEM((wide, edge, edge), density.dtype),
            pltpu.SemaphoreType.DMA((2 * far + 1,)),
            pltpu.SemaphoreType.DMA((-(-wide // WIDTH),)),
        ],
        compiler_params=pltpu.CompilerParams(vmem_limit_bytes=36 * 2**20),
        cost_estimate=pl.CostEstimate(flops=17 * 10**9, bytes_accessed=15 * 2**20, transcendentals=0),
    )(place, *tables)
    return result[None]


def solution(mesh):
    in_specs = (P(AXES, None, None, None), P(AXES, None), P(AXES, None))
    out_specs = P(AXES, None, None, None)
    return jax.shard_map(shards, mesh=mesh, in_specs=in_specs, out_specs=out_specs, check_vma=False)
```

```python
import functools

import jax
import jax.numpy as jnp
import numpy as np
from jax import lax
from jax.experimental import pallas as pl
from jax.experimental.pallas import tpu as pltpu
from jax.sharding import PartitionSpec as P

NOTE = 16
GROUP = 2
WIDTH = 4
AXES = ("row", "col")


def cube(own, count, cut, gather):
    x, z1, z2, z3, core, y = 1, 2, 4, 6, 8, 16
    full = own.shape[0]
    found = []

    def swap(value, mask):
        return lax.ppermute(value, AXES, [(i, i ^ mask) for i in range(count)])

    def whole(*masks):
        return [(mask, 0, full) for mask in masks]

    def cross(*items):
        arrays = [array for array, _ in items]
        batch = swap(jnp.concatenate(arrays, axis=0) if len(arrays) > 1 else arrays[0], core)
        found.extend(items)
        found.append((batch, [(mask | core, start, size) for _, parts in items for mask, start, size in parts]))
        return len(found) - 1

    def finish(spot, *arrays):
        batch, *arrays = lax.optimization_barrier((found[spot][0],) + arrays)
        found[spot] = (batch, found[spot][1])
        return arrays

    x0, y0, d0, f1, f3 = (swap(own, mask) for mask in (x, y, x | y, z1, z3))
    pair = jnp.concatenate([f1, f3], axis=0)
    xp, yp, f2, d2 = swap(pair, x), swap(pair, y), swap(f3, z1), swap(d0, z2)
    spot = cross(
        (own, whole(0)), (x0, whole(x)), (y0, whole(y)), (d0, whole(x | y)), (f1, whole(z1)), (f3, whole(z3))
    )
    xp, yp, f2, d0 = finish(spot, xp, yp, f2, d0)
    xl = swap(jnp.concatenate([f2, yp[full : full + cut]], axis=0), x)
    yl = swap(jnp.concatenate([f2, xp[full + cut :]], axis=0), y)
    d1 = swap(d0, z1)
    cross((xp, whole(z1 | x, z3 | x)))
    cross((yp, whole(z1 | y, z3 | y)))
    band = gather(found + [(f2, whole(z2)), (d2, whole(z2 | x | y))])
    band, xl, yl, d1, f2, d2 = lax.optimization_barrier((band, xl, yl, d1, f2, d2))
    del found[:]
    cross((xl, [(z2 | x, 0, full), (z3 | x | y, 0, cut)]))
    cross((yl, [(z2 | y, 0, full), (z3 | x | y, cut, full - cut)]))
    for row, mask in ((f2, z2), (d2, z2 | x | y), (d1, z1 | x | y)):
        cross((row, whole(mask)))
    return band, [item for item in found if item[0] is not f2 and item[0] is not d2]


def window(payload, need, cut):
    groups, width = lax.axis_size("row"), lax.axis_size("col")
    count = groups * width
    size = payload.shape[0]
    column = lax.axis_index("col")
    here = lax.axis_index("row") * width + column

    def places(offsets):
        return jnp.where(jnp.abs(offsets) <= need, offsets + need, -1)

    if (groups, width) == (4, 8):

        def split(found):
            masks = np.array([mask for _, parts in found for mask, _, _ in parts])
            device = np.arange(count)[:, None]
            offsets = ((device ^ masks) - device + count // 2) % count - count // 2
            pieces = [(array, [(start, rows) for _, start, rows in parts]) for array, parts in found]
            return pieces, places(jnp.asarray(offsets.astype(np.int32))[here])

        band, late = cube(payload, count, cut, lambda found: assemble(*split(found), size, need))
        return band, *split(late)
    pieces, offsets = [], []
    block = lax.all_gather(payload, "col", axis=0, tiled=True)
    pieces.append((block, [(0, size)] * width))
    offsets.append(jnp.arange(width, dtype=jnp.int32) - column)
    for hop in range(1, -(-need // width) + 1):
        part = min(width, need - (hop - 1) * width)
        up = [(g, (g + hop) % groups) for g in range(groups)]
        down = [(g, (g - hop) % groups) for g in range(groups)]
        steps = jnp.arange(part, dtype=jnp.int32) - column
        pieces.append((lax.ppermute(block[(width - part) * size :], "row", up), [(0, size)] * part))
        offsets.append(steps - (hop - 1) * width - part)
        pieces.append((lax.ppermute(block[: part * size], "row", down), [(0, size)] * part))
        offsets.append(steps + hop * width)
    band = assemble(pieces, places(jnp.concatenate(offsets).astype(jnp.int32)), size, need)
    return band, [], jnp.zeros((1,), jnp.int32)


def row_copies(layout, place, tables, band, arrived, pitch):
    copies = []
    for table, parts in zip(tables, layout):
        begin = 0
        for start, size in parts:
            k = place[len(copies)]
            copy = pltpu.make_async_copy(
                table.at[pl.ds(begin, size)],
                band.at[pl.ds(pl.multiple_of(jnp.maximum(k, 0) * pitch + start, NOTE), size)],
                arrived.at[len(copies)],
            )
            copies.append((k, copy))
            begin += size
    for k, copy in copies:

        @pl.when(k >= 0)
        def _(copy=copy):
            copy.start()

    return copies


def wait_all(copies):
    for k, copy in copies:

        @pl.when(k >= 0)
        def _(copy=copy):
            copy.wait()


def assemble(pieces, place, pitch, need):
    tables = [array for array, _ in pieces]
    layout = [parts for _, parts in pieces]
    kind, edge = tables[0].dtype, tables[0].shape[1]
    rows = 2 * need + 2

    def body(place, *refs):
        band, arrived = refs[len(tables) :]
        copies = row_copies(layout, place, refs[: len(tables)], band, arrived, pitch)

        def clear(s, carry):
            band[pl.ds(pl.multiple_of((rows - 1) * pitch + s * NOTE, NOTE), NOTE), :] = jnp.zeros((NOTE, edge), kind)
            return carry

        lax.fori_loop(0, pitch // NOTE, clear, 0)
        wait_all(copies)

    return pl.pallas_call(
        body,
        out_shape=pltpu.VMEM((rows * pitch, edge), kind),
        in_specs=[pl.BlockSpec(memory_space=pltpu.SMEM)] + [pl.BlockSpec(memory_space=pl.ANY)] * len(tables),
        out_specs=pl.BlockSpec(memory_space=pltpu.VMEM),
        scratch_shapes=[pltpu.SemaphoreType.DMA((sum(len(parts) for parts in layout),))],
        compiler_params=pltpu.CompilerParams(vmem_limit_bytes=2 * 2**20),
        cost_estimate=pl.CostEstimate(flops=0, bytes_accessed=rows * pitch * edge * 4, transcendentals=0),
    )(place, *tables)


def purify(reach, edge, layout, place, *refs):
    count = len(layout)
    tables, (_, band, out, square, own, result, arrived, left_out) = refs[:count], refs[count:]
    far = 2 * reach
    slots, wide = 2 * reach + 1, 4 * reach + 1
    pitch = slots * edge + NOTE
    kind = band.dtype
    copies = row_copies(layout, place, tables, band, arrived, pitch)
    wait_all(copies)

    zero = jnp.zeros((edge, edge), kind)

    def block(k, s):
        return band[pl.ds(pl.multiple_of(k * pitch + s * edge, NOTE), edge), :]

    spots = -(-wide // 8) * 8
    diagonal = lax.broadcasted_iota(jnp.int32, (spots, edge), 0) == lax.broadcasted_iota(jnp.int32, (spots, edge), 1)

    def masks(k):
        line = band[pl.ds(pl.multiple_of(k * pitch + slots * edge, NOTE), NOTE), :].astype(jnp.float32)[:1]
        value = jnp.sum(jnp.where(diagonal, line, 0.0), axis=1, keepdims=True)
        return jnp.broadcast_to(value, (spots, edge))

    def strip(k, first, n):
        return jnp.concatenate(
            [block(k, s) if 0 <= s < slots else zero for s in range(first, first + n)], axis=1
        )

    def square_strip(r, first, n):
        return jnp.concatenate(
            [
                square[r * edge : (r + 1) * edge, u * edge : (u + 1) * edge] if 0 <= u < wide else zero
                for u in range(first, first + n)
            ],
            axis=1,
        )

    def row_group(group, carry):
        r = GROUP * group
        middle = jnp.where(group == reach // GROUP, 1, 0)
        keep = [masks(r + reach + i) for i in range(GROUP)]
        for d in range(-far, far + GROUP, 2):
            low, high = max(-reach, d - reach), min(reach + GROUP - 1, d + reach + 1)
            size = high - low + 1
            left = jnp.concatenate([strip(r + reach + i, low + reach - i, size) for i in range(GROUP)], axis=0)
            right = jnp.concatenate([strip(r + reach + e, d - e + reach, 2) for e in range(low, high + 1)], axis=0)
            product = jnp.dot(left, right, preferred_element_type=jnp.float32)
            for i in range(GROUP):
                for j in range(2):
                    u = d + far - i + j
                    if 0 <= u < wide:
                        kept = product[i * edge : (i + 1) * edge, j * edge : (j + 1) * edge]
                        kept = kept * keep[i][u : u + 1, :]
                        rows = pl.ds(pl.multiple_of((r + i) * edge, edge), edge)
                        square[rows, u * edge : (u + 1) * edge] = kept.astype(kind)
                        if i == reach % GROUP:
                            own[middle, :, u * edge : (u + 1) * edge] = kept
        return carry

    lax.fori_loop(0, (slots + 1) // GROUP, row_group, 0)

    keep = masks(far)
    copies = []
    for c in range(-far, far + 1, WIDTH):
        low, high = max(-reach, c - far), min(reach, c + far + WIDTH - 1)
        left = strip(far, low + reach, high - low + 1)
        right = jnp.concatenate(
            [square_strip(r + reach, c - r + far, WIDTH) for r in range(low, high + 1)], axis=0
        )
        cube = jnp.dot(left, right, preferred_element_type=jnp.float32)
        first, last = c + far, min(c + far + WIDTH, wide)
        for u in range(first, last):
            j = u - first
            value = 3.0 * own[1, :, u * edge : (u + 1) * edge] - 2.0 * cube[:, j * edge : (j + 1) * edge]
            result[u] = (keep[u : u + 1, :] * value).astype(out.dtype)
        copies.append(
            pltpu.make_async_copy(
                result.at[pl.ds(first, last - first)], out.at[pl.ds(first, last - first)], left_out.at[len(copies)]
            )
        )
        copies[-1].start()
    for copy in copies:
        copy.wait()


def pack(pattern, filter_mask, density, payload):
    slots, edge = density.shape[0], density.shape[1]
    for s in range(slots):
        scale = pattern[0, s].astype(jnp.float32)
        payload[s * edge : (s + 1) * edge] = (density[s].astype(jnp.float32) * scale).astype(payload.dtype)
    lane = lax.broadcasted_iota(jnp.int32, (NOTE, edge), 1)
    note = jnp.zeros((NOTE, edge), jnp.float32)
    for u in range(filter_mask.shape[1]):
        note = jnp.where(lane == u, filter_mask[0, u].astype(jnp.float32), note)
    payload[slots * edge :] = note.astype(payload.dtype)


def shards(density, pattern, filter_mask):
    slots, edge = density.shape[1], density.shape[2]
    wide = filter_mask.shape[1]
    reach = (slots - 1) // 2
    far = 2 * reach
    smem, vmem = pl.BlockSpec(memory_space=pltpu.SMEM), pl.BlockSpec(memory_space=pltpu.VMEM)
    payload = pl.pallas_call(
        pack,
        out_shape=jax.ShapeDtypeStruct((slots * edge + NOTE, edge), density.dtype),
        in_specs=[smem, smem, vmem],
        out_specs=vmem,
        compiler_params=pltpu.CompilerParams(vmem_limit_bytes=4 * 2**20),
    )(pattern, filter_mask, density[0])
    band, pieces, place = window(payload, far, (slots + 1) // 2 * edge)
    tables = [array for array, _ in pieces]
    layout = [parts for _, parts in pieces]
    anywhere = pl.BlockSpec(memory_space=pl.ANY)
    _, result = pl.pallas_call(
        functools.partial(purify, reach, edge, layout),
        out_shape=[pltpu.VMEM(band.shape, band.dtype), jax.ShapeDtypeStruct((wide, edge, edge), density.dtype)],
        in_specs=[smem] + [anywhere] * len(tables) + [vmem],
        out_specs=[vmem, anywhere],
        input_output_aliases={1 + len(tables): 0},
        scratch_shapes=[
            pltpu.VMEM(((slots + 1) * edge, wide * edge), density.dtype),
            pltpu.VMEM((2, edge, wide * edge), jnp.float32),
            pltpu.VMEM((wide, edge, edge), density.dtype),
            pltpu.SemaphoreType.DMA((max(1, sum(len(parts) for parts in layout)),)),
            pltpu.SemaphoreType.DMA((-(-wide // WIDTH),)),
        ],
        compiler_params=pltpu.CompilerParams(vmem_limit_bytes=24 * 2**20),
        cost_estimate=pl.CostEstimate(flops=17 * 10**9, bytes_accessed=15 * 2**20, transcendentals=0),
    )(place, *tables, band)
    return result[None]


def solution(mesh):
    in_specs = (P(AXES, None, None, None), P(AXES, None), P(AXES, None))
    out_specs = P(AXES, None, None, None)
    return jax.shard_map(shards, mesh=mesh, in_specs=in_specs, out_specs=out_specs, check_vma=False)
```

```python
import functools

import jax
import jax.numpy as jnp
from jax import lax
from jax.experimental import pallas as pl
from jax.experimental.pallas import tpu as pltpu
from jax.sharding import PartitionSpec as P

NOTE = 16
GROUP = 2
WIDTH = 4
AXES = ("row", "col")


def cube(own, count, cut, gather):
    x, z1, z2, z3, core, y = 1, 2, 4, 6, 8, 16
    full = own.shape[0]
    found = []

    def swap(value, mask):
        return lax.ppermute(value, AXES, [(i, i ^ mask) for i in range(count)])

    def whole(*masks):
        return [(mask, 0, full) for mask in masks]

    def cross(*items):
        arrays = [array for array, _ in items]
        batch = swap(jnp.concatenate(arrays, axis=0) if len(arrays) > 1 else arrays[0], core)
        found.extend(items)
        found.append((batch, [(mask | core, start, size) for _, parts in items for mask, start, size in parts]))
        return len(found) - 1

    def finish(spot, *arrays):
        batch, *arrays = lax.optimization_barrier((found[spot][0],) + arrays)
        found[spot] = (batch, found[spot][1])
        return arrays

    x0, y0, d0, f1, f3 = (swap(own, mask) for mask in (x, y, x | y, z1, z3))
    pair = jnp.concatenate([f1, f3], axis=0)
    xp, yp, f2, d2 = swap(pair, x), swap(pair, y), swap(f3, z1), swap(d0, z2)
    spot = cross(
        (own, whole(0)), (x0, whole(x)), (y0, whole(y)), (d0, whole(x | y)), (f1, whole(z1)), (f3, whole(z3))
    )
    xp, yp, f2, d0 = finish(spot, xp, yp, f2, d0)
    xl = swap(jnp.concatenate([f2, yp[full : full + cut]], axis=0), x)
    yl = swap(jnp.concatenate([f2, xp[full + cut :]], axis=0), y)
    d1 = swap(d0, z1)
    cross((xp, whole(z1 | x, z3 | x)))
    cross((yp, whole(z1 | y, z3 | y)))
    band = gather(found + [(f2, whole(z2)), (d2, whole(z2 | x | y))])
    band, xl, yl, d1, f2, d2 = lax.optimization_barrier((band, xl, yl, d1, f2, d2))
    del found[:]
    cross((xl, [(z2 | x, 0, full), (z3 | x | y, 0, cut)]))
    cross((yl, [(z2 | y, 0, full), (z3 | x | y, cut, full - cut)]))
    for row, mask in ((f2, z2), (d2, z2 | x | y), (d1, z1 | x | y)):
        cross((row, whole(mask)))
    return band, [item for item in found if item[0] is not f2 and item[0] is not d2]


def window(payload, need, cut):
    groups, width = lax.axis_size("row"), lax.axis_size("col")
    count = groups * width
    size = payload.shape[0]

    def flipped(mask):
        def offset():
            here = lax.axis_index("row") * width + lax.axis_index("col")
            return (((here ^ mask) - here + count // 2) & (count - 1)) - count // 2

        return offset

    def shifted(place):
        return lambda: place - lax.axis_index("col")

    if (groups, width) == (4, 8):

        def pieces(found):
            return [(array, [(start, rows, flipped(mask)) for mask, start, rows in parts]) for array, parts in found]

        band, late = cube(payload, count, cut, lambda found: assemble(pieces(found), size, need))
        return band, pieces(late)

    def piece(array, first):
        return array, [(0, size, shifted(first + j)) for j in range(array.shape[0] // size)]

    block = lax.all_gather(payload, "col", axis=0, tiled=True)
    pieces = [piece(block, 0)]
    for hop in range(1, -(-need // width) + 1):
        part = min(width, need - (hop - 1) * width)
        up = [(g, (g + hop) % groups) for g in range(groups)]
        down = [(g, (g - hop) % groups) for g in range(groups)]
        pieces.append(piece(lax.ppermute(block[(width - part) * size :], "row", up), (1 - hop) * width - part))
        pieces.append(piece(lax.ppermute(block[: part * size], "row", down), hop * width))
    return assemble(pieces, size, need), []


def row_copies(layout, need, tables, band, arrived, pitch):
    copies = []
    for table, parts in zip(tables, layout):
        begin = 0
        for start, size, offset in parts:
            k = offset() + need
            wanted = (k >= 0) & (k <= 2 * need)
            row = jnp.where(wanted, k, 0)
            copy = pltpu.make_async_copy(
                table.at[pl.ds(begin, size)],
                band.at[pl.ds(pl.multiple_of(row * pitch + start, NOTE), size)],
                arrived.at[len(copies)],
            )
            copies.append((wanted, copy))
            begin += size
    for wanted, copy in copies:

        @pl.when(wanted)
        def _(copy=copy):
            copy.start()

    return copies


def wait_all(copies):
    for wanted, copy in copies:

        @pl.when(wanted)
        def _(copy=copy):
            copy.wait()


def assemble(pieces, pitch, need):
    tables = [array for array, _ in pieces]
    layout = [parts for _, parts in pieces]
    kind, edge = tables[0].dtype, tables[0].shape[1]
    rows = 2 * need + 2

    def body(*refs):
        band, arrived = refs[len(tables) :]
        copies = row_copies(layout, need, refs[: len(tables)], band, arrived, pitch)

        def clear(s, carry):
            band[pl.ds(pl.multiple_of((rows - 1) * pitch + s * NOTE, NOTE), NOTE), :] = jnp.zeros((NOTE, edge), kind)
            return carry

        lax.fori_loop(0, pitch // NOTE, clear, 0)
        wait_all(copies)

    return pl.pallas_call(
        body,
        out_shape=pltpu.VMEM((rows * pitch, edge), kind),
        in_specs=[pl.BlockSpec(memory_space=pl.ANY)] * len(tables),
        out_specs=pl.BlockSpec(memory_space=pltpu.VMEM),
        scratch_shapes=[pltpu.SemaphoreType.DMA((sum(len(parts) for parts in layout),))],
        compiler_params=pltpu.CompilerParams(vmem_limit_bytes=2 * 2**20),
        cost_estimate=pl.CostEstimate(flops=0, bytes_accessed=rows * pitch * edge * 4, transcendentals=0),
    )(*tables)


def purify(reach, edge, layout, *refs):
    count = len(layout)
    tables, (_, band, out, square, own, result, arrived, left_out) = refs[:count], refs[count:]
    far = 2 * reach
    slots, wide = 2 * reach + 1, 4 * reach + 1
    pitch = slots * edge + NOTE
    kind = band.dtype
    copies = row_copies(layout, far, tables, band, arrived, pitch)
    wait_all(copies)

    zero = jnp.zeros((edge, edge), kind)

    def block(k, s):
        return band[pl.ds(pl.multiple_of(k * pitch + s * edge, NOTE), edge), :]

    spots = -(-wide // 8) * 8
    diagonal = lax.broadcasted_iota(jnp.int32, (spots, edge), 0) == lax.broadcasted_iota(jnp.int32, (spots, edge), 1)

    def masks(k):
        line = band[pl.ds(pl.multiple_of(k * pitch + slots * edge, NOTE), NOTE), :].astype(jnp.float32)[:1]
        value = jnp.sum(jnp.where(diagonal, line, 0.0), axis=1, keepdims=True)
        return jnp.broadcast_to(value, (spots, edge))

    def strip(k, first, n):
        return jnp.concatenate(
            [block(k, s) if 0 <= s < slots else zero for s in range(first, first + n)], axis=1
        )

    def square_strip(r, first, n):
        return jnp.concatenate(
            [
                square[r * edge : (r + 1) * edge, u * edge : (u + 1) * edge] if 0 <= u < wide else zero
                for u in range(first, first + n)
            ],
            axis=1,
        )

    def row_group(group, carry):
        r = GROUP * group
        middle = jnp.where(group == reach // GROUP, 1, 0)
        keep = [masks(r + reach + i) for i in range(GROUP)]
        for d in range(-far, far + GROUP, 2):
            low, high = max(-reach, d - reach), min(reach + GROUP - 1, d + reach + 1)
            size = high - low + 1
            left = jnp.concatenate([strip(r + reach + i, low + reach - i, size) for i in range(GROUP)], axis=0)
            right = jnp.concatenate([strip(r + reach + e, d - e + reach, 2) for e in range(low, high + 1)], axis=0)
            product = jnp.dot(left, right, preferred_element_type=jnp.float32)
            for i in range(GROUP):
                for j in range(2):
                    u = d + far - i + j
                    if 0 <= u < wide:
                        kept = product[i * edge : (i + 1) * edge, j * edge : (j + 1) * edge]
                        kept = kept * keep[i][u : u + 1, :]
                        rows = pl.ds(pl.multiple_of((r + i) * edge, edge), edge)
                        square[rows, u * edge : (u + 1) * edge] = kept.astype(kind)
                        if i == reach % GROUP:
                            own[middle, :, u * edge : (u + 1) * edge] = kept
        return carry

    lax.fori_loop(0, (slots + 1) // GROUP, row_group, 0)

    keep = masks(far)
    copies = []
    for c in range(-far, far + 1, WIDTH):
        low, high = max(-reach, c - far), min(reach, c + far + WIDTH - 1)
        left = strip(far, low + reach, high - low + 1)
        right = jnp.concatenate(
            [square_strip(r + reach, c - r + far, WIDTH) for r in range(low, high + 1)], axis=0
        )
        cube = jnp.dot(left, right, preferred_element_type=jnp.float32)
        first, last = c + far, min(c + far + WIDTH, wide)
        for u in range(first, last):
            j = u - first
            value = 3.0 * own[1, :, u * edge : (u + 1) * edge] - 2.0 * cube[:, j * edge : (j + 1) * edge]
            result[u] = (keep[u : u + 1, :] * value).astype(out.dtype)
        copies.append(
            pltpu.make_async_copy(
                result.at[pl.ds(first, last - first)], out.at[pl.ds(first, last - first)], left_out.at[len(copies)]
            )
        )
        copies[-1].start()
    for copy in copies:
        copy.wait()


def pack(pattern, filter_mask, density, payload):
    slots, edge = density.shape[0], density.shape[1]
    for s in range(slots):
        scale = pattern[0, s].astype(jnp.float32)
        payload[s * edge : (s + 1) * edge] = (density[s].astype(jnp.float32) * scale).astype(payload.dtype)
    lane = lax.broadcasted_iota(jnp.int32, (NOTE, edge), 1)
    note = jnp.zeros((NOTE, edge), jnp.float32)
    for u in range(filter_mask.shape[1]):
        note = jnp.where(lane == u, filter_mask[0, u].astype(jnp.float32), note)
    payload[slots * edge :] = note.astype(payload.dtype)


def shards(density, pattern, filter_mask):
    slots, edge = density.shape[1], density.shape[2]
    wide = filter_mask.shape[1]
    reach = (slots - 1) // 2
    far = 2 * reach
    smem, vmem = pl.BlockSpec(memory_space=pltpu.SMEM), pl.BlockSpec(memory_space=pltpu.VMEM)
    payload = pl.pallas_call(
        pack,
        out_shape=jax.ShapeDtypeStruct((slots * edge + NOTE, edge), density.dtype),
        in_specs=[smem, smem, vmem],
        out_specs=vmem,
        compiler_params=pltpu.CompilerParams(vmem_limit_bytes=4 * 2**20),
    )(pattern, filter_mask, density[0])
    band, pieces = window(payload, far, (slots + 1) // 2 * edge)
    tables = [array for array, _ in pieces]
    layout = [parts for _, parts in pieces]
    anywhere = pl.BlockSpec(memory_space=pl.ANY)
    _, result = pl.pallas_call(
        functools.partial(purify, reach, edge, layout),
        out_shape=[pltpu.VMEM(band.shape, band.dtype), jax.ShapeDtypeStruct((wide, edge, edge), density.dtype)],
        in_specs=[anywhere] * len(tables) + [vmem],
        out_specs=[vmem, anywhere],
        input_output_aliases={len(tables): 0},
        scratch_shapes=[
            pltpu.VMEM(((slots + 1) * edge, wide * edge), density.dtype),
            pltpu.VMEM((2, edge, wide * edge), jnp.float32),
            pltpu.VMEM((wide, edge, edge), density.dtype),
            pltpu.SemaphoreType.DMA((max(1, sum(len(parts) for parts in layout)),)),
            pltpu.SemaphoreType.DMA((-(-wide // WIDTH),)),
        ],
        compiler_params=pltpu.CompilerParams(vmem_limit_bytes=24 * 2**20),
        cost_estimate=pl.CostEstimate(flops=17 * 10**9, bytes_accessed=15 * 2**20, transcendentals=0),
    )(*tables, band)
    return result[None]


def solution(mesh):
    in_specs = (P(AXES, None, None, None), P(AXES, None), P(AXES, None))
    out_specs = P(AXES, None, None, None)
    return jax.shard_map(shards, mesh=mesh, in_specs=in_specs, out_specs=out_specs, check_vma=False)
```

```python
import functools

import jax
import jax.numpy as jnp
from jax import lax
from jax.experimental import pallas as pl
from jax.experimental.pallas import tpu as pltpu
from jax.sharding import PartitionSpec as P

NOTE = 16
GROUP = 2
WIDTH = 4
PIECES = 3
AXES = ("row", "col")


def cube(own, count, cut, gather):
    x, z1, z2, z3, core, y = 1, 2, 4, 6, 8, 16
    full = own.shape[0]
    found = []

    def swap(value, mask):
        return lax.ppermute(value, AXES, [(i, i ^ mask) for i in range(count)])

    def whole(*masks):
        return [(mask, 0, full) for mask in masks]

    def cross(*items):
        arrays = [array for array, _ in items]
        batch = swap(jnp.concatenate(arrays, axis=0) if len(arrays) > 1 else arrays[0], core)
        found.extend(items)
        found.append((batch, [(mask | core, start, size) for _, parts in items for mask, start, size in parts]))
        return len(found) - 1

    def finish(spot, *arrays):
        batch, *arrays = lax.optimization_barrier((found[spot][0],) + arrays)
        found[spot] = (batch, found[spot][1])
        return arrays

    x0, y0, d0, f1, f3 = (swap(own, mask) for mask in (x, y, x | y, z1, z3))
    pair = jnp.concatenate([f1, f3], axis=0)
    xp, yp, f2, d2 = swap(pair, x), swap(pair, y), swap(f3, z1), swap(d0, z2)
    spot = cross(
        (own, whole(0)), (x0, whole(x)), (y0, whole(y)), (d0, whole(x | y)), (f1, whole(z1)), (f3, whole(z3))
    )
    xp, yp, f2, d0 = finish(spot, xp, yp, f2, d0)
    xl = swap(jnp.concatenate([f2, yp[full : full + cut]], axis=0), x)
    yl = swap(jnp.concatenate([f2, xp[full + cut :]], axis=0), y)
    d1 = swap(d0, z1)
    cross((xp, whole(z1 | x, z3 | x)))
    cross((yp, whole(z1 | y, z3 | y)))
    band = gather(found + [(f2, whole(z2)), (d2, whole(z2 | x | y))])
    band, xl, yl, d1, f2, d2 = lax.optimization_barrier((band, xl, yl, d1, f2, d2))
    del found[:]
    cross((xl, [(z2 | x, 0, full), (z3 | x | y, 0, cut)]))
    cross((yl, [(z2 | y, 0, full), (z3 | x | y, cut, full - cut)]))
    for row, mask in ((f2, z2), (d2, z2 | x | y), (d1, z1 | x | y)):
        cross((row, whole(mask)))
    return band, [item for item in found if item[0] is not f2 and item[0] is not d2]


def window(payload, need, cut):
    groups, width = lax.axis_size("row"), lax.axis_size("col")
    count = groups * width
    size = payload.shape[0]

    def flipped(mask):
        def offset():
            here = lax.axis_index("row") * width + lax.axis_index("col")
            return (((here ^ mask) - here + count // 2) & (count - 1)) - count // 2

        return offset

    def shifted(place):
        return lambda: place - lax.axis_index("col")

    if (groups, width) == (4, 8):

        def pieces(found):
            return [(array, [(start, rows, flipped(mask)) for mask, start, rows in parts]) for array, parts in found]

        band, late = cube(payload, count, cut, lambda found: assemble(pieces(found), size, need))
        return band, pieces(late)

    def piece(array, first):
        return array, [(0, size, shifted(first + j)) for j in range(array.shape[0] // size)]

    block = lax.all_gather(payload, "col", axis=0, tiled=True)
    pieces = [piece(block, 0)]
    for hop in range(1, -(-need // width) + 1):
        part = min(width, need - (hop - 1) * width)
        up = [(g, (g + hop) % groups) for g in range(groups)]
        down = [(g, (g - hop) % groups) for g in range(groups)]
        pieces.append(piece(lax.ppermute(block[(width - part) * size :], "row", up), (1 - hop) * width - part))
        pieces.append(piece(lax.ppermute(block[: part * size], "row", down), hop * width))
    return assemble(pieces, size, need), []


def row_copies(layout, need, tables, band, arrived, pitch):
    copies = []
    for table, parts in zip(tables, layout):
        begin = 0
        for start, size, offset in parts:
            k = offset() + need
            wanted = (k >= 0) & (k <= 2 * need)
            row = jnp.where(wanted, k, 0)
            copy = pltpu.make_async_copy(
                table.at[pl.ds(begin, size)],
                band.at[pl.ds(pl.multiple_of(row * pitch + start, NOTE), size)],
                arrived.at[len(copies)],
            )
            copies.append((wanted, copy))
            begin += size
    for wanted, copy in copies:

        @pl.when(wanted)
        def _(copy=copy):
            copy.start()

    return copies


def wait_all(copies):
    for wanted, copy in copies:

        @pl.when(wanted)
        def _(copy=copy):
            copy.wait()


def assemble(pieces, pitch, need):
    tables = [array for array, _ in pieces]
    layout = [parts for _, parts in pieces]
    kind, edge = tables[0].dtype, tables[0].shape[1]
    rows = 2 * need + 1

    def body(*refs):
        band, arrived = refs[len(tables) :]
        copies = row_copies(layout, need, refs[: len(tables)], band, arrived, pitch)
        wait_all(copies)

    return pl.pallas_call(
        body,
        out_shape=pltpu.VMEM((rows * pitch, edge), kind),
        in_specs=[pl.BlockSpec(memory_space=pl.ANY)] * len(tables),
        out_specs=pl.BlockSpec(memory_space=pltpu.VMEM),
        scratch_shapes=[pltpu.SemaphoreType.DMA((sum(len(parts) for parts in layout),))],
        compiler_params=pltpu.CompilerParams(vmem_limit_bytes=2 * 2**20),
        cost_estimate=pl.CostEstimate(flops=0, bytes_accessed=rows * pitch * edge * 4, transcendentals=0),
    )(*tables)


def purify(reach, edge, layout, *refs):
    count = len(layout)
    tables, (_, band, out, square, own, result, arrived, left_out) = refs[:count], refs[count:]
    far = 2 * reach
    slots, wide = 2 * reach + 1, 4 * reach + 1
    pitch = slots * edge + NOTE
    kind = band.dtype
    copies = row_copies(layout, far, tables, band, arrived, pitch)
    wait_all(copies)

    zero = jnp.zeros((edge, edge), kind)

    def from_row(first, n):
        return pl.ds(first if isinstance(first, int) else pl.multiple_of(first, NOTE), n)

    def block(k, s):
        return band[from_row(k * pitch + s * edge, edge), :]

    spots = -(-wide // 8) * 8
    diagonal = lax.broadcasted_iota(jnp.int32, (spots, edge), 0) == lax.broadcasted_iota(jnp.int32, (spots, edge), 1)

    def masks(k):
        line = band[from_row(k * pitch + slots * edge, NOTE), :].astype(jnp.float32)[:1]
        value = jnp.sum(jnp.where(diagonal, line, 0.0), axis=1, keepdims=True)
        return jnp.broadcast_to(value, (spots, edge))

    def strip(k, first, n):
        return jnp.concatenate(
            [block(k, s) if 0 <= s < slots else zero for s in range(first, first + n)], axis=1
        )

    def square_strip(r, first, n):
        return jnp.concatenate(
            [
                square[r * edge : (r + 1) * edge, u * edge : (u + 1) * edge] if 0 <= u < wide else zero
                for u in range(first, first + n)
            ],
            axis=1,
        )

    def square_rows(r, n, slot, own_row, offsets):
        keep = [masks(r + reach + i) for i in range(n)]
        for d in offsets:
            low, high = max(-reach, d - reach), min(reach + n - 1, d + reach + 1)
            size = high - low + 1
            left = jnp.concatenate([strip(r + reach + i, low + reach - i, size) for i in range(n)], axis=0)
            right = jnp.concatenate([strip(r + reach + e, d - e + reach, 2) for e in range(low, high + 1)], axis=0)
            product = jnp.dot(left, right, preferred_element_type=jnp.float32)
            for i in range(n):
                for j in range(2):
                    u = d + far - i + j
                    if 0 <= u < wide:
                        kept = product[i * edge : (i + 1) * edge, j * edge : (j + 1) * edge]
                        kept = kept * keep[i][u : u + 1, :]
                        square[from_row((r + i) * edge, edge), u * edge : (u + 1) * edge] = kept.astype(kind)
                        if i == own_row:
                            own[slot, :, u * edge : (u + 1) * edge] = kept

    def row_group(group, carry):
        slot = jnp.where(group == reach // GROUP, 1, 0)
        square_rows(GROUP * group, GROUP, slot, reach % GROUP, range(-far, far + GROUP, 2))
        return carry

    lax.fori_loop(0, slots // GROUP, row_group, 0)
    for r in range(slots // GROUP * GROUP, slots):
        square_rows(r, 1, 0, None, range(-far, far + reach - r + 1, 2))

    keep = masks(far)
    copies = []
    for c in range(-far, far + 1, WIDTH):
        low, high = max(-reach, c - far), min(reach, c + far + WIDTH - 1)
        left = strip(far, low + reach, high - low + 1)
        right = jnp.concatenate(
            [square_strip(r + reach, c - r + far, WIDTH) for r in range(low, high + 1)], axis=0
        )
        cube = jnp.dot(left, right, preferred_element_type=jnp.float32)
        first, last = c + far, min(c + far + WIDTH, wide)
        for u in range(first, last):
            j = u - first
            value = 3.0 * own[1, :, u * edge : (u + 1) * edge] - 2.0 * cube[:, j * edge : (j + 1) * edge]
            result[u] = (keep[u : u + 1, :] * value).astype(out.dtype)
        copies.append(
            pltpu.make_async_copy(
                result.at[pl.ds(first, last - first)], out.at[pl.ds(first, last - first)], left_out.at[len(copies)]
            )
        )
        copies[-1].start()
    for copy in copies:
        copy.wait()


def pack(pattern, filter_mask, density, payload, blocks, packed, arrived, left):
    slots, edge = density.shape[0], density.shape[1]
    bounds = [slots * part // PIECES for part in range(PIECES + 1)]
    fetches, stores = [], []
    for part in range(PIECES):
        held = pl.ds(bounds[part], bounds[part + 1] - bounds[part])
        fetches.append(pltpu.make_async_copy(density.at[held], blocks.at[held], arrived.at[part]))
        fetches[-1].start()
    lane = lax.broadcasted_iota(jnp.int32, (NOTE, edge), 1)
    note = jnp.zeros((NOTE, edge), jnp.float32)
    for u in range(filter_mask.shape[1]):
        note = jnp.where(lane == u, filter_mask[0, u].astype(jnp.float32), note)
    packed[slots * edge :] = note.astype(packed.dtype)
    for part in range(PIECES):
        fetches[part].wait()
        for s in range(bounds[part], bounds[part + 1]):
            scale = pattern[0, s].astype(jnp.float32)
            packed[s * edge : (s + 1) * edge] = (blocks[s].astype(jnp.float32) * scale).astype(packed.dtype)
        end = bounds[part + 1] * edge + (NOTE if part == PIECES - 1 else 0)
        held = pl.ds(bounds[part] * edge, end - bounds[part] * edge)
        stores.append(pltpu.make_async_copy(packed.at[held], payload.at[held], left.at[part]))
        stores[-1].start()
    for store in stores:
        store.wait()


def shards(density, pattern, filter_mask):
    slots, edge = density.shape[1], density.shape[2]
    wide = filter_mask.shape[1]
    reach = (slots - 1) // 2
    far = 2 * reach
    smem, vmem = pl.BlockSpec(memory_space=pltpu.SMEM), pl.BlockSpec(memory_space=pltpu.VMEM)
    anywhere = pl.BlockSpec(memory_space=pl.ANY)
    payload = pl.pallas_call(
        pack,
        out_shape=jax.ShapeDtypeStruct((slots * edge + NOTE, edge), density.dtype),
        in_specs=[smem, smem, anywhere],
        out_specs=anywhere,
        scratch_shapes=[
            pltpu.VMEM((slots, edge, edge), density.dtype),
            pltpu.VMEM((slots * edge + NOTE, edge), density.dtype),
            pltpu.SemaphoreType.DMA((PIECES,)),
            pltpu.SemaphoreType.DMA((PIECES,)),
        ],
        compiler_params=pltpu.CompilerParams(vmem_limit_bytes=60 * 2**20),
    )(pattern, filter_mask, density[0])
    band, pieces = window(payload, far, (slots + 1) // 2 * edge)
    tables = [array for array, _ in pieces]
    layout = [parts for _, parts in pieces]
    _, result = pl.pallas_call(
        functools.partial(purify, reach, edge, layout),
        out_shape=[pltpu.VMEM(band.shape, band.dtype), jax.ShapeDtypeStruct((wide, edge, edge), density.dtype)],
        in_specs=[anywhere] * len(tables) + [vmem],
        out_specs=[vmem, anywhere],
        input_output_aliases={len(tables): 0},
        scratch_shapes=[
            pltpu.VMEM((slots * edge, wide * edge), density.dtype),
            pltpu.VMEM((2, edge, wide * edge), jnp.float32),
            pltpu.VMEM((wide, edge, edge), density.dtype),
            pltpu.SemaphoreType.DMA((max(1, sum(len(parts) for parts in layout)),)),
            pltpu.SemaphoreType.DMA((-(-wide // WIDTH),)),
        ],
        compiler_params=pltpu.CompilerParams(vmem_limit_bytes=24 * 2**20),
        cost_estimate=pl.CostEstimate(flops=17 * 10**9, bytes_accessed=15 * 2**20, transcendentals=0),
    )(*tables, band)
    return result[None]


def solution(mesh):
    in_specs = (P(AXES, None, None, None), P(AXES, None), P(AXES, None))
    out_specs = P(AXES, None, None, None)
    return jax.shard_map(shards, mesh=mesh, in_specs=in_specs, out_specs=out_specs, check_vma=False)
```

```python
import functools

import jax
import jax.numpy as jnp
from jax import lax
from jax.experimental import pallas as pl
from jax.experimental.pallas import tpu as pltpu
from jax.sharding import PartitionSpec as P

NOTE = 16
GROUP = 2
WIDTH = 4
AXES = ("row", "col")


def cube(own, count, cut, gather):
    x, z1, z2, z3, core, y = 1, 2, 4, 6, 8, 16
    full = own.shape[0]
    found = []

    def swap(value, mask):
        return lax.ppermute(value, AXES, [(i, i ^ mask) for i in range(count)])

    def whole(*masks):
        return [(mask, 0, full) for mask in masks]

    def cross(*items):
        arrays = [array for array, _ in items]
        batch = swap(jnp.concatenate(arrays, axis=0) if len(arrays) > 1 else arrays[0], core)
        found.extend(items)
        found.append((batch, [(mask | core, start, size) for _, parts in items for mask, start, size in parts]))
        return len(found) - 1

    def finish(spot, *arrays):
        batch, *arrays = lax.optimization_barrier((found[spot][0],) + arrays)
        found[spot] = (batch, found[spot][1])
        return arrays

    x0, y0, d0, f1, f3 = (swap(own, mask) for mask in (x, y, x | y, z1, z3))
    pair = jnp.concatenate([f1, f3], axis=0)
    xp, yp, f2, d2 = swap(pair, x), swap(pair, y), swap(f3, z1), swap(d0, z2)
    spot = cross(
        (own, whole(0)), (x0, whole(x)), (y0, whole(y)), (d0, whole(x | y)), (f1, whole(z1)), (f3, whole(z3))
    )
    xp, yp, f2, d0 = finish(spot, xp, yp, f2, d0)
    xl = swap(jnp.concatenate([f2, yp[full : full + cut]], axis=0), x)
    yl = swap(jnp.concatenate([f2, xp[full + cut :]], axis=0), y)
    d1 = swap(d0, z1)
    cross((xp, whole(z1 | x, z3 | x)))
    cross((yp, whole(z1 | y, z3 | y)))
    band = gather(None, found + [(f2, whole(z2)), (d2, whole(z2 | x | y))])
    band, xl, yl, d1, f2, d2 = lax.optimization_barrier((band, xl, yl, d1, f2, d2))
    del found[:]
    cross((xl, [(z2 | x, 0, full), (z3 | x | y, 0, cut)]))
    cross((yl, [(z2 | y, 0, full), (z3 | x | y, cut, full - cut)]))
    for row, mask in ((f2, z2), (d2, z2 | x | y), (d1, z1 | x | y)):
        cross((row, whole(mask)))
    return gather(band, [item for item in found if any(item[0] is late for late in (xl, yl, d1))]), found[1::2]


def window(payload, need, cut):
    groups, width = lax.axis_size("row"), lax.axis_size("col")
    count = groups * width
    size = payload.shape[0]

    def flipped(mask):
        def offset():
            here = lax.axis_index("row") * width + lax.axis_index("col")
            return (((here ^ mask) - here + count // 2) & (count - 1)) - count // 2

        return offset

    def shifted(place):
        return lambda: place - lax.axis_index("col")

    if (groups, width) == (4, 8):

        def pieces(found):
            return [(array, [(start, rows, flipped(mask)) for mask, start, rows in parts]) for array, parts in found]

        def gather(band, found):
            return assemble(pieces(found), size, need, band)

        band, late = cube(payload, count, cut, gather)
        return band, pieces(late)

    def piece(array, first):
        return array, [(0, size, shifted(first + j)) for j in range(array.shape[0] // size)]

    block = lax.all_gather(payload, "col", axis=0, tiled=True)
    pieces = [piece(block, 0)]
    for hop in range(1, -(-need // width) + 1):
        part = min(width, need - (hop - 1) * width)
        up = [(g, (g + hop) % groups) for g in range(groups)]
        down = [(g, (g - hop) % groups) for g in range(groups)]
        pieces.append(piece(lax.ppermute(block[(width - part) * size :], "row", up), (1 - hop) * width - part))
        pieces.append(piece(lax.ppermute(block[: part * size], "row", down), hop * width))
    return assemble(pieces, size, need), []


def row_copies(layout, need, tables, band, arrived, pitch):
    copies = []
    for table, parts in zip(tables, layout):
        begin = 0
        for start, size, offset in parts:
            k = offset() + need
            wanted = (k >= 0) & (k <= 2 * need)
            row = jnp.where(wanted, k, 0)
            copy = pltpu.make_async_copy(
                table.at[pl.ds(begin, size)],
                band.at[pl.ds(pl.multiple_of(row * pitch + start, NOTE), size)],
                arrived.at[len(copies)],
            )
            copies.append((wanted, row, copy))
            begin += size
    for wanted, _, copy in copies:

        @pl.when(wanted)
        def _(copy=copy):
            copy.start()

    return copies


def wait_all(copies):
    for wanted, _, copy in copies:

        @pl.when(wanted)
        def _(copy=copy):
            copy.wait()


def assemble(pieces, pitch, need, band=None):
    tables = [array for array, _ in pieces]
    layout = [parts for _, parts in pieces]
    kind, edge = tables[0].dtype, tables[0].shape[1]
    rows = 2 * need + 1

    vmem = pl.BlockSpec(memory_space=pltpu.VMEM)
    given = [] if band is None else [band]

    def body(*refs):
        band, arrived = refs[-2:]
        wait_all(row_copies(layout, need, refs[: len(tables)], band, arrived, pitch))

    return pl.pallas_call(
        body,
        out_shape=pltpu.VMEM((rows * pitch, edge), kind),
        in_specs=[pl.BlockSpec(memory_space=pl.ANY)] * len(tables) + [vmem] * len(given),
        out_specs=vmem,
        input_output_aliases={len(tables): 0} if given else {},
        scratch_shapes=[pltpu.SemaphoreType.DMA((sum(len(parts) for parts in layout),))],
        compiler_params=pltpu.CompilerParams(vmem_limit_bytes=2 * 2**20),
        cost_estimate=pl.CostEstimate(
            flops=0, bytes_accessed=sum(table.size for table in tables) * 4, transcendentals=0
        ),
    )(*tables, *given)


def purify(reach, edge, layout, *refs):
    count = len(layout)
    tables, (_, band, out, square, own, result, arrived, left_out) = refs[:count], refs[count:]
    far = 2 * reach
    slots, wide = 2 * reach + 1, 4 * reach + 1
    pitch = slots * edge + NOTE
    kind = band.dtype
    late = row_copies(layout, far, tables, band, arrived, pitch)

    zero = jnp.zeros((edge, edge), kind)

    def from_row(first, n):
        return pl.ds(first if isinstance(first, int) else pl.multiple_of(first, NOTE), n)

    def block(k, s):
        return band[from_row(k * pitch + s * edge, edge), :]

    spots = -(-wide // 8) * 8
    diagonal = lax.broadcasted_iota(jnp.int32, (spots, edge), 0) == lax.broadcasted_iota(jnp.int32, (spots, edge), 1)

    def masks(k):
        line = band[from_row(k * pitch + slots * edge, NOTE), :].astype(jnp.float32)[:1]
        value = jnp.sum(jnp.where(diagonal, line, 0.0), axis=1, keepdims=True)
        return jnp.broadcast_to(value, (spots, edge))

    def strip(k, first, n):
        return jnp.concatenate(
            [block(k, s) if 0 <= s < slots else zero for s in range(first, first + n)], axis=1
        )

    def square_strip(r, first, n):
        return jnp.concatenate(
            [
                square[r * edge : (r + 1) * edge, u * edge : (u + 1) * edge] if 0 <= u < wide else zero
                for u in range(first, first + n)
            ],
            axis=1,
        )

    def square_rows(r, n, slot, own_row, offsets):
        keep = [masks(r + reach + i) for i in range(n)]
        for d in offsets:
            low, high = max(-reach, d - reach), min(reach + n - 1, d + reach + 1)
            size = high - low + 1
            left = jnp.concatenate([strip(r + reach + i, low + reach - i, size) for i in range(n)], axis=0)
            right = jnp.concatenate([strip(r + reach + e, d - e + reach, 2) for e in range(low, high + 1)], axis=0)
            product = jnp.dot(left, right, preferred_element_type=jnp.float32)
            for i in range(n):
                for j in range(2):
                    u = d + far - i + j
                    if 0 <= u < wide:
                        kept = product[i * edge : (i + 1) * edge, j * edge : (j + 1) * edge]
                        kept = kept * keep[i][u : u + 1, :]
                        square[from_row((r + i) * edge, edge), u * edge : (u + 1) * edge] = kept.astype(kind)
                        if i == own_row:
                            own[slot, :, u * edge : (u + 1) * edge] = kept

    def first_user(row):
        return jnp.minimum(lax.div(jnp.maximum(row - far, 0), GROUP), slots // GROUP - 1)

    def row_group(group, carry):
        needed = [(first_user(row) == group) & wanted for wanted, row, _ in late]
        wait_all([(now, row, copy) for now, (_, row, copy) in zip(needed, late)])
        slot = jnp.where(group == reach // GROUP, 1, 0)
        square_rows(GROUP * group, GROUP, slot, reach % GROUP, range(-far, far + GROUP, 2))
        return carry

    lax.fori_loop(0, slots // GROUP, row_group, 0)
    for r in range(slots // GROUP * GROUP, slots):
        square_rows(r, 1, 0, None, range(-far, far + reach - r + 1, 2))

    keep = masks(far)
    copies = []
    for c in range(-far, far + 1, WIDTH):
        low, high = max(-reach, c - far), min(reach, c + far + WIDTH - 1)
        left = strip(far, low + reach, high - low + 1)
        right = jnp.concatenate(
            [square_strip(r + reach, c - r + far, WIDTH) for r in range(low, high + 1)], axis=0
        )
        cube = jnp.dot(left, right, preferred_element_type=jnp.float32)
        first, last = c + far, min(c + far + WIDTH, wide)
        for u in range(first, last):
            j = u - first
            value = 3.0 * own[1, :, u * edge : (u + 1) * edge] - 2.0 * cube[:, j * edge : (j + 1) * edge]
            result[u] = (keep[u : u + 1, :] * value).astype(out.dtype)
        copies.append(
            pltpu.make_async_copy(
                result.at[pl.ds(first, last - first)], out.at[pl.ds(first, last - first)], left_out.at[len(copies)]
            )
        )
        copies[-1].start()
    for copy in copies:
        copy.wait()


def pack(pattern, filter_mask, density, payload):
    slots, edge = density.shape[0], density.shape[1]
    for s in range(slots):
        scale = pattern[0, s].astype(jnp.float32)
        payload[s * edge : (s + 1) * edge] = (density[s].astype(jnp.float32) * scale).astype(payload.dtype)
    lane = lax.broadcasted_iota(jnp.int32, (NOTE, edge), 1)
    note = jnp.zeros((NOTE, edge), jnp.float32)
    for u in range(filter_mask.shape[1]):
        note = jnp.where(lane == u, filter_mask[0, u].astype(jnp.float32), note)
    payload[slots * edge :] = note.astype(payload.dtype)


def shards(density, pattern, filter_mask):
    slots, edge = density.shape[1], density.shape[2]
    wide = filter_mask.shape[1]
    reach = (slots - 1) // 2
    far = 2 * reach
    smem, vmem = pl.BlockSpec(memory_space=pltpu.SMEM), pl.BlockSpec(memory_space=pltpu.VMEM)
    anywhere = pl.BlockSpec(memory_space=pl.ANY)
    payload = pl.pallas_call(
        pack,
        out_shape=jax.ShapeDtypeStruct((slots * edge + NOTE, edge), density.dtype),
        in_specs=[smem, smem, vmem],
        out_specs=vmem,
        compiler_params=pltpu.CompilerParams(vmem_limit_bytes=60 * 2**20),
    )(pattern, filter_mask, density[0])
    band, pieces = window(payload, far, (slots + 1) // 2 * edge)
    tables = [array for array, _ in pieces]
    layout = [parts for _, parts in pieces]
    _, result = pl.pallas_call(
        functools.partial(purify, reach, edge, layout),
        out_shape=[pltpu.VMEM(band.shape, band.dtype), jax.ShapeDtypeStruct((wide, edge, edge), density.dtype)],
        in_specs=[anywhere] * len(tables) + [vmem],
        out_specs=[vmem, anywhere],
        input_output_aliases={len(tables): 0},
        scratch_shapes=[
            pltpu.VMEM((slots * edge, wide * edge), density.dtype),
            pltpu.VMEM((2, edge, wide * edge), jnp.float32),
            pltpu.VMEM((wide, edge, edge), density.dtype),
            pltpu.SemaphoreType.DMA((max(1, sum(len(parts) for parts in layout)),)),
            pltpu.SemaphoreType.DMA((-(-wide // WIDTH),)),
        ],
        compiler_params=pltpu.CompilerParams(vmem_limit_bytes=24 * 2**20),
        cost_estimate=pl.CostEstimate(flops=17 * 10**9, bytes_accessed=15 * 2**20, transcendentals=0),
    )(*tables, band)
    return result[None]


def solution(mesh):
    in_specs = (P(AXES, None, None, None), P(AXES, None), P(AXES, None))
    out_specs = P(AXES, None, None, None)
    return jax.shard_map(shards, mesh=mesh, in_specs=in_specs, out_specs=out_specs, check_vma=False)
```

```python
import functools

import jax
import jax.numpy as jnp
from jax import lax
from jax.experimental import pallas as pl
from jax.experimental.pallas import tpu as pltpu
from jax.sharding import PartitionSpec as P

NOTE = 16
GROUP = 2
WIDTH = 4
AXES = ("row", "col")


def cube(own, count, cut, gather):
    x, z1, z2, z3, core, y = 1, 2, 4, 6, 8, 16
    full = own.shape[0]
    found = []

    def swap(value, mask):
        return lax.ppermute(value, AXES, [(i, i ^ mask) for i in range(count)])

    def whole(*masks):
        return [(mask, 0, full) for mask in masks]

    def cross(*items):
        arrays = [array for array, _ in items]
        batch = swap(jnp.concatenate(arrays, axis=0) if len(arrays) > 1 else arrays[0], core)
        found.extend(items)
        found.append((batch, [(mask | core, start, size) for _, parts in items for mask, start, size in parts]))
        return len(found) - 1

    def finish(spot, *arrays):
        batch, *arrays = lax.optimization_barrier((found[spot][0],) + arrays)
        found[spot] = (batch, found[spot][1])
        return arrays

    x0, y0, d0, f1, f3 = (swap(own, mask) for mask in (x, y, x | y, z1, z3))
    pair = jnp.concatenate([f1, f3], axis=0)
    xp, yp, f2, d2 = swap(pair, x), swap(pair, y), swap(f3, z1), swap(d0, z2)
    spot = cross(
        (own, whole(0)), (x0, whole(x)), (y0, whole(y)), (d0, whole(x | y)), (f1, whole(z1)), (f3, whole(z3))
    )
    yp, xp, f2, d0 = finish(spot, yp, xp, f2, d0)
    xl = swap(jnp.concatenate([f2, yp[full : full + cut]], axis=0), x)
    yl = swap(jnp.concatenate([f2, xp[full + cut :]], axis=0), y)
    d1 = swap(d0, z1)
    cross((xp, whole(z1 | x, z3 | x)))
    cross((yp, whole(z1 | y, z3 | y)))
    band = gather(None, found + [(f2, whole(z2)), (d2, whole(z2 | x | y))])
    band, xl, yl, d1, f2, d2 = lax.optimization_barrier((band, xl, yl, d1, f2, d2))
    del found[:]
    cross((xl, [(z2 | x, 0, full), (z3 | x | y, 0, cut)]))
    cross((yl, [(z2 | y, 0, full), (z3 | x | y, cut, full - cut)]))
    for row, mask in ((f2, z2), (d2, z2 | x | y), (d1, z1 | x | y)):
        cross((row, whole(mask)))
    return gather(band, [item for item in found if any(item[0] is late for late in (xl, yl, d1))]), found[1::2]


def window(payload, need, cut):
    groups, width = lax.axis_size("row"), lax.axis_size("col")
    count = groups * width
    size = payload.shape[0]

    def flipped(mask):
        def offset():
            here = lax.axis_index("row") * width + lax.axis_index("col")
            return (((here ^ mask) - here + count // 2) & (count - 1)) - count // 2

        return offset

    def shifted(place):
        return lambda: place - lax.axis_index("col")

    if (groups, width) == (4, 8):

        def pieces(found):
            return [(array, [(start, rows, flipped(mask)) for mask, start, rows in parts]) for array, parts in found]

        def gather(band, found):
            return assemble(pieces(found), size, need, band)

        band, late = cube(payload, count, cut, gather)
        return band, pieces(late)

    def piece(array, first):
        return array, [(0, size, shifted(first + j)) for j in range(array.shape[0] // size)]

    block = lax.all_gather(payload, "col", axis=0, tiled=True)
    pieces = [piece(block, 0)]
    for hop in range(1, -(-need // width) + 1):
        part = min(width, need - (hop - 1) * width)
        up = [(g, (g + hop) % groups) for g in range(groups)]
        down = [(g, (g - hop) % groups) for g in range(groups)]
        pieces.append(piece(lax.ppermute(block[(width - part) * size :], "row", up), (1 - hop) * width - part))
        pieces.append(piece(lax.ppermute(block[: part * size], "row", down), hop * width))
    return assemble(pieces, size, need), []


def row_copies(layout, need, tables, band, arrived, pitch):
    copies = []
    for table, parts in zip(tables, layout):
        begin = 0
        for start, size, offset in parts:
            k = offset() + need
            wanted = (k >= 0) & (k <= 2 * need)
            row = jnp.where(wanted, k, 0)
            copy = pltpu.make_async_copy(
                table.at[pl.ds(begin, size)],
                band.at[pl.ds(pl.multiple_of(row * pitch + start, NOTE), size)],
                arrived.at[len(copies)],
            )
            copies.append((wanted, row, copy))
            begin += size
    for wanted, _, copy in copies:

        @pl.when(wanted)
        def _(copy=copy):
            copy.start()

    return copies


def wait_all(copies):
    for wanted, _, copy in copies:

        @pl.when(wanted)
        def _(copy=copy):
            copy.wait()


def assemble(pieces, pitch, need, band=None):
    tables = [array for array, _ in pieces]
    layout = [parts for _, parts in pieces]
    kind, edge = tables[0].dtype, tables[0].shape[1]
    rows = 2 * need + 1

    vmem = pl.BlockSpec(memory_space=pltpu.VMEM)
    given = [] if band is None else [band]

    def body(*refs):
        band, arrived = refs[-2:]
        wait_all(row_copies(layout, need, refs[: len(tables)], band, arrived, pitch))

    return pl.pallas_call(
        body,
        out_shape=pltpu.VMEM((rows * pitch, edge), kind),
        in_specs=[pl.BlockSpec(memory_space=pl.ANY)] * len(tables) + [vmem] * len(given),
        out_specs=vmem,
        input_output_aliases={len(tables): 0} if given else {},
        scratch_shapes=[pltpu.SemaphoreType.DMA((sum(len(parts) for parts in layout),))],
        compiler_params=pltpu.CompilerParams(vmem_limit_bytes=2 * 2**20),
        cost_estimate=pl.CostEstimate(
            flops=0, bytes_accessed=sum(table.size for table in tables) * 4, transcendentals=0
        ),
    )(*tables, *given)


def purify(reach, edge, layout, *refs):
    count = len(layout)
    tables, (_, band, out, square, own, result, arrived, left_out) = refs[:count], refs[count:]
    far = 2 * reach
    slots, wide = 2 * reach + 1, 4 * reach + 1
    pitch = slots * edge + NOTE
    kind = band.dtype
    late = row_copies(layout, far, tables, band, arrived, pitch)

    zero = jnp.zeros((edge, edge), kind)

    def from_row(first, n):
        return pl.ds(first if isinstance(first, int) else pl.multiple_of(first, NOTE), n)

    def block(k, s):
        return band[from_row(k * pitch + s * edge, edge), :]

    spots = -(-wide // 8) * 8
    diagonal = lax.broadcasted_iota(jnp.int32, (spots, edge), 0) == lax.broadcasted_iota(jnp.int32, (spots, edge), 1)

    def masks(k):
        line = band[from_row(k * pitch + slots * edge, NOTE), :].astype(jnp.float32)[:1]
        value = jnp.sum(jnp.where(diagonal, line, 0.0), axis=1, keepdims=True)
        return jnp.broadcast_to(value, (spots, edge))

    def strip(k, first, n):
        return jnp.concatenate(
            [block(k, s) if 0 <= s < slots else zero for s in range(first, first + n)], axis=1
        )

    def square_strip(r, first, n):
        return jnp.concatenate(
            [
                square[r * edge : (r + 1) * edge, u * edge : (u + 1) * edge] if 0 <= u < wide else zero
                for u in range(first, first + n)
            ],
            axis=1,
        )

    def square_rows(r, n, slot, own_row, offsets):
        keep = [masks(r + reach + i) for i in range(n)]
        for d in offsets:
            low, high = max(-reach, d - reach), min(reach + n - 1, d + reach + 1)
            size = high - low + 1
            left = jnp.concatenate([strip(r + reach + i, low + reach - i, size) for i in range(n)], axis=0)
            right = jnp.concatenate([strip(r + reach + e, d - e + reach, 2) for e in range(low, high + 1)], axis=0)
            product = jnp.dot(left, right, preferred_element_type=jnp.float32)
            for i in range(n):
                for j in range(2):
                    u = d + far - i + j
                    if 0 <= u < wide:
                        kept = product[i * edge : (i + 1) * edge, j * edge : (j + 1) * edge]
                        kept = kept * keep[i][u : u + 1, :]
                        square[from_row((r + i) * edge, edge), u * edge : (u + 1) * edge] = kept.astype(kind)
                        if i == own_row:
                            own[slot, :, u * edge : (u + 1) * edge] = kept

    def first_user(row):
        return jnp.minimum(lax.div(jnp.maximum(row - far, 0), GROUP), slots // GROUP - 1)

    def row_group(group, carry):
        needed = [(first_user(row) == group) & wanted for wanted, row, _ in late]
        wait_all([(now, row, copy) for now, (_, row, copy) in zip(needed, late)])
        slot = jnp.where(group == reach // GROUP, 1, 0)
        square_rows(GROUP * group, GROUP, slot, reach % GROUP, range(-far, far + GROUP, 2))
        return carry

    lax.fori_loop(0, slots // GROUP, row_group, 0)
    for r in range(slots // GROUP * GROUP, slots):
        square_rows(r, 1, 0, None, range(-far, far + reach - r + 1, 2))

    keep = masks(far)
    copies = []
    for c in range(-far, far + 1, WIDTH):
        low, high = max(-reach, c - far), min(reach, c + far + WIDTH - 1)
        left = strip(far, low + reach, high - low + 1)
        right = jnp.concatenate(
            [square_strip(r + reach, c - r + far, WIDTH) for r in range(low, high + 1)], axis=0
        )
        cube = jnp.dot(left, right, preferred_element_type=jnp.float32)
        first, last = c + far, min(c + far + WIDTH, wide)
        for u in range(first, last):
            j = u - first
            value = 3.0 * own[1, :, u * edge : (u + 1) * edge] - 2.0 * cube[:, j * edge : (j + 1) * edge]
            result[u] = (keep[u : u + 1, :] * value).astype(out.dtype)
        copies.append(
            pltpu.make_async_copy(
                result.at[pl.ds(first, last - first)], out.at[pl.ds(first, last - first)], left_out.at[len(copies)]
            )
        )
        copies[-1].start()
    for copy in copies:
        copy.wait()


def pack(pattern, filter_mask, density, payload):
    slots, edge = density.shape[0], density.shape[1]
    for s in range(slots):
        scale = pattern[0, s].astype(jnp.float32)
        payload[s * edge : (s + 1) * edge] = (density[s].astype(jnp.float32) * scale).astype(payload.dtype)
    lane = lax.broadcasted_iota(jnp.int32, (NOTE, edge), 1)
    note = jnp.zeros((NOTE, edge), jnp.float32)
    for u in range(filter_mask.shape[1]):
        note = jnp.where(lane == u, filter_mask[0, u].astype(jnp.float32), note)
    payload[slots * edge :] = note.astype(payload.dtype)


def shards(density, pattern, filter_mask):
    slots, edge = density.shape[1], density.shape[2]
    wide = filter_mask.shape[1]
    reach = (slots - 1) // 2
    far = 2 * reach
    smem, vmem = pl.BlockSpec(memory_space=pltpu.SMEM), pl.BlockSpec(memory_space=pltpu.VMEM)
    anywhere = pl.BlockSpec(memory_space=pl.ANY)
    payload = pl.pallas_call(
        pack,
        out_shape=jax.ShapeDtypeStruct((slots * edge + NOTE, edge), density.dtype),
        in_specs=[smem, smem, vmem],
        out_specs=vmem,
        compiler_params=pltpu.CompilerParams(vmem_limit_bytes=60 * 2**20),
    )(pattern, filter_mask, density[0])
    band, pieces = window(payload, far, (slots + 1) // 2 * edge)
    tables = [array for array, _ in pieces]
    layout = [parts for _, parts in pieces]
    _, result = pl.pallas_call(
        functools.partial(purify, reach, edge, layout),
        out_shape=[pltpu.VMEM(band.shape, band.dtype), jax.ShapeDtypeStruct((wide, edge, edge), density.dtype)],
        in_specs=[anywhere] * len(tables) + [vmem],
        out_specs=[vmem, anywhere],
        input_output_aliases={len(tables): 0},
        scratch_shapes=[
            pltpu.VMEM((slots * edge, wide * edge), density.dtype),
            pltpu.VMEM((2, edge, wide * edge), jnp.float32),
            pltpu.VMEM((wide, edge, edge), density.dtype),
            pltpu.SemaphoreType.DMA((max(1, sum(len(parts) for parts in layout)),)),
            pltpu.SemaphoreType.DMA((-(-wide // WIDTH),)),
        ],
        compiler_params=pltpu.CompilerParams(vmem_limit_bytes=24 * 2**20),
        cost_estimate=pl.CostEstimate(flops=17 * 10**9, bytes_accessed=15 * 2**20, transcendentals=0),
    )(*tables, band)
    return result[None]


def solution(mesh):
    in_specs = (P(AXES, None, None, None), P(AXES, None), P(AXES, None))
    out_specs = P(AXES, None, None, None)
    return jax.shard_map(shards, mesh=mesh, in_specs=in_specs, out_specs=out_specs, check_vma=False)
```

```python
import functools

import jax
import jax.numpy as jnp
from jax import lax
from jax.experimental import pallas as pl
from jax.experimental.pallas import tpu as pltpu
from jax.sharding import PartitionSpec as P

NOTE = 16
GROUP = 2
WIDTH = 4
AXES = ("row", "col")


def cube(own, count, cut, gather):
    x, z1, z2, z3, core, y = 1, 2, 4, 6, 8, 16
    full = own.shape[0]
    found = []

    def swap(value, mask):
        return lax.ppermute(value, AXES, [(i, i ^ mask) for i in range(count)])

    def whole(*masks):
        return [(mask, 0, full) for mask in masks]

    def cross(*items):
        arrays = [array for array, _ in items]
        batch = swap(jnp.concatenate(arrays, axis=0) if len(arrays) > 1 else arrays[0], core)
        found.extend(items)
        found.append((batch, [(mask | core, start, size) for _, parts in items for mask, start, size in parts]))
        return len(found) - 1

    def finish(spot, *arrays):
        batch, *arrays = lax.optimization_barrier((found[spot][0],) + arrays)
        found[spot] = (batch, found[spot][1])
        return arrays

    x0, y0, d0, f1, f3 = (swap(own, mask) for mask in (x, y, x | y, z1, z3))
    pair = jnp.concatenate([f3, f1], axis=0)
    xp, yp, f2, d2 = swap(pair, x), swap(pair, y), swap(f3, z1), swap(d0, z2)
    spot = cross(
        (own, whole(0)), (x0, whole(x)), (y0, whole(y)), (f3, whole(z3)), (f1, whole(z1)), (d0, whole(x | y))
    )
    yp, xp, f2, d0 = finish(spot, yp, xp, f2, d0)
    xl = swap(jnp.concatenate([f2, yp[:cut]], axis=0), x)
    yl = swap(jnp.concatenate([f2, xp[cut:full]], axis=0), y)
    d1 = swap(d0, z1)
    cross((xp, whole(z3 | x, z1 | x)))
    cross((yp, whole(z3 | y, z1 | y)))
    band = gather(None, found + [(f2, whole(z2)), (d2, whole(z2 | x | y))])
    band, xl, yl, d1, f2, d2 = lax.optimization_barrier((band, xl, yl, d1, f2, d2))
    del found[:]
    cross((xl, [(z2 | x, 0, full), (z3 | x | y, 0, cut)]))
    cross((yl, [(z2 | y, 0, full), (z3 | x | y, cut, full - cut)]))
    for row, mask in ((f2, z2), (d2, z2 | x | y), (d1, z1 | x | y)):
        cross((row, whole(mask)))
    return gather(band, [item for item in found if any(item[0] is late for late in (xl, yl, d1))]), found[1::2]


def window(payload, need, cut):
    groups, width = lax.axis_size("row"), lax.axis_size("col")
    count = groups * width
    size = payload.shape[0]

    def flipped(mask):
        def offset():
            here = lax.axis_index("row") * width + lax.axis_index("col")
            return (((here ^ mask) - here + count // 2) & (count - 1)) - count // 2

        return offset

    def shifted(place):
        return lambda: place - lax.axis_index("col")

    if (groups, width) == (4, 8):

        def pieces(found):
            return [(array, [(start, rows, flipped(mask)) for mask, start, rows in parts]) for array, parts in found]

        def gather(band, found):
            return assemble(pieces(found), size, need, band)

        band, late = cube(payload, count, cut, gather)
        return band, pieces(late)

    def piece(array, first):
        return array, [(0, size, shifted(first + j)) for j in range(array.shape[0] // size)]

    block = lax.all_gather(payload, "col", axis=0, tiled=True)
    pieces = [piece(block, 0)]
    for hop in range(1, -(-need // width) + 1):
        part = min(width, need - (hop - 1) * width)
        up = [(g, (g + hop) % groups) for g in range(groups)]
        down = [(g, (g - hop) % groups) for g in range(groups)]
        pieces.append(piece(lax.ppermute(block[(width - part) * size :], "row", up), (1 - hop) * width - part))
        pieces.append(piece(lax.ppermute(block[: part * size], "row", down), hop * width))
    return assemble(pieces, size, need), []


def row_copies(layout, need, tables, band, arrived, pitch):
    copies = []
    for table, parts in zip(tables, layout):
        begin = 0
        for start, size, offset in parts:
            k = offset() + need
            wanted = (k >= 0) & (k <= 2 * need)
            row = jnp.where(wanted, k, 0)
            copy = pltpu.make_async_copy(
                table.at[pl.ds(begin, size)],
                band.at[pl.ds(pl.multiple_of(row * pitch + start, NOTE), size)],
                arrived.at[len(copies)],
            )
            copies.append((wanted, row, copy))
            begin += size
    for wanted, _, copy in copies:

        @pl.when(wanted)
        def _(copy=copy):
            copy.start()

    return copies


def wait_all(copies):
    for wanted, _, copy in copies:

        @pl.when(wanted)
        def _(copy=copy):
            copy.wait()


def assemble(pieces, pitch, need, band=None):
    tables = [array for array, _ in pieces]
    layout = [parts for _, parts in pieces]
    kind, edge = tables[0].dtype, tables[0].shape[1]
    rows = 2 * need + 1

    vmem = pl.BlockSpec(memory_space=pltpu.VMEM)
    given = [] if band is None else [band]

    def body(*refs):
        band, arrived = refs[-2:]
        wait_all(row_copies(layout, need, refs[: len(tables)], band, arrived, pitch))

    return pl.pallas_call(
        body,
        out_shape=pltpu.VMEM((rows * pitch, edge), kind),
        in_specs=[pl.BlockSpec(memory_space=pl.ANY)] * len(tables) + [vmem] * len(given),
        out_specs=vmem,
        input_output_aliases={len(tables): 0} if given else {},
        scratch_shapes=[pltpu.SemaphoreType.DMA((sum(len(parts) for parts in layout),))],
        compiler_params=pltpu.CompilerParams(vmem_limit_bytes=2 * 2**20),
        cost_estimate=pl.CostEstimate(
            flops=0, bytes_accessed=sum(table.size for table in tables) * 4, transcendentals=0
        ),
    )(*tables, *given)


def purify(reach, edge, layout, *refs):
    count = len(layout)
    tables, (_, band, out, square, own, result, arrived, left_out) = refs[:count], refs[count:]
    far = 2 * reach
    slots, wide = 2 * reach + 1, 4 * reach + 1
    pitch = slots * edge + NOTE
    kind = band.dtype
    late = row_copies(layout, far, tables, band, arrived, pitch)

    zero = jnp.zeros((edge, edge), kind)

    def from_row(first, n):
        return pl.ds(first if isinstance(first, int) else pl.multiple_of(first, NOTE), n)

    def block(k, s):
        return band[from_row(k * pitch + s * edge, edge), :]

    spots = -(-wide // 8) * 8
    diagonal = lax.broadcasted_iota(jnp.int32, (spots, edge), 0) == lax.broadcasted_iota(jnp.int32, (spots, edge), 1)

    def masks(k):
        line = band[from_row(k * pitch + slots * edge, NOTE), :].astype(jnp.float32)[:1]
        value = jnp.sum(jnp.where(diagonal, line, 0.0), axis=1, keepdims=True)
        return jnp.broadcast_to(value, (spots, edge))

    def strip(k, first, n):
        return jnp.concatenate(
            [block(k, s) if 0 <= s < slots else zero for s in range(first, first + n)], axis=1
        )

    def square_strip(r, first, n):
        return jnp.concatenate(
            [
                square[r * edge : (r + 1) * edge, u * edge : (u + 1) * edge] if 0 <= u < wide else zero
                for u in range(first, first + n)
            ],
            axis=1,
        )

    def square_rows(r, n, slot, own_row, offsets):
        keep = [masks(r + reach + i) for i in range(n)]
        for d in offsets:
            low, high = max(-reach, d - reach), min(reach + n - 1, d + reach + 1)
            size = high - low + 1
            left = jnp.concatenate([strip(r + reach + i, low + reach - i, size) for i in range(n)], axis=0)
            right = jnp.concatenate([strip(r + reach + e, d - e + reach, 2) for e in range(low, high + 1)], axis=0)
            product = jnp.dot(left, right, preferred_element_type=jnp.float32)
            for i in range(n):
                for j in range(2):
                    u = d + far - i + j
                    if 0 <= u < wide:
                        kept = product[i * edge : (i + 1) * edge, j * edge : (j + 1) * edge]
                        kept = kept * keep[i][u : u + 1, :]
                        square[from_row((r + i) * edge, edge), u * edge : (u + 1) * edge] = kept.astype(kind)
                        if i == own_row:
                            own[slot, :, u * edge : (u + 1) * edge] = kept

    def first_user(row):
        return jnp.minimum(lax.div(jnp.maximum(row - far, 0), GROUP), slots // GROUP - 1)

    def row_group(group, carry):
        needed = [(first_user(row) == group) & wanted for wanted, row, _ in late]
        wait_all([(now, row, copy) for now, (_, row, copy) in zip(needed, late)])
        slot = jnp.where(group == reach // GROUP, 1, 0)
        square_rows(GROUP * group, GROUP, slot, reach % GROUP, range(-far, far + GROUP, 2))
        return carry

    lax.fori_loop(0, slots // GROUP, row_group, 0)
    for r in range(slots // GROUP * GROUP, slots):
        square_rows(r, 1, 0, None, range(-far, far + reach - r + 1, 2))

    keep = masks(far)
    copies = []
    for c in range(-far, far + 1, WIDTH):
        low, high = max(-reach, c - far), min(reach, c + far + WIDTH - 1)
        left = strip(far, low + reach, high - low + 1)
        right = jnp.concatenate(
            [square_strip(r + reach, c - r + far, WIDTH) for r in range(low, high + 1)], axis=0
        )
        cube = jnp.dot(left, right, preferred_element_type=jnp.float32)
        first, last = c + far, min(c + far + WIDTH, wide)
        for u in range(first, last):
            j = u - first
            value = 3.0 * own[1, :, u * edge : (u + 1) * edge] - 2.0 * cube[:, j * edge : (j + 1) * edge]
            result[u] = (keep[u : u + 1, :] * value).astype(out.dtype)
        copies.append(
            pltpu.make_async_copy(
                result.at[pl.ds(first, last - first)], out.at[pl.ds(first, last - first)], left_out.at[len(copies)]
            )
        )
        copies[-1].start()
    for copy in copies:
        copy.wait()


def pack(pattern, filter_mask, density, payload):
    slots, edge = density.shape[0], density.shape[1]
    for s in range(slots):
        scale = pattern[0, s].astype(jnp.float32)
        payload[s * edge : (s + 1) * edge] = (density[s].astype(jnp.float32) * scale).astype(payload.dtype)
    lane = lax.broadcasted_iota(jnp.int32, (NOTE, edge), 1)
    note = jnp.zeros((NOTE, edge), jnp.float32)
    for u in range(filter_mask.shape[1]):
        note = jnp.where(lane == u, filter_mask[0, u].astype(jnp.float32), note)
    payload[slots * edge :] = note.astype(payload.dtype)


def shards(density, pattern, filter_mask):
    slots, edge = density.shape[1], density.shape[2]
    wide = filter_mask.shape[1]
    reach = (slots - 1) // 2
    far = 2 * reach
    smem, vmem = pl.BlockSpec(memory_space=pltpu.SMEM), pl.BlockSpec(memory_space=pltpu.VMEM)
    anywhere = pl.BlockSpec(memory_space=pl.ANY)
    payload = pl.pallas_call(
        pack,
        out_shape=jax.ShapeDtypeStruct((slots * edge + NOTE, edge), density.dtype),
        in_specs=[smem, smem, vmem],
        out_specs=vmem,
        compiler_params=pltpu.CompilerParams(vmem_limit_bytes=60 * 2**20),
    )(pattern, filter_mask, density[0])
    band, pieces = window(payload, far, (slots + 1) // 2 * edge)
    tables = [array for array, _ in pieces]
    layout = [parts for _, parts in pieces]
    _, result = pl.pallas_call(
        functools.partial(purify, reach, edge, layout),
        out_shape=[pltpu.VMEM(band.shape, band.dtype), jax.ShapeDtypeStruct((wide, edge, edge), density.dtype)],
        in_specs=[anywhere] * len(tables) + [vmem],
        out_specs=[vmem, anywhere],
        input_output_aliases={len(tables): 0},
        scratch_shapes=[
            pltpu.VMEM((slots * edge, wide * edge), density.dtype),
            pltpu.VMEM((2, edge, wide * edge), jnp.float32),
            pltpu.VMEM((wide, edge, edge), density.dtype),
            pltpu.SemaphoreType.DMA((max(1, sum(len(parts) for parts in layout)),)),
            pltpu.SemaphoreType.DMA((-(-wide // WIDTH),)),
        ],
        compiler_params=pltpu.CompilerParams(vmem_limit_bytes=24 * 2**20),
        cost_estimate=pl.CostEstimate(flops=17 * 10**9, bytes_accessed=15 * 2**20, transcendentals=0),
    )(*tables, band)
    return result[None]


def solution(mesh):
    in_specs = (P(AXES, None, None, None), P(AXES, None), P(AXES, None))
    out_specs = P(AXES, None, None, None)
    return jax.shard_map(shards, mesh=mesh, in_specs=in_specs, out_specs=out_specs, check_vma=False)
```

```python
import functools

import jax
import jax.numpy as jnp
from jax import lax
from jax.experimental import pallas as pl
from jax.experimental.pallas import tpu as pltpu
from jax.sharding import PartitionSpec as P

NOTE = 16
GROUP = 4
WIDTH = 4
AXES = ("row", "col")


def cube(own, count, cut, gather):
    x, z1, z2, z3, core, y = 1, 2, 4, 6, 8, 16
    full = own.shape[0]
    found = []

    def swap(value, mask):
        return lax.ppermute(value, AXES, [(i, i ^ mask) for i in range(count)])

    def whole(*masks):
        return [(mask, 0, full) for mask in masks]

    def cross(*items):
        arrays = [array for array, _ in items]
        batch = swap(jnp.concatenate(arrays, axis=0) if len(arrays) > 1 else arrays[0], core)
        found.extend(items)
        found.append((batch, [(mask | core, start, size) for _, parts in items for mask, start, size in parts]))
        return len(found) - 1

    def finish(spot, *arrays):
        batch, *arrays = lax.optimization_barrier((found[spot][0],) + arrays)
        found[spot] = (batch, found[spot][1])
        return arrays

    x0, y0, d0, f1, f3 = (swap(own, mask) for mask in (x, y, x | y, z1, z3))
    pair = jnp.concatenate([f3, f1], axis=0)
    xp, yp, f2, d2 = swap(pair, x), swap(pair, y), swap(f3, z1), swap(d0, z2)
    spot = cross(
        (own, whole(0)), (x0, whole(x)), (y0, whole(y)), (f3, whole(z3)), (f1, whole(z1)), (d0, whole(x | y))
    )
    yp, xp, f2, d0 = finish(spot, yp, xp, f2, d0)
    xl = swap(jnp.concatenate([f2, yp[:cut]], axis=0), x)
    yl = swap(jnp.concatenate([f2, xp[cut:full]], axis=0), y)
    d1 = swap(d0, z1)
    cross((xp, whole(z3 | x, z1 | x)))
    cross((yp, whole(z3 | y, z1 | y)))
    band = gather(None, found + [(f2, whole(z2)), (d2, whole(z2 | x | y))])
    band, xl, yl, d1, f2, d2 = lax.optimization_barrier((band, xl, yl, d1, f2, d2))
    del found[:]
    cross((xl, [(z2 | x, 0, full), (z3 | x | y, 0, cut)]))
    cross((yl, [(z2 | y, 0, full), (z3 | x | y, cut, full - cut)]))
    for row, mask in ((f2, z2), (d2, z2 | x | y), (d1, z1 | x | y)):
        cross((row, whole(mask)))
    return gather(band, [item for item in found if any(item[0] is late for late in (xl, yl, d1))]), found[1::2]


def window(payload, need, cut):
    groups, width = lax.axis_size("row"), lax.axis_size("col")
    count = groups * width
    size = payload.shape[0]

    def flipped(mask):
        def offset():
            here = lax.axis_index("row") * width + lax.axis_index("col")
            return (((here ^ mask) - here + count // 2) & (count - 1)) - count // 2

        return offset

    def shifted(place):
        return lambda: place - lax.axis_index("col")

    if (groups, width) == (4, 8):

        def pieces(found):
            return [(array, [(start, rows, flipped(mask)) for mask, start, rows in parts]) for array, parts in found]

        def gather(band, found):
            return assemble(pieces(found), size, need, band)

        band, late = cube(payload, count, cut, gather)
        return band, pieces(late)

    def piece(array, first):
        return array, [(0, size, shifted(first + j)) for j in range(array.shape[0] // size)]

    block = lax.all_gather(payload, "col", axis=0, tiled=True)
    pieces = [piece(block, 0)]
    for hop in range(1, -(-need // width) + 1):
        part = min(width, need - (hop - 1) * width)
        up = [(g, (g + hop) % groups) for g in range(groups)]
        down = [(g, (g - hop) % groups) for g in range(groups)]
        pieces.append(piece(lax.ppermute(block[(width - part) * size :], "row", up), (1 - hop) * width - part))
        pieces.append(piece(lax.ppermute(block[: part * size], "row", down), hop * width))
    return assemble(pieces, size, need), []


def row_copies(layout, need, tables, band, arrived, pitch):
    copies = []
    for table, parts in zip(tables, layout):
        begin = 0
        for start, size, offset in parts:
            k = offset() + need
            wanted = (k >= 0) & (k <= 2 * need)
            row = jnp.where(wanted, k, 0)
            copy = pltpu.make_async_copy(
                table.at[pl.ds(begin, size)],
                band.at[pl.ds(pl.multiple_of(row * pitch + start, NOTE), size)],
                arrived.at[len(copies)],
            )
            copies.append((wanted, row, copy))
            begin += size
    for wanted, _, copy in copies:

        @pl.when(wanted)
        def _(copy=copy):
            copy.start()

    return copies


def wait_all(copies):
    for wanted, _, copy in copies:

        @pl.when(wanted)
        def _(copy=copy):
            copy.wait()


def assemble(pieces, pitch, need, band=None):
    tables = [array for array, _ in pieces]
    layout = [parts for _, parts in pieces]
    kind, edge = tables[0].dtype, tables[0].shape[1]
    rows = 2 * need + 1

    vmem = pl.BlockSpec(memory_space=pltpu.VMEM)
    given = [] if band is None else [band]

    def body(*refs):
        band, arrived = refs[-2:]
        wait_all(row_copies(layout, need, refs[: len(tables)], band, arrived, pitch))

    return pl.pallas_call(
        body,
        out_shape=pltpu.VMEM((rows * pitch, edge), kind),
        in_specs=[pl.BlockSpec(memory_space=pl.ANY)] * len(tables) + [vmem] * len(given),
        out_specs=vmem,
        input_output_aliases={len(tables): 0} if given else {},
        scratch_shapes=[pltpu.SemaphoreType.DMA((sum(len(parts) for parts in layout),))],
        compiler_params=pltpu.CompilerParams(vmem_limit_bytes=2 * 2**20),
        cost_estimate=pl.CostEstimate(
            flops=0, bytes_accessed=sum(table.size for table in tables) * 4, transcendentals=0
        ),
    )(*tables, *given)


def purify(reach, edge, layout, *refs):
    count = len(layout)
    tables, (_, band, out, square, own, result, arrived, left_out) = refs[:count], refs[count:]
    far = 2 * reach
    slots, wide = 2 * reach + 1, 4 * reach + 1
    pitch = slots * edge + NOTE
    kind = band.dtype
    late = row_copies(layout, far, tables, band, arrived, pitch)

    zero = jnp.zeros((edge, edge), kind)

    def from_row(first, n):
        return pl.ds(first if isinstance(first, int) else pl.multiple_of(first, NOTE), n)

    def block(k, s):
        return band[from_row(k * pitch + s * edge, edge), :]

    spots = -(-wide // 8) * 8
    diagonal = lax.broadcasted_iota(jnp.int32, (spots, edge), 0) == lax.broadcasted_iota(jnp.int32, (spots, edge), 1)

    def masks(k):
        line = band[from_row(k * pitch + slots * edge, NOTE), :].astype(jnp.float32)[:1]
        value = jnp.sum(jnp.where(diagonal, line, 0.0), axis=1, keepdims=True)
        return jnp.broadcast_to(value, (spots, edge))

    def strip(k, first, n):
        return jnp.concatenate(
            [block(k, s) if 0 <= s < slots else zero for s in range(first, first + n)], axis=1
        )

    def square_strip(r, first, n):
        return jnp.concatenate(
            [
                square[r * edge : (r + 1) * edge, u * edge : (u + 1) * edge] if 0 <= u < wide else zero
                for u in range(first, first + n)
            ],
            axis=1,
        )

    def square_rows(r, n, slot, own_row, offsets):
        keep = [masks(r + reach + i) for i in range(n)]
        for d in offsets:
            low, high = max(-reach, d - reach), min(reach + n - 1, d + reach + 1)
            size = high - low + 1
            left = jnp.concatenate([strip(r + reach + i, low + reach - i, size) for i in range(n)], axis=0)
            right = jnp.concatenate([strip(r + reach + e, d - e + reach, 2) for e in range(low, high + 1)], axis=0)
            product = jnp.dot(left, right, preferred_element_type=jnp.float32)
            for i in range(n):
                for j in range(2):
                    u = d + far - i + j
                    if 0 <= u < wide:
                        kept = product[i * edge : (i + 1) * edge, j * edge : (j + 1) * edge]
                        kept = kept * keep[i][u : u + 1, :]
                        square[from_row((r + i) * edge, edge), u * edge : (u + 1) * edge] = kept.astype(kind)
                        if i == own_row:
                            own[slot, :, u * edge : (u + 1) * edge] = kept

    def first_user(row):
        return jnp.minimum(lax.div(jnp.maximum(row - far, 0), GROUP), slots // GROUP - 1)

    def row_group(group, carry):
        needed = [(first_user(row) == group) & wanted for wanted, row, _ in late]
        wait_all([(now, row, copy) for now, (_, row, copy) in zip(needed, late)])
        slot = jnp.where(group == reach // GROUP, 1, 0)
        square_rows(GROUP * group, GROUP, slot, reach % GROUP, range(-far, far + GROUP, 2))
        return carry

    lax.fori_loop(0, slots // GROUP, row_group, 0)
    r = slots // GROUP * GROUP
    square_rows(r, slots - r, 0, None, range(-far, far + reach - r + 1, 2))

    keep = masks(far)
    copies = []
    for c in range(-far, far + 1, WIDTH):
        low, high = max(-reach, c - far), min(reach, c + far + WIDTH - 1)
        left = strip(far, low + reach, high - low + 1)
        right = jnp.concatenate(
            [square_strip(r + reach, c - r + far, WIDTH) for r in range(low, high + 1)], axis=0
        )
        cube = jnp.dot(left, right, preferred_element_type=jnp.float32)
        first, last = c + far, min(c + far + WIDTH, wide)
        for u in range(first, last):
            j = u - first
            value = 3.0 * own[1, :, u * edge : (u + 1) * edge] - 2.0 * cube[:, j * edge : (j + 1) * edge]
            result[u] = (keep[u : u + 1, :] * value).astype(out.dtype)
        copies.append(
            pltpu.make_async_copy(
                result.at[pl.ds(first, last - first)], out.at[pl.ds(first, last - first)], left_out.at[len(copies)]
            )
        )
        copies[-1].start()
    for copy in copies:
        copy.wait()


def pack(pattern, filter_mask, density, payload):
    slots, edge = density.shape[0], density.shape[1]
    for s in range(slots):
        scale = pattern[0, s].astype(jnp.float32)
        payload[s * edge : (s + 1) * edge] = (density[s].astype(jnp.float32) * scale).astype(payload.dtype)
    lane = lax.broadcasted_iota(jnp.int32, (NOTE, edge), 1)
    note = jnp.zeros((NOTE, edge), jnp.float32)
    for u in range(filter_mask.shape[1]):
        note = jnp.where(lane == u, filter_mask[0, u].astype(jnp.float32), note)
    payload[slots * edge :] = note.astype(payload.dtype)


def shards(density, pattern, filter_mask):
    slots, edge = density.shape[1], density.shape[2]
    wide = filter_mask.shape[1]
    reach = (slots - 1) // 2
    far = 2 * reach
    smem, vmem = pl.BlockSpec(memory_space=pltpu.SMEM), pl.BlockSpec(memory_space=pltpu.VMEM)
    anywhere = pl.BlockSpec(memory_space=pl.ANY)
    payload = pl.pallas_call(
        pack,
        out_shape=jax.ShapeDtypeStruct((slots * edge + NOTE, edge), density.dtype),
        in_specs=[smem, smem, vmem],
        out_specs=vmem,
        compiler_params=pltpu.CompilerParams(vmem_limit_bytes=60 * 2**20),
    )(pattern, filter_mask, density[0])
    band, pieces = window(payload, far, (slots + 1) // 2 * edge)
    tables = [array for array, _ in pieces]
    layout = [parts for _, parts in pieces]
    _, result = pl.pallas_call(
        functools.partial(purify, reach, edge, layout),
        out_shape=[pltpu.VMEM(band.shape, band.dtype), jax.ShapeDtypeStruct((wide, edge, edge), density.dtype)],
        in_specs=[anywhere] * len(tables) + [vmem],
        out_specs=[vmem, anywhere],
        input_output_aliases={len(tables): 0},
        scratch_shapes=[
            pltpu.VMEM((slots * edge, wide * edge), density.dtype),
            pltpu.VMEM((2, edge, wide * edge), jnp.float32),
            pltpu.VMEM((wide, edge, edge), density.dtype),
            pltpu.SemaphoreType.DMA((max(1, sum(len(parts) for parts in layout)),)),
            pltpu.SemaphoreType.DMA((-(-wide // WIDTH),)),
        ],
        compiler_params=pltpu.CompilerParams(vmem_limit_bytes=24 * 2**20),
        cost_estimate=pl.CostEstimate(flops=17 * 10**9, bytes_accessed=15 * 2**20, transcendentals=0),
    )(*tables, band)
    return result[None]


def solution(mesh):
    in_specs = (P(AXES, None, None, None), P(AXES, None), P(AXES, None))
    out_specs = P(AXES, None, None, None)
    return jax.shard_map(shards, mesh=mesh, in_specs=in_specs, out_specs=out_specs, check_vma=False)
```

```python
import functools

import jax
import jax.numpy as jnp
from jax import lax
from jax.experimental import pallas as pl
from jax.experimental.pallas import tpu as pltpu
from jax.sharding import PartitionSpec as P

NOTE = 16
GROUP = 2
WIDTH = 4
AXES = ("row", "col")


def cube(own, count, cut, gather):
    x, z1, z2, z3, core, y = 1, 2, 4, 6, 8, 16
    full = own.shape[0]
    found = []

    def swap(value, mask):
        return lax.ppermute(value, AXES, [(i, i ^ mask) for i in range(count)])

    def whole(*masks):
        return [(mask, 0, full) for mask in masks]

    def cross(*items):
        arrays = [array for array, _ in items]
        batch = swap(jnp.concatenate(arrays, axis=0) if len(arrays) > 1 else arrays[0], core)
        found.extend(items)
        found.append((batch, [(mask | core, start, size) for _, parts in items for mask, start, size in parts]))
        return len(found) - 1

    def finish(spot, *arrays):
        batch, *arrays = lax.optimization_barrier((found[spot][0],) + arrays)
        found[spot] = (batch, found[spot][1])
        return arrays

    x0, y0, d0, f1, f3 = (swap(own, mask) for mask in (x, y, x | y, z1, z3))
    pair = jnp.concatenate([f3, f1], axis=0)
    xp, yp, f2, d2 = swap(pair, x), swap(pair, y), swap(f3, z1), swap(d0, z2)
    spot = cross(
        (own, whole(0)), (x0, whole(x)), (y0, whole(y)), (f3, whole(z3)), (f1, whole(z1)), (d0, whole(x | y))
    )
    yp, xp, f2, d0 = finish(spot, yp, xp, f2, d0)
    xl = swap(jnp.concatenate([f2, yp[:cut]], axis=0), x)
    yl = swap(jnp.concatenate([f2, xp[cut:full]], axis=0), y)
    d1 = swap(d0, z1)
    cross((xp, whole(z3 | x, z1 | x)))
    cross((yp, whole(z3 | y, z1 | y)))
    band = gather(None, found + [(f2, whole(z2)), (d2, whole(z2 | x | y))])
    band, xl, yl, d1, f2, d2 = lax.optimization_barrier((band, xl, yl, d1, f2, d2))
    del found[:]
    cross((xl, [(z2 | x, 0, full), (z3 | x | y, 0, cut)]))
    cross((yl, [(z2 | y, 0, full), (z3 | x | y, cut, full - cut)]))
    for row, mask in ((f2, z2), (d2, z2 | x | y), (d1, z1 | x | y)):
        cross((row, whole(mask)))
    return gather(band, [item for item in found if any(item[0] is late for late in (xl, yl, d1))]), found[1::2]


def window(payload, need, cut):
    groups, width = lax.axis_size("row"), lax.axis_size("col")
    count = groups * width
    size = payload.shape[0]

    def flipped(mask):
        def offset():
            here = lax.axis_index("row") * width + lax.axis_index("col")
            return (((here ^ mask) - here + count // 2) & (count - 1)) - count // 2

        return offset

    def shifted(place):
        return lambda: place - lax.axis_index("col")

    if (groups, width) == (4, 8):

        def pieces(found):
            return [(array, [(start, rows, flipped(mask)) for mask, start, rows in parts]) for array, parts in found]

        def gather(band, found):
            return assemble(pieces(found), size, need, band)

        band, late = cube(payload, count, cut, gather)
        return band, pieces(late)

    def piece(array, first):
        return array, [(0, size, shifted(first + j)) for j in range(array.shape[0] // size)]

    block = lax.all_gather(payload, "col", axis=0, tiled=True)
    pieces = [piece(block, 0)]
    for hop in range(1, -(-need // width) + 1):
        part = min(width, need - (hop - 1) * width)
        up = [(g, (g + hop) % groups) for g in range(groups)]
        down = [(g, (g - hop) % groups) for g in range(groups)]
        pieces.append(piece(lax.ppermute(block[(width - part) * size :], "row", up), (1 - hop) * width - part))
        pieces.append(piece(lax.ppermute(block[: part * size], "row", down), hop * width))
    return assemble(pieces, size, need), []


def row_copies(layout, need, tables, band, arrived, pitch):
    copies = []
    for table, parts in zip(tables, layout):
        begin = 0
        for start, size, offset in parts:
            k = offset() + need
            wanted = (k >= 0) & (k <= 2 * need)
            row = jnp.where(wanted, k, 0)
            copy = pltpu.make_async_copy(
                table.at[pl.ds(begin, size)],
                band.at[pl.ds(pl.multiple_of(row * pitch + start, NOTE), size)],
                arrived.at[len(copies)],
            )
            copies.append((wanted, row, copy))
            begin += size
    for wanted, _, copy in copies:

        @pl.when(wanted)
        def _(copy=copy):
            copy.start()

    return copies


def wait_all(copies):
    for wanted, _, copy in copies:

        @pl.when(wanted)
        def _(copy=copy):
            copy.wait()


def assemble(pieces, pitch, need, band=None):
    tables = [array for array, _ in pieces]
    layout = [parts for _, parts in pieces]
    kind, edge = tables[0].dtype, tables[0].shape[1]
    rows = 2 * need + 1

    vmem = pl.BlockSpec(memory_space=pltpu.VMEM)
    given = [] if band is None else [band]

    def body(*refs):
        band, arrived = refs[-2:]
        wait_all(row_copies(layout, need, refs[: len(tables)], band, arrived, pitch))

    return pl.pallas_call(
        body,
        out_shape=pltpu.VMEM((rows * pitch, edge), kind),
        in_specs=[pl.BlockSpec(memory_space=pl.ANY)] * len(tables) + [vmem] * len(given),
        out_specs=vmem,
        input_output_aliases={len(tables): 0} if given else {},
        scratch_shapes=[pltpu.SemaphoreType.DMA((sum(len(parts) for parts in layout),))],
        compiler_params=pltpu.CompilerParams(vmem_limit_bytes=2 * 2**20),
        cost_estimate=pl.CostEstimate(
            flops=0, bytes_accessed=sum(table.size for table in tables) * 4, transcendentals=0
        ),
    )(*tables, *given)


def purify(reach, edge, layout, *refs):
    count = len(layout)
    tables, (_, band, out, square, own, result, arrived, left_out) = refs[:count], refs[count:]
    far = 2 * reach
    slots, wide = 2 * reach + 1, 4 * reach + 1
    pitch = slots * edge + NOTE
    kind = band.dtype
    late = row_copies(layout, far, tables, band, arrived, pitch)

    zero = jnp.zeros((edge, edge), kind)

    def from_row(first, n):
        return pl.ds(first if isinstance(first, int) else pl.multiple_of(first, NOTE), n)

    def block(k, s):
        return band[from_row(k * pitch + s * edge, edge), :]

    spots = -(-wide // 8) * 8
    diagonal = lax.broadcasted_iota(jnp.int32, (spots, edge), 0) == lax.broadcasted_iota(jnp.int32, (spots, edge), 1)

    def masks(k):
        line = band[from_row(k * pitch + slots * edge, NOTE), :].astype(jnp.float32)[:1]
        value = jnp.sum(jnp.where(diagonal, line, 0.0), axis=1, keepdims=True)
        return jnp.broadcast_to(value, (spots, edge))

    def strip(k, first, n):
        return jnp.concatenate(
            [block(k, s) if 0 <= s < slots else zero for s in range(first, first + n)], axis=1
        )

    def square_strip(r, first, n):
        return jnp.concatenate(
            [
                square[r * edge : (r + 1) * edge, u * edge : (u + 1) * edge] if 0 <= u < wide else zero
                for u in range(first, first + n)
            ],
            axis=1,
        )

    def square_rows(r, n, slot, own_row, offsets):
        keep = [masks(r + reach + i) for i in range(n)]
        for d in offsets:
            low, high = max(-reach, d - reach), min(reach + n - 1, d + reach + WIDTH - 1)
            size = high - low + 1
            left = jnp.concatenate([strip(r + reach + i, low + reach - i, size) for i in range(n)], axis=0)
            right = jnp.concatenate([strip(r + reach + e, d - e + reach, WIDTH) for e in range(low, high + 1)], axis=0)
            product = jnp.dot(left, right, preferred_element_type=jnp.float32)
            for i in range(n):
                for j in range(WIDTH):
                    u = d + far - i + j
                    if 0 <= u < wide:
                        kept = product[i * edge : (i + 1) * edge, j * edge : (j + 1) * edge]
                        kept = kept * keep[i][u : u + 1, :]
                        square[from_row((r + i) * edge, edge), u * edge : (u + 1) * edge] = kept.astype(kind)
                        if i == own_row:
                            own[slot, :, u * edge : (u + 1) * edge] = kept

    def first_user(row):
        return jnp.minimum(lax.div(jnp.maximum(row - far, 0), GROUP), slots // GROUP - 1)

    def row_group(group, carry):
        needed = [(first_user(row) == group) & wanted for wanted, row, _ in late]
        wait_all([(now, row, copy) for now, (_, row, copy) in zip(needed, late)])
        slot = jnp.where(group == reach // GROUP, 1, 0)
        square_rows(GROUP * group, GROUP, slot, reach % GROUP, range(-far, far + GROUP, WIDTH))
        return carry

    lax.fori_loop(0, slots // GROUP, row_group, 0)
    for r in range(slots // GROUP * GROUP, slots):
        square_rows(r, 1, 0, None, range(-far, far + reach - r + 1, WIDTH))

    keep = masks(far)
    copies = []
    for c in range(-far, far + 1, WIDTH):
        low, high = max(-reach, c - far), min(reach, c + far + WIDTH - 1)
        left = strip(far, low + reach, high - low + 1)
        right = jnp.concatenate(
            [square_strip(r + reach, c - r + far, WIDTH) for r in range(low, high + 1)], axis=0
        )
        cube = jnp.dot(left, right, preferred_element_type=jnp.float32)
        first, last = c + far, min(c + far + WIDTH, wide)
        for u in range(first, last):
            j = u - first
            value = 3.0 * own[1, :, u * edge : (u + 1) * edge] - 2.0 * cube[:, j * edge : (j + 1) * edge]
            result[u] = (keep[u : u + 1, :] * value).astype(out.dtype)
        copies.append(
            pltpu.make_async_copy(
                result.at[pl.ds(first, last - first)], out.at[pl.ds(first, last - first)], left_out.at[len(copies)]
            )
        )
        copies[-1].start()
    for copy in copies:
        copy.wait()


def pack(pattern, filter_mask, density, payload):
    slots, edge = density.shape[0], density.shape[1]
    for s in range(slots):
        scale = pattern[0, s].astype(jnp.float32)
        payload[s * edge : (s + 1) * edge] = (density[s].astype(jnp.float32) * scale).astype(payload.dtype)
    lane = lax.broadcasted_iota(jnp.int32, (NOTE, edge), 1)
    note = jnp.zeros((NOTE, edge), jnp.float32)
    for u in range(filter_mask.shape[1]):
        note = jnp.where(lane == u, filter_mask[0, u].astype(jnp.float32), note)
    payload[slots * edge :] = note.astype(payload.dtype)


def shards(density, pattern, filter_mask):
    slots, edge = density.shape[1], density.shape[2]
    wide = filter_mask.shape[1]
    reach = (slots - 1) // 2
    far = 2 * reach
    smem, vmem = pl.BlockSpec(memory_space=pltpu.SMEM), pl.BlockSpec(memory_space=pltpu.VMEM)
    anywhere = pl.BlockSpec(memory_space=pl.ANY)
    payload = pl.pallas_call(
        pack,
        out_shape=jax.ShapeDtypeStruct((slots * edge + NOTE, edge), density.dtype),
        in_specs=[smem, smem, vmem],
        out_specs=vmem,
        compiler_params=pltpu.CompilerParams(vmem_limit_bytes=60 * 2**20),
    )(pattern, filter_mask, density[0])
    band, pieces = window(payload, far, (slots + 1) // 2 * edge)
    tables = [array for array, _ in pieces]
    layout = [parts for _, parts in pieces]
    _, result = pl.pallas_call(
        functools.partial(purify, reach, edge, layout),
        out_shape=[pltpu.VMEM(band.shape, band.dtype), jax.ShapeDtypeStruct((wide, edge, edge), density.dtype)],
        in_specs=[anywhere] * len(tables) + [vmem],
        out_specs=[vmem, anywhere],
        input_output_aliases={len(tables): 0},
        scratch_shapes=[
            pltpu.VMEM((slots * edge, wide * edge), density.dtype),
            pltpu.VMEM((2, edge, wide * edge), jnp.float32),
            pltpu.VMEM((wide, edge, edge), density.dtype),
            pltpu.SemaphoreType.DMA((max(1, sum(len(parts) for parts in layout)),)),
            pltpu.SemaphoreType.DMA((-(-wide // WIDTH),)),
        ],
        compiler_params=pltpu.CompilerParams(vmem_limit_bytes=24 * 2**20),
        cost_estimate=pl.CostEstimate(flops=17 * 10**9, bytes_accessed=15 * 2**20, transcendentals=0),
    )(*tables, band)
    return result[None]


def solution(mesh):
    in_specs = (P(AXES, None, None, None), P(AXES, None), P(AXES, None))
    out_specs = P(AXES, None, None, None)
    return jax.shard_map(shards, mesh=mesh, in_specs=in_specs, out_specs=out_specs, check_vma=False)
```
